32 devices in a mesh: dp: 8 (over y, x, core), mp: 4 (over z).
Axes of the slice: x: 2, y: 2, z: 4, core: 2. Of those that a mesh axis runs over, the one named last changes fastest.
Arguments:
- inputs: bfloat16 [32, 512, 768], P('dp', 'mp'), may hold values from -6 to 6
- segment_ids: int32 [32, 512], P('dp'), may hold values from 0 to 3, never falling along the last dimension, each value on 1 to 256 neighbouring positions
- w_query: bfloat16 [768, 768], P('dp', 'mp'), may hold values from -0.21875 to 0.21875
- w_key: bfloat16 [768, 768], P('dp', 'mp'), may hold values from -0.21875 to 0.21875
- w_value: bfloat16 [768, 768], P('dp', 'mp'), may hold values from -0.21875 to 0.21875
- w_output: bfloat16 [768, 768], P('mp', 'dp'), may hold values from -1.75 to 1.75
- w_up: bfloat16 [768, 3072], P('dp', 'mp'), may hold values from -0.21875 to 0.21875
- w_down: bfloat16 [3072, 768], P('mp', 'dp'), may hold values from -0.109375 to 0.109375
- gain_attn: bfloat16 [768], P('dp'), may hold values from 0.5 to 1.5
- gain_ffn: bfloat16 [768], P('dp'), may hold values from 0.5 to 1.5
- cotangent: bfloat16 [32, 512, 768], P('dp', 'mp'), may hold values from -6 to 6
Outputs:
- layer_output: bfloat16 [32, 512, 768], P('dp', 'mp')
- input_grad: bfloat16 [32, 512, 768], P('dp', 'mp')
- grad_query: float32 [768, 768], P('dp', 'mp')
- grad_key: float32 [768, 768], P('dp', 'mp')
- grad_value: float32 [768, 768], P('dp', 'mp')
- grad_output: float32 [768, 768], P('mp', 'dp')
- grad_up: float32 [768, 3072], P('dp', 'mp')
- grad_down: float32 [3072, 768], P('mp', 'dp')
- grad_gain_attn: float32 [768], P('dp')
- grad_gain_ffn: float32 [768], P('dp')
The draws below stay inside these ranges and needn't reach their ends.
Inputs may be any that keep to these rules, and one draw needn't show every extreme that they name: `segment_ids`: within a row the numbers never fall; each document has 1 to 256 molecules, and one of each row has exactly 256.
All inputs are finite; a program needn't handle non-finite values.
Results may differ from the reference program's by a relative error of at most 0.018.
Values may be sent and summed in bfloat16 or wider, within the bound.
A program may use at most 128 MiB of HBM per device.

```python
import math
import jax
import jax.numpy as jnp
import numpy as np
from jax import lax

D = 768
HEADS = 12
HEAD = 64
FF = 3072
LEN = 512
ROWS = 32


def levels(own_key, extent, shards, smallest, largest):
    loudness = 1.0
    for position, shards_of in shards:
        steps = jax.random.uniform(jax.random.fold_in(jax.random.fold_in(own_key, 6), position), (shards_of,), jnp.float32, smallest / len(shards), largest / len(shards))
        loudness = loudness * jnp.repeat(jnp.exp(steps), extent[position] // shards_of).reshape((-1,) + (1,) * (len(extent) - 1 - position))
    return loudness


def split_up(count, total, reach, lean):
    loads = [(1 << 20) // math.isqrt(standing ** lean) + 1 for standing in range(2, count + 1)]
    surplus, counts = total - reach - (count - 1), [1] * (count - 1)
    while surplus > 0:
        candidates = [i for i in range(count - 1) if counts[i] < reach]
        whole, budget = sum([loads[i] for i in candidates]), surplus
        for i in candidates:
            extra = min(reach - counts[i], max(1, budget * loads[i] // whole), surplus)
            counts[i] = counts[i] + extra
            surplus = surplus - extra
    return np.array([reach] + counts)


def uneven(rng, count, total, most, skew):
    if count == 2:
        one = jax.random.randint(rng, (), max(1, total - most), min(most, total - 1) + 1)
        return jnp.stack([one, total - one])
    lengths = jnp.asarray(split_up(count, total, most, skew), jnp.int32)
    couples = (count - 1) // 2
    source_of, sink = lengths[1:1 + 2 * couples:2], lengths[2:2 + 2 * couples:2]
    room = jnp.minimum(source_of - 1, most - sink)
    passed = jax.random.randint(jax.random.fold_in(rng, 1), (couples,), 0, 1 << 20) % (room + 1)
    lengths = lengths.at[1:1 + 2 * couples:2].set(source_of - passed).at[2:2 + 2 * couples:2].set(sink + passed)
    return lengths[jax.random.permutation(jax.random.fold_in(rng, 2), count)]


def centred(stream_key, dims, scale, most, pieces=(), held_as=jnp.bfloat16):
    factor_of = levels(stream_key, dims, pieces, -0.22, 0.18) if pieces else 1.0
    result = jax.random.normal(stream_key, dims, jnp.float32) * scale * factor_of
    return jnp.minimum(jnp.maximum(result, -most), most).astype(held_as)


def setup_inputs(seed: int = 0) -> dict:
    arg_keys = jax.random.split(jax.random.key(seed), 12)
    inputs = centred(arg_keys[0], (ROWS, LEN, D), 1.0, 6.0, ((0, 8), (1, 4)))
    segment_ids = jax.vmap(lambda own: jnp.searchsorted(jnp.cumsum(uneven(own, 4, LEN, LEN // 2, 0)), jnp.arange(LEN), side="right"))(jax.random.split(arg_keys[1], ROWS)).reshape((ROWS, LEN)).astype(jnp.int32)
    w_query = centred(arg_keys[2], (D, D), D ** -0.5, 0.21875, ((0, 8), (1, 4)))
    w_key = centred(arg_keys[3], (D, D), D ** -0.5, 0.21875, ((0, 8), (1, 4)))
    w_value = centred(arg_keys[4], (D, D), D ** -0.5, 0.21875, ((0, 8), (1, 4)))
    w_output = centred(arg_keys[5], (D, D), (D // 64) ** -0.5, 1.75, ((0, 4), (1, 8)))
    w_up = centred(arg_keys[6], (D, FF), D ** -0.5, 0.21875, ((0, 8), (1, 4)))
    w_down = centred(arg_keys[7], (FF, D), FF ** -0.5, 0.109375, ((0, 4), (1, 8)))
    gain_attn = jnp.clip(1.0 + 0.1 * jax.random.normal(arg_keys[8], (D,), jnp.float32), 0.5, 1.5).astype(jnp.bfloat16)
    gain_ffn = jnp.clip(1.0 + 0.1 * jax.random.normal(arg_keys[9], (D,), jnp.float32), 0.5, 1.5).astype(jnp.bfloat16)
    cotangent = centred(arg_keys[10], (ROWS, LEN, D), 1.0, 6.0, ((0, 8), (1, 4)))
    return {"inputs": inputs, "segment_ids": segment_ids, "w_query": w_query, "w_key": w_key, "w_value": w_value, "w_output": w_output, "w_up": w_up, "w_down": w_down, "gain_attn": gain_attn, "gain_ffn": gain_ffn, "cotangent": cotangent}


@jax.custom_vjp
def low(v):
    return lax.optimization_barrier(v.astype(jnp.bfloat16)).astype(jnp.float32)

@jax.custom_vjp
def low_back(v):
    return v

def low_keep(v):
    return (low(v), None)

def low_pass(kept, grad):
    return (grad,)

def back_keep(v):
    return (v, None)

def back_low(kept, grad):
    return (low(grad),)
low.defvjp(low_keep, low_pass)
low_back.defvjp(back_keep, back_low)
EPS = 1e-05

def layer_norm(values, gain_vector):
    center = lax.optimization_barrier(jnp.mean(values, axis=-1, keepdims=True))
    shifted = values - center
    spread = lax.optimization_barrier(jnp.mean(shifted * shifted, axis=-1, keepdims=True))
    return shifted * lax.rsqrt(spread + EPS) * gain_vector

def matmul(left, right):
    return jnp.einsum('rtd,df->rtf', left, right, precision=lax.Precision.HIGHEST)

def block_layer(pack, weights):
    rows, segment = pack
    w_query, w_key, w_value, w_output, w_up, w_down, gain_attn, gain_ffn = weights
    count = rows.shape[0]
    normed = low(layer_norm(rows, gain_attn))
    query = low(low_back(matmul(normed, w_query))).reshape(count, LEN, HEADS, HEAD)
    keys = low(low_back(matmul(normed, w_key))).reshape(count, LEN, HEADS, HEAD)
    values = low(low_back(matmul(normed, w_value))).reshape(count, LEN, HEADS, HEAD)
    scores = jnp.einsum('rqhd,rkhd->rhqk', query, keys, precision=lax.Precision.HIGHEST) * HEAD ** (-0.5)
    scores = low_back(scores)
    same = (segment[:, :, None] == segment[:, None, :])[:, None, :, :]
    scores = jnp.where(same, scores, -1e+30)
    highest = lax.optimization_barrier(jnp.max(scores, axis=-1, keepdims=True))
    exponent = jnp.exp(scores - highest)
    probs = exponent / lax.optimization_barrier(jnp.sum(exponent, axis=-1, keepdims=True))
    context = jnp.einsum('rhqk,rkhd->rqhd', low(probs), values, precision=lax.Precision.HIGHEST)
    context = low(low_back(context.reshape(count, LEN, D)))
    attended = low_back(matmul(context, w_output))
    middle = rows + attended
    normalized_feedforward_input = low(layer_norm(middle, gain_ffn))
    hidden = low_back(matmul(normalized_feedforward_input, w_up))
    activated = low(jax.nn.gelu(hidden, approximate=False))
    return middle + low_back(matmul(activated, w_down))

def forward(rows, segment_ids, weights):
    block = math.gcd(rows.shape[0], 8)
    blocks = rows.reshape(-1, block, LEN, D)
    segment_blocks = segment_ids.reshape(-1, block, LEN)
    runner = jax.checkpoint(lambda pack: block_layer(pack, weights))
    return lax.map(runner, (blocks, segment_blocks)).reshape(rows.shape)

def reference(inputs, segment_ids, w_query, w_key, w_value, w_output, w_up, w_down, gain_attn, gain_ffn, cotangent):
    weights = (w_query.astype(jnp.float32), w_key.astype(jnp.float32), w_value.astype(jnp.float32), w_output.astype(jnp.float32), w_up.astype(jnp.float32), w_down.astype(jnp.float32), gain_attn.astype(jnp.float32), gain_ffn.astype(jnp.float32))
    rows = inputs.astype(jnp.float32)

    def whole(rows_in, weights_in):
        return forward(rows_in, segment_ids, weights_in)
    output, pullback = jax.vjp(whole, rows, weights)
    grad_rows, grads = pullback(cotangent.astype(jnp.float32))
    return (output.astype(jnp.bfloat16), grad_rows.astype(jnp.bfloat16), grads[0], grads[1], grads[2], grads[3], grads[4], grads[5], grads[6], grads[7])
```

```python
import functools

import jax
import jax.numpy as jnp
from jax import lax
from jax.experimental import pallas as pl
from jax.experimental.pallas import tpu as pltpu
from jax.sharding import PartitionSpec as P

D = 768
HEADS = 12
HEAD = 64
EPS = 1e-05
MESH = pl.DeviceIdType.MESH
BF = jnp.bfloat16
F32 = jnp.float32


def dot(left, right, dims):
    return lax.dot_general(left, right, (dims, ((), ())), preferred_element_type=F32)


def natural(left, right):
    return dot(left, right, ((1,), (0,)))


def against(left, right):
    return dot(left, right, ((1,), (1,)))


def inner(left, right):
    return dot(left, right, ((0,), (0,)))


def norm(values):
    shifted = values - jnp.mean(values, axis=1, keepdims=True)
    scale = lax.rsqrt(jnp.mean(shifted * shifted, axis=1, keepdims=True) + EPS)
    return shifted * scale, scale


def norm_back(grad, xhat, scale, gain):
    e = grad * gain
    back = scale * (
        e - jnp.mean(e, axis=1, keepdims=True) - xhat * jnp.mean(e * xhat, axis=1, keepdims=True)
    )
    return back, jnp.sum(grad * xhat, axis=0)


def columns(w, first, count):
    part = w[:, :, first : first + count]
    return jnp.swapaxes(part, 0, 1).reshape(D, -1)


def row_layer(x, cotangent, segment, weights, gain_attn, gain_ffn):
    length = x.shape[0]
    quarters = weights.shape[1]
    width = D // quarters
    attn, up, down = weights[0], weights[1], weights[2]
    w_query, w_value, w_key, w_out = (columns(attn, i * width, width) for i in range(4))
    w_up, w_down = columns(up, 0, D), columns(down, 0, D)
    x = x.astype(F32)
    xhat_a, scale_a = norm(x)
    normed_a = (xhat_a * gain_attn).astype(BF)
    query, keys, values = (
        natural(normed_a, w).astype(BF).reshape(length, HEADS, HEAD) for w in (w_query, w_key, w_value)
    )
    same = segment[:, None] == segment[None, :]
    scores = jnp.einsum("qhd,khd->hqk", query, keys, preferred_element_type=F32) * HEAD**-0.5
    scores = jnp.where(same[None], scores, -1e30)
    exponent = jnp.exp(scores - jnp.max(scores, axis=2, keepdims=True))
    probs = exponent / jnp.sum(exponent, axis=2, keepdims=True)
    context = jnp.einsum("hqk,khd->qhd", probs.astype(BF), values, preferred_element_type=F32)
    context = context.reshape(length, D).astype(BF)
    middle = x + against(context, w_out)
    xhat_f, scale_f = norm(middle)
    normed_f = (xhat_f * gain_ffn).astype(BF)
    hidden = natural(normed_f, w_up)
    activated, gelu_back = jax.vjp(lambda v: jax.nn.gelu(v, approximate=False), hidden)
    activated = activated.astype(BF)
    output = (middle + against(activated, w_down)).astype(BF)

    grad_down = inner(cotangent, activated)
    grad_hidden = gelu_back(natural(cotangent, w_down))[0].astype(BF)
    grad_up = inner(normed_f, grad_hidden)
    back, grad_gain_ffn = norm_back(against(grad_hidden, w_up), xhat_f, scale_f, gain_ffn)
    grad_middle = cotangent.astype(F32) + back
    grad_attended = grad_middle.astype(BF)
    grad_out = inner(grad_attended, context)
    grad_context = natural(grad_attended, w_out).astype(BF).reshape(length, HEADS, HEAD)
    grad_probs = jnp.einsum("qhd,khd->hqk", grad_context, values, preferred_element_type=F32)
    grad_scores = (
        probs * (grad_probs - jnp.sum(probs * grad_probs, axis=2, keepdims=True))
    ).astype(BF)
    query_grad = jnp.einsum("hqk,khd->qhd", grad_scores, keys, preferred_element_type=F32) * HEAD**-0.5
    key_grad = jnp.einsum("hqk,qhd->khd", grad_scores, query, preferred_element_type=F32) * HEAD**-0.5
    value_grad = jnp.einsum(
        "hqk,qhd->khd", probs.astype(BF), grad_context, preferred_element_type=F32
    )
    query_grad, key_grad, value_grad = (
        g.reshape(length, D).astype(BF) for g in (query_grad, key_grad, value_grad)
    )
    grad_normed_a = (
        against(query_grad, w_query) + against(key_grad, w_key) + against(value_grad, w_value)
    )
    back, grad_gain_attn = norm_back(grad_normed_a, xhat_a, scale_a, gain_attn)
    input_grad = (grad_middle + back).astype(BF)

    def quarter(g, count):
        return g.astype(BF).reshape(D, quarters, count).swapaxes(0, 1)

    grads_attn = jnp.concatenate(
        [
            quarter(g, width)
            for g in (
                inner(normed_a, query_grad),
                inner(normed_a, value_grad),
                inner(normed_a, key_grad),
                grad_out,
            )
        ],
        axis=2,
    )
    grads = jnp.stack([grads_attn, quarter(grad_up, D), quarter(grad_down, D)])
    return output, input_grad, grads, jnp.stack([grad_gain_attn, grad_gain_ffn])


def place():
    dp, z = lax.axis_index("dp"), lax.axis_index("mp")
    c, x, y = lax.rem(dp, 2), lax.rem(dp // 2, 2), dp // 4
    return dp, z, c, dp + 2 - 4 * x, dp + 4 - 8 * y, dp + 1 - 2 * c


def greet(dp, z, parts, quarters):
    barrier = pltpu.get_barrier_semaphore()
    for i in range(1, parts):
        pl.semaphore_signal(barrier, inc=1, device_id=(lax.rem(dp + i, parts), z), device_id_type=MESH)
    for i in range(1, quarters):
        pl.semaphore_signal(barrier, inc=1, device_id=(dp, lax.rem(z + i, quarters)), device_id_type=MESH)
    pl.semaphore_wait(barrier, parts + quarters - 2)


def send(src, dst, ssem, rsem, device):
    return pltpu.make_async_remote_copy(
        src_ref=src, dst_ref=dst, send_sem=ssem, recv_sem=rsem, device_id=device, device_id_type=MESH
    )


def nearest(z, k):
    inner_place = lax.rem((z + 1) // 2, 2)
    first_two = 1 - k // 2
    base = k + inner_place * first_two * (1 - 2 * k)
    return base + (z // 2) * (3 - 2 * base)


def gather_kernel(
    own_ref, gain_ref, x_ref, ct_ref,
    w_ref, gains_ref, xrow_ref, ctrow_ref,
    local_sem, zs, zr, xs, xr, ys, yr, ds, dr, cs, cr, gs, gr, as_, ar,
):
    dp, z, c, nx, ny, nc = place()
    yx, yx_x, yx_y, yx_d = dp // 2, nx // 2, ny // 2, 3 - dp // 2
    greet(dp, z, 8, 4)

    def tile(g, q, d):
        return w_ref.at[g, q, d]

    def rows_out(i, src, dst):
        for j in range(1, 4):
            q = lax.rem(z + j, 4)
            send(src.at[q], dst.at[z], as_.at[i, q], ar.at[i, z], (dp, q)).start()
        pltpu.make_async_copy(src.at[z], dst.at[z], local_sem.at[i]).start()

    def rows_wait(i, src, dst):
        for j in range(1, 4):
            q = lax.rem(z + j, 4)
            cp = send(src.at[q], dst.at[q], as_.at[i, q], ar.at[i, q], (dp, q))
            cp.wait_send()
            cp.wait_recv()
        pltpu.make_async_copy(src.at[z], dst.at[z], local_sem.at[i]).wait()

    def z_copy(g, q, side):
        to = z + (1 if side else -1)
        src = own_ref.at[g] if q is None else tile(g, q, dp)
        q = z if q is None else q
        return send(src, tile(g, q, dp), zs.at[g, q, side], zr.at[g, q], (dp, to))

    def z_start(g, q):
        from_left = z if q is None else q
        @pl.when(jnp.logical_and(from_left <= z, z < 3))
        def _():
            z_copy(g, q, 1).start()

        @pl.when(jnp.logical_and(from_left >= z, z > 0))
        def _():
            z_copy(g, q, 0).start()

    def z_done(g, q):
        @pl.when(jnp.logical_and(q <= z, z < 3))
        def _():
            z_copy(g, q, 1).wait_send()

        @pl.when(jnp.logical_and(q >= z, z > 0))
        def _():
            z_copy(g, q, 0).wait_send()

    def copies(g, q, d, src=None):
        src = tile(g, q, d) if src is None else src
        return (
            send(src, tile(g, q, d), xs.at[g, q], xr.at[g, q], (nx, z)),
            send(src, tile(g, q, d), ys.at[g, q], yr.at[g, q], (ny, z)),
        )

    def core_copy(g, q, pos, src=None):
        d = 2 * pos + c
        src = tile(g, q, d) if src is None else src
        return send(src, tile(g, q, d), cs.at[g, q, pos], cr.at[g, q, pos], (nc, z))

    def forward(g, q, along_y):
        if along_y:
            return send(tile(g, q, nx), tile(g, q, nx), ds.at[g, q], dr.at[g, q], (ny, z))
        return send(tile(g, q, ny), tile(g, q, ny), ds.at[g, q], dr.at[g, q], (nx, z))

    def own_start(g):
        z_start(g, None)
        for cp in copies(g, z, dp, own_ref.at[g]) + (core_copy(g, z, yx, own_ref.at[g]),):
            cp.start()
        pltpu.make_async_copy(own_ref.at[g], tile(g, z, dp), local_sem.at[2 + g]).start()

    def z_phase(g):
        def step(k, _):
            q = nearest(z, k)
            send(tile(g, q, dp), tile(g, q, dp), zs.at[g, q, 0], zr.at[g, q], (dp, z)).wait_recv()
            z_start(g, q)
            for cp in copies(g, q, dp) + (core_copy(g, q, yx),):
                cp.start()
            return 0

        lax.fori_loop(1, 4, step, 0)

    def xy_phase(g):
        def step(k, _):
            q = nearest(z, k)
            copies(g, q, nx)[0].wait_recv()

            @pl.when(q < 2)
            def _():
                forward(g, q, True).start()

            core_copy(g, q, yx_x).start()
            copies(g, q, ny)[1].wait_recv()

            @pl.when(q >= 2)
            def _():
                forward(g, q, False).start()

            core_copy(g, q, yx_y).start()
            return 0

        lax.fori_loop(0, 4, step, 0)

    def diagonal_phase(g):
        def step(k, _):
            q = nearest(z, k)
            d = 2 * yx_d + c
            send(tile(g, q, d), tile(g, q, d), ds.at[g, q], dr.at[g, q], (nx, z)).wait_recv()
            core_copy(g, q, yx_d).start()
            return 0

        lax.fori_loop(0, 4, step, 0)

    def finish(g):
        def step(q, _):
            z_done(g, q)
            for cp in copies(g, q, dp):
                cp.wait_send()

            @pl.when(q < 2)
            def _():
                forward(g, q, True).wait_send()

            @pl.when(q >= 2)
            def _():
                forward(g, q, False).wait_send()

            for pos in range(4):
                core_copy(g, q, pos).wait_send()
                d = 2 * pos + 1 - c
                send(
                    tile(g, q, d), tile(g, q, d), cs.at[g, q, pos], cr.at[g, q, pos], (nc, z)
                ).wait_recv()
            return 0

        lax.fori_loop(0, 4, step, 0)
        pltpu.make_async_copy(own_ref.at[g], tile(g, z, dp), local_sem.at[2 + g]).wait()

    own_start(0)
    rows_out(0, x_ref, xrow_ref)
    for i in range(1, 8):
        to = lax.rem(dp + i, 8)
        send(gain_ref, gains_ref.at[dp], gs.at[to], gr.at[dp], (to, z)).start()
    pltpu.make_async_copy(gain_ref, gains_ref.at[dp], local_sem.at[5]).start()
    own_start(1)
    z_phase(0)
    rows_out(1, ct_ref, ctrow_ref)
    z_phase(1)
    own_start(2)
    xy_phase(0)
    z_phase(2)
    xy_phase(1)
    diagonal_phase(0)
    xy_phase(2)
    diagonal_phase(1)
    diagonal_phase(2)
    rows_wait(0, x_ref, xrow_ref)
    rows_wait(1, ct_ref, ctrow_ref)
    for i in range(1, 8):
        other = lax.rem(dp + i, 8)
        cp = send(gain_ref, gains_ref.at[other], gs.at[other], gr.at[other], (other, z))
        cp.wait_send()
        cp.wait_recv()
    pltpu.make_async_copy(gain_ref, gains_ref.at[dp], local_sem.at[5]).wait()
    for g in range(3):
        finish(g)


def gather(own, gain, x, ct):
    sem = pltpu.SemaphoreType.DMA
    anywhere = pl.BlockSpec(memory_space=pl.ANY)
    return pl.pallas_call(
        gather_kernel,
        out_shape=(
            jax.ShapeDtypeStruct((3, 4, 8, 96, D), BF),
            jax.ShapeDtypeStruct((8,) + gain.shape, gain.dtype),
            jax.ShapeDtypeStruct(x.shape, BF),
            jax.ShapeDtypeStruct(ct.shape, BF),
        ),
        in_specs=[anywhere] * 4,
        out_specs=(anywhere,) * 4,
        scratch_shapes=[
            sem((6,)),
            sem((3, 4, 2)), sem((3, 4)),
            sem((3, 4)), sem((3, 4)),
            sem((3, 4)), sem((3, 4)),
            sem((3, 4)), sem((3, 4)),
            sem((3, 4, 4)), sem((3, 4, 4)),
            sem((8,)), sem((8,)),
            sem((2, 4)), sem((2, 4)),
        ],
        compiler_params=pltpu.CompilerParams(collective_id=0, has_side_effects=True),
        name="gather_weights_and_rows",
    )(own, gain, x, ct)


def scatter_kernel(
    grads_ref, gg_ref, out_ref, dx_ref,
    total_ref, gain_ref, outs_ref, dxs_ref,
    sums, from_core, corner, from_x, from_y, from_z, small, small_z,
    local_sem, cs, cr, ks, kr, xs, xr, ys, yr, zs, zr, gs, gr, gzs, gzr, as_, ar,
):
    dp, z, c, nx, ny, nc = place()
    yx, yx_x, yx_y, yx_d = dp // 2, nx // 2, ny // 2, 3 - dp // 2
    greet(dp, z, 8, 4)

    def rows_out(i, src, dst):
        for j in range(1, 4):
            q = lax.rem(z + j, 4)
            send(src.at[q], dst.at[z], as_.at[i, q], ar.at[i, z], (dp, q)).start()
        pltpu.make_async_copy(src.at[z], dst.at[z], local_sem.at[i]).start()

    def rows_wait(i, src, dst):
        for j in range(1, 4):
            q = lax.rem(z + j, 4)
            cp = send(src.at[q], dst.at[q], as_.at[i, q], ar.at[i, q], (dp, q))
            cp.wait_send()
            cp.wait_recv()
        pltpu.make_async_copy(src.at[z], dst.at[z], local_sem.at[i]).wait()

    def core_copy(g, q):
        return send(
            grads_ref.at[g, q, :, 1 - c], from_core.at[g, q], cs.at[g, q], cr.at[g, q], (nc, z)
        )

    def corner_copy(g, q):
        to = nx if q < 2 else ny
        return send(sums.at[g, q, yx_d], corner.at[g, q], ks.at[g, q], kr.at[g, q], (to, z))

    def x_copy(g, q):
        return send(sums.at[g, q, yx_x], from_x.at[g, q], xs.at[g, q], xr.at[g, q], (nx, z))

    def y_copy(g, q):
        return send(sums.at[g, q, yx_y], from_y.at[g, q], ys.at[g, q], yr.at[g, q], (ny, z))

    def z_copy(g, q):
        return send(sums.at[g, q, yx], from_z.at[g, z], zs.at[g, q], zr.at[g, z], (dp, q))

    def core_start(g):
        for q in range(4):
            core_copy(g, q).start()

    def core_add(g):
        for q in range(4):
            core_copy(g, q).wait_recv()

            def step(pos, _):
                sums[g, q, pos] = (
                    grads_ref[g, q, pos, c].astype(F32) + from_core[g, q, pos].astype(F32)
                ).astype(BF)
                return 0

            lax.fori_loop(0, 4, step, 0)
            corner_copy(g, q).start()
            (x_copy if q < 2 else y_copy)(g, q).start()

    def corner_add(g):
        for q in range(4):
            corner_copy(g, q).wait_recv()
            pos = yx_y if q < 2 else yx_x
            sums[g, q, pos] = (
                sums[g, q, pos].astype(F32) + corner[g, q].astype(F32)
            ).astype(BF)
            (y_copy if q < 2 else x_copy)(g, q).start()

    def plane_add(g):
        for q in range(4):
            x_copy(g, q).wait_recv()
            y_copy(g, q).wait_recv()
            sums[g, q, yx] = (
                sums[g, q, yx].astype(F32) + from_x[g, q].astype(F32) + from_y[g, q].astype(F32)
            ).astype(BF)

            @pl.when(z != q)
            def _():
                z_copy(g, q).start()

    def last_add(g):
        total = sums[g, z, yx].astype(F32)
        for j in range(1, 4):
            q = lax.rem(z + j, 4)
            send(sums.at[g, q, yx], from_z.at[g, q], zs.at[g, q], zr.at[g, q], (dp, q)).wait_recv()
            total = total + from_z[g, q].astype(F32)
        total_ref[g] = total

    def finish(g):
        for q in range(4):
            core_copy(g, q).wait_send()
            corner_copy(g, q).wait_send()
            x_copy(g, q).wait_send()
            y_copy(g, q).wait_send()

            @pl.when(z != q)
            def _():
                z_copy(g, q).wait_send()

    for g in (2, 1, 0):
        core_start(g)
    rows_out(0, out_ref, outs_ref)
    rows_out(1, dx_ref, dxs_ref)
    core_add(2)
    core_add(1)
    corner_add(2)
    core_add(0)
    corner_add(1)
    plane_add(2)
    gain_ref[...] = gg_ref[...]
    for i, to in enumerate((nc, nx, ny)):
        cp = send(gain_ref, small.at[i], gs.at[i], gr.at[i], (to, z))
        cp.start()
        cp.wait()
        gain_ref[...] += small[i]
    corner_add(0)
    plane_add(1)
    for j in range(1, 4):
        q = lax.rem(z + j, 4)
        send(gain_ref, small_z.at[z], gzs.at[q], gzr.at[z], (dp, q)).start()
    last_add(2)
    plane_add(0)
    last_add(1)
    total = gain_ref[...]
    for j in range(1, 4):
        q = lax.rem(z + j, 4)
        cp = send(gain_ref, small_z.at[q], gzs.at[q], gzr.at[q], (dp, q))
        cp.wait_recv()
        cp.wait_send()
        total = total + small_z[q]
    gain_ref[...] = total
    last_add(0)
    for g in (2, 1, 0):
        finish(g)
    rows_wait(0, out_ref, outs_ref)
    rows_wait(1, dx_ref, dxs_ref)


def scatter(grads, gg, out, dx):
    sem = pltpu.SemaphoreType.DMA
    anywhere = pl.BlockSpec(memory_space=pl.ANY)
    vmem = pl.BlockSpec(memory_space=pltpu.VMEM)
    return pl.pallas_call(
        scatter_kernel,
        out_shape=(
            jax.ShapeDtypeStruct((3, 96, D), F32),
            jax.ShapeDtypeStruct((8, D), F32),
            jax.ShapeDtypeStruct(out.shape, BF),
            jax.ShapeDtypeStruct(dx.shape, BF),
        ),
        in_specs=[vmem, vmem, anywhere, anywhere],
        out_specs=(vmem, vmem, anywhere, anywhere),
        scratch_shapes=[
            pltpu.VMEM((3, 4, 4, 96, D), BF),
            pltpu.VMEM((3, 4, 4, 96, D), BF),
            pltpu.VMEM((3, 4, 96, D), BF),
            pltpu.VMEM((3, 4, 96, D), BF),
            pltpu.VMEM((3, 4, 96, D), BF),
            pltpu.VMEM((3, 4, 96, D), BF),
            pltpu.VMEM((3, 8, D), F32),
            pltpu.VMEM((4, 8, D), F32),
            sem((2,)),
            sem((3, 4)), sem((3, 4)),
            sem((3, 4)), sem((3, 4)),
            sem((3, 4)), sem((3, 4)),
            sem((3, 4)), sem((3, 4)),
            sem((3, 4)), sem((3, 4)),
            sem((3,)), sem((3,)),
            sem((4,)), sem((4,)),
            sem((2, 4)), sem((2, 4)),
        ],
        compiler_params=pltpu.CompilerParams(
            collective_id=1, has_side_effects=True, vmem_limit_bytes=56 * 2**20
        ),
        name="sum_gradients_and_return_rows",
    )(grads, gg, out, dx)


def shards(
    inputs, segment_ids, w_query, w_key, w_value, w_output, w_up, w_down, gain_attn, gain_ffn, cotangent,
    *, parts, quarters,
):
    rows, local, _ = inputs.shape
    depth = w_up.shape[0]
    width = w_query.shape[1]
    z = lax.axis_index("mp")
    segment = lax.dynamic_index_in_dim(segment_ids, z, 0, keepdims=False)
    own = jnp.stack(
        [jnp.concatenate([w_query, w_value, w_key, w_output.T], axis=1), w_up, w_down.T]
    )
    kernels = parts == 8 and quarters == 4
    if kernels:
        gain = jnp.zeros((16, 128), BF)
        gain = gain.at[0, :depth].set(gain_attn).at[1, :depth].set(gain_ffn)
        weights, gains, x, ct = gather(own, gain, inputs, cotangent)
        weights = weights.reshape(3, quarters, D, D)
        gains = gains[:, :2, :depth].swapaxes(0, 1).reshape(2, D)
    else:
        weights = lax.all_gather(own, ("dp", "mp"), axis=0).reshape(parts, quarters, 3, depth, D)
        weights = weights.transpose(2, 1, 0, 3, 4).reshape(3, quarters, D, D)
        gains = jnp.stack(
            [lax.all_gather(g, "dp", axis=0, tiled=True) for g in (gain_attn, gain_ffn)]
        )
        x, ct = (
            lax.all_to_all(a, "mp", split_axis=0, concat_axis=0, tiled=True) for a in (inputs, cotangent)
        )
    gains = gains.astype(F32)
    out, dx, grads, gg = row_layer(
        x.reshape(-1, D), ct.reshape(-1, D), segment, weights, gains[0], gains[1]
    )
    out, dx = out.reshape(inputs.shape), dx.reshape(inputs.shape)
    if kernels:
        total, gg, out, dx = scatter(
            grads.reshape(3, 4, 4, 2, 96, D), jnp.pad(gg, ((0, 6), (0, 0))), out, dx
        )
        gg = lax.dynamic_slice_in_dim(gg, lax.axis_index("dp") * depth, depth, 1)
    else:
        grads = grads.reshape(3, quarters, parts, depth, D).transpose(2, 1, 0, 3, 4)
        grads = grads.reshape(parts * quarters, 3, depth, D)
        total = lax.psum_scatter(grads, ("dp", "mp"), scatter_dimension=0).astype(F32)
        gg = lax.psum(lax.psum_scatter(gg, "dp", scatter_dimension=1, tiled=True), "mp")
        out, dx = (
            lax.all_to_all(a, "mp", split_axis=0, concat_axis=0, tiled=True) for a in (out, dx)
        )
    return (
        out,
        dx,
        total[0, :, :width],
        total[0, :, 2 * width : 3 * width],
        total[0, :, width : 2 * width],
        total[0, :, 3 * width :].T,
        total[1],
        total[2].T,
        gg[0],
        gg[1],
    )


def solution(mesh):
    by_row = P("dp", "mp", None)
    grids = (P("dp", "mp"), P("dp", "mp"), P("dp", "mp"), P("mp", "dp"), P("dp", "mp"), P("mp", "dp"))
    gains = (P("dp"), P("dp"))
    return jax.shard_map(
        functools.partial(shards, parts=mesh.shape["dp"], quarters=mesh.shape["mp"]),
        mesh=mesh,
        in_specs=(by_row, P("dp", None)) + grids + gains + (by_row,),
        out_specs=(by_row, by_row) + grids + gains,
        check_vma=False,
    )
```

```python
import functools

import jax
import jax.numpy as jnp
from jax import lax
from jax.experimental import pallas as pl
from jax.experimental.pallas import tpu as pltpu
from jax.sharding import PartitionSpec as P

D = 768
HEADS = 12
HEAD = 64
EPS = 1e-05
MESH = pl.DeviceIdType.MESH
BF = jnp.bfloat16
F32 = jnp.float32


def dot(left, right, dims):
    return lax.dot_general(left, right, (dims, ((), ())), preferred_element_type=F32)


def natural(left, right):
    return dot(left, right, ((1,), (0,)))


def against(left, right):
    return dot(left, right, ((1,), (1,)))


def inner(left, right):
    return dot(left, right, ((0,), (0,)))


def norm(values):
    shifted = values - jnp.mean(values, axis=1, keepdims=True)
    scale = lax.rsqrt(jnp.mean(shifted * shifted, axis=1, keepdims=True) + EPS)
    return shifted * scale, scale


def norm_back(grad, xhat, scale, gain):
    e = grad * gain
    back = scale * (
        e - jnp.mean(e, axis=1, keepdims=True) - xhat * jnp.mean(e * xhat, axis=1, keepdims=True)
    )
    return back, jnp.sum(grad * xhat, axis=0)


def columns(w, first, count):
    part = w[:, :, first : first + count]
    return jnp.swapaxes(part, 0, 1).reshape(D, -1)


def row_layer(x, cotangent, segment, weights, gain_attn, gain_ffn):
    length = x.shape[0]
    quarters = weights.shape[1]
    width = D // quarters
    attn, up, down = weights[0], weights[1], weights[2]
    w_query, w_value, w_key, w_out = (columns(attn, i * width, width) for i in range(4))
    w_up, w_down = columns(up, 0, D), columns(down, 0, D)
    x = x.astype(F32)
    xhat_a, scale_a = norm(x)
    normed_a = (xhat_a * gain_attn).astype(BF)
    query, keys, values = (
        natural(normed_a, w).astype(BF).reshape(length, HEADS, HEAD) for w in (w_query, w_key, w_value)
    )
    same = segment[:, None] == segment[None, :]
    scores = jnp.einsum("qhd,khd->hqk", query, keys, preferred_element_type=F32) * HEAD**-0.5
    scores = jnp.where(same[None], scores, -1e30)
    exponent = jnp.exp(scores - jnp.max(scores, axis=2, keepdims=True))
    probs = exponent / jnp.sum(exponent, axis=2, keepdims=True)
    context = jnp.einsum("hqk,khd->qhd", probs.astype(BF), values, preferred_element_type=F32)
    context = context.reshape(length, D).astype(BF)
    middle = x + against(context, w_out)
    xhat_f, scale_f = norm(middle)
    normed_f = (xhat_f * gain_ffn).astype(BF)
    hidden = natural(normed_f, w_up)
    activated, gelu_back = jax.vjp(lambda v: jax.nn.gelu(v, approximate=False), hidden)
    activated = activated.astype(BF)
    output = (middle + against(activated, w_down)).astype(BF)

    grad_down = inner(cotangent, activated)
    grad_hidden = gelu_back(natural(cotangent, w_down))[0].astype(BF)
    grad_up = inner(normed_f, grad_hidden)
    back, grad_gain_ffn = norm_back(against(grad_hidden, w_up), xhat_f, scale_f, gain_ffn)
    grad_middle = cotangent.astype(F32) + back
    grad_attended = grad_middle.astype(BF)
    grad_out = inner(grad_attended, context)
    grad_context = natural(grad_attended, w_out).astype(BF).reshape(length, HEADS, HEAD)
    grad_probs = jnp.einsum("qhd,khd->hqk", grad_context, values, preferred_element_type=F32)
    grad_scores = (
        probs * (grad_probs - jnp.sum(probs * grad_probs, axis=2, keepdims=True))
    ).astype(BF)
    query_grad = jnp.einsum("hqk,khd->qhd", grad_scores, keys, preferred_element_type=F32) * HEAD**-0.5
    key_grad = jnp.einsum("hqk,qhd->khd", grad_scores, query, preferred_element_type=F32) * HEAD**-0.5
    value_grad = jnp.einsum(
        "hqk,qhd->khd", probs.astype(BF), grad_context, preferred_element_type=F32
    )
    query_grad, key_grad, value_grad = (
        g.reshape(length, D).astype(BF) for g in (query_grad, key_grad, value_grad)
    )
    grad_normed_a = (
        against(query_grad, w_query) + against(key_grad, w_key) + against(value_grad, w_value)
    )
    back, grad_gain_attn = norm_back(grad_normed_a, xhat_a, scale_a, gain_attn)
    input_grad = (grad_middle + back).astype(BF)

    def quarter(g, count):
        return g.astype(BF).reshape(D, quarters, count).swapaxes(0, 1)

    grads_attn = jnp.concatenate(
        [
            quarter(g, width)
            for g in (
                inner(normed_a, query_grad),
                inner(normed_a, value_grad),
                inner(normed_a, key_grad),
                grad_out,
            )
        ],
        axis=2,
    )
    grads = jnp.stack([grads_attn, quarter(grad_up, D), quarter(grad_down, D)])
    return output, input_grad, grads, jnp.stack([grad_gain_attn, grad_gain_ffn])


def between(value, first, count):
    lane = lax.broadcasted_iota(jnp.int32, value.shape, 1)
    return jnp.where((lane >= first) & (lane < first + count), value, jnp.zeros_like(value))


def place():
    dp, z = lax.axis_index("dp"), lax.axis_index("mp")
    c, x, y = lax.rem(dp, 2), lax.rem(dp // 2, 2), dp // 4
    return dp, z, c, dp + 2 - 4 * x, dp + 4 - 8 * y, dp + 1 - 2 * c


def send(src, dst, ssem, rsem, device):
    return pltpu.make_async_remote_copy(
        src_ref=src, dst_ref=dst, send_sem=ssem, recv_sem=rsem, device_id=device, device_id_type=MESH
    )


def nearest(z, k):
    inner_place = lax.rem((z + 1) // 2, 2)
    first_two = 1 - k // 2
    base = k + inner_place * first_two * (1 - 2 * k)
    return base + (z // 2) * (3 - 2 * base)


def gain_row(parts_ref, index):
    r = lax.broadcasted_iota(jnp.int32, (128, D), 0)
    col = lax.broadcasted_iota(jnp.int32, (128, D), 1)
    spread = jnp.where(lax.rem(col, 96) == r, 1.0, 0.0).astype(BF)
    total = jnp.zeros((1, D), F32)
    col = lax.broadcasted_iota(jnp.int32, (16, D), 1)
    row = lax.broadcasted_iota(jnp.int32, (16, D), 0)
    for p in range(8):
        full = natural(parts_ref[p], spread)
        keep = (row == index) & (col >= 96 * p) & (col < 96 * (p + 1))
        total = total + jnp.sum(jnp.where(keep, full, 0.0), axis=0, keepdims=True)
    return total


BLOCK = 128
LEN = 512


def block(i):
    return pl.ds(pl.multiple_of(i * BLOCK, BLOCK), BLOCK)


def loop(count, step):
    def body(i, _):
        step(i)
        return 0

    lax.fori_loop(0, count, body, 0)


def layer_kernel(
    x_in, ct_in, seg_ref, wq_ref, wk_ref, wv_ref, wo_ref, wup_ref, wdown_ref, ga_ref, gf_ref,
    total_ref, gain_ref, outs_ref, dxs_ref, wide_ref,
    own, gain_own, gain_all, attn, held, x_ref, ct_ref, out_ref, dx_ref,
    nrm, na_t, nf_t, ct_t, ga_t, qb, kb, vb, cb, lse_ref, bias, mid, acc, act, gp,
    staged, sums, from_core, corner, from_plane, from_z, small, small_z, gain_sum,
    local_sem, held_sem, zs, zr, xs, xr, ys, yr, ds, dr, cs, cr, gs, gr, as_, ar,
    ecs, ecr, eks, ekr, eps, epr, ezs, ezr, egs, egr, egzs, egzr,
):
    dp, z, c, nx, ny, nc = place()
    yx, yx_x, yx_y, yx_d = dp // 2, nx // 2, ny // 2, 3 - dp // 2

    barrier = pltpu.get_barrier_semaphore()
    for i in range(1, 8):
        pl.semaphore_signal(barrier, inc=1, device_id=(lax.rem(dp + i, 8), z), device_id_type=MESH)
    for i in range(1, 4):
        pl.semaphore_signal(barrier, inc=1, device_id=(dp, lax.rem(z + i, 4)), device_id_type=MESH)

    own[0] = jnp.concatenate(
        [wq_ref[...], wv_ref[...], wk_ref[...], wo_ref[...].T], axis=1
    )
    own[1] = wup_ref[...]
    own[2] = wdown_ref[...].T
    gain_own[...] = jnp.zeros_like(gain_own)
    gain_own[0:1, 0:96] = ga_ref[...]
    gain_own[1:2, 0:96] = gf_ref[...]
    pl.semaphore_wait(barrier, 10)

    def rows_start(i, src, dst):
        for j in range(1, 4):
            q = lax.rem(z + j, 4)
            send(src.at[q], dst.at[z], as_.at[i, q], ar.at[i, z], (dp, q)).start()
        pltpu.make_async_copy(src.at[z], dst.at[z], local_sem.at[i]).start()

    def rows_wait(i, src, dst):
        for j in range(1, 4):
            q = lax.rem(z + j, 4)
            cp = send(src.at[q], dst.at[q], as_.at[i, q], ar.at[i, q], (dp, q))
            cp.wait_send()
            cp.wait_recv()
        pltpu.make_async_copy(src.at[z], dst.at[z], local_sem.at[i]).wait()

    def tile(g, q, d):
        return attn.at[q, d] if g == 0 else wide_ref.at[g - 1, q, d]

    def z_copy(g, q, side):
        to = z + (1 if side else -1)
        src = own.at[g] if q is None else tile(g, q, dp)
        q = z if q is None else q
        return send(src, tile(g, q, dp), zs.at[g, q, side], zr.at[g, q], (dp, to))

    def z_pass(g, q):
        origin = z if q is None else q

        @pl.when((origin <= z) & (z < 3))
        def _():
            z_copy(g, q, 1).start()

        @pl.when((origin >= z) & (z > 0))
        def _():
            z_copy(g, q, 0).start()

    def z_done(g, q):
        @pl.when((q <= z) & (z < 3))
        def _():
            z_copy(g, q, 1).wait_send()

        @pl.when((q >= z) & (z > 0))
        def _():
            z_copy(g, q, 0).wait_send()

    def x_copy(g, q, src=None):
        src = tile(g, q, dp) if src is None else src
        return send(src, tile(g, q, dp), xs.at[g, q], xr.at[g, q], (nx, z))

    def y_copy(g, q, src=None):
        src = tile(g, q, dp) if src is None else src
        return send(src, tile(g, q, dp), ys.at[g, q], yr.at[g, q], (ny, z))

    def core_copy(g, q, pos, src=None):
        d = 2 * pos + c
        src = tile(g, q, d) if src is None else src
        return send(src, tile(g, q, d), cs.at[g, q, pos], cr.at[g, q, pos], (nc, z))

    def forward(g, q, along_y):
        src, to = (nx, ny) if along_y else (ny, nx)
        return send(tile(g, q, src), tile(g, q, src), ds.at[g, q], dr.at[g, q], (to, z))

    def own_start(g):
        z_pass(g, None)
        x_copy(g, z, own.at[g]).start()
        y_copy(g, z, own.at[g]).start()
        core_copy(g, z, yx, own.at[g]).start()
        pltpu.make_async_copy(own.at[g], tile(g, z, dp), local_sem.at[4 + g]).start()

    def z_step(g, k):
        q = nearest(z, k)
        send(tile(g, q, dp), tile(g, q, dp), zs.at[g, q, 0], zr.at[g, q], (dp, z)).wait_recv()
        z_pass(g, q)
        x_copy(g, q).start()
        y_copy(g, q).start()
        core_copy(g, q, yx).start()

    def plane_step(g, k):
        q = nearest(z, k)
        x_copy(g, q).wait_recv()

        @pl.when(q < 2)
        def _():
            forward(g, q, True).start()

        core_copy(g, q, yx_x).start()
        y_copy(g, q).wait_recv()

        @pl.when(q >= 2)
        def _():
            forward(g, q, False).start()

        core_copy(g, q, yx_y).start()

    def far_step(g, k):
        q = nearest(z, k)
        d = 2 * yx_d + c
        send(tile(g, q, d), tile(g, q, d), ds.at[g, q], dr.at[g, q], (nx, z)).wait_recv()
        core_copy(g, q, yx_d).start()

    def core_ready(g, q):
        for pos in range(4):
            d = 2 * pos + 1 - c
            send(
                tile(g, q, d), tile(g, q, d), cs.at[g, q, pos], cr.at[g, q, pos], (nc, z)
            ).wait_recv()

    def weights_sent(g):
        def step(q):
            z_done(g, q)
            x_copy(g, q).wait_send()
            y_copy(g, q).wait_send()

            @pl.when(q < 2)
            def _():
                forward(g, q, True).wait_send()

            @pl.when(q >= 2)
            def _():
                forward(g, q, False).wait_send()

            for pos in range(4):
                core_copy(g, q, pos).wait_send()

        loop(4, step)

    def own_ready(g):
        pltpu.make_async_copy(own.at[g], tile(g, z, dp), local_sem.at[4 + g]).wait()

    def hold(g, q, slot):
        return pltpu.make_async_copy(wide_ref.at[g - 1, q], held.at[slot], held_sem.at[slot])

    def out_core(g, q):
        return send(staged.at[q], from_core.at[g, q], ecs.at[g, q], ecr.at[g, q], (nc, z))

    def out_corner(g, q):
        to = nx + (ny - nx) * (q // 2)
        return send(sums.at[g, q, yx_d], corner.at[g, q], eks.at[g, q], ekr.at[g, q], (to, z))

    def out_plane(g, q, side):
        to = nx + (ny - nx) * side
        pos = yx_x + (yx_y - yx_x) * side
        return send(
            sums.at[g, q, pos], from_plane.at[g, q, side], eps.at[g, q, side], epr.at[g, q, side], (to, z)
        )

    def out_z(g, q):
        return send(sums.at[g, q, yx], from_z.at[g, z], ezs.at[g, q], ezr.at[g, z], (dp, q))

    def core_add(g, q):
        out_core(g, q).wait_recv()

        def step(pos):
            sums[g, q, pos] = (
                sums[g, q, pos].astype(F32) + from_core[g, q, pos].astype(F32)
            ).astype(BF)

        loop(4, step)
        out_corner(g, q).start()
        out_plane(g, q, q // 2).start()

    def corner_add(g, q):
        side = 1 - q // 2
        pos = yx_x + (yx_y - yx_x) * side
        out_corner(g, q).wait_recv()
        sums[g, q, pos] = (sums[g, q, pos].astype(F32) + corner[g, q].astype(F32)).astype(BF)
        out_plane(g, q, side).start()

    def plane_add(g, q):
        out_plane(g, q, 0).wait_recv()
        out_plane(g, q, 1).wait_recv()
        sums[g, q, yx] = (
            sums[g, q, yx].astype(F32)
            + from_plane[g, q, 0].astype(F32)
            + from_plane[g, q, 1].astype(F32)
        ).astype(BF)

        @pl.when(z != q)
        def _():
            out_z(g, q).start()

    def last_add(g):
        total = sums[g, z, yx].astype(F32)
        for j in range(1, 4):
            q = lax.rem(z + j, 4)
            send(sums.at[g, q, yx], from_z.at[g, q], ezs.at[g, q], ezr.at[g, q], (dp, q)).wait_recv()
            total = total + from_z[g, q].astype(F32)
        total_ref[g] = total

    def grads_sent(g):
        def step(q):
            out_corner(g, q).wait_send()
            out_plane(g, q, 0).wait_send()
            out_plane(g, q, 1).wait_send()

            @pl.when(z != q)
            def _():
                out_z(g, q).wait_send()

        loop(4, step)

    def emit(g, q, left, right, left_2=None, right_2=None):
        if g < 2:
            out_core(g + 1, q).wait_send()
        for other in (True, False):
            half = 1 - c if other else c
            dst = staged.at[q] if other else sums.at[g, q]
            v = natural(left[:, half].reshape(384, LEN), right)
            if right_2 is None:
                dst[...] = v.astype(BF).reshape(4, 96, D)
            else:
                v2 = natural(left_2[:, half].reshape(384, LEN), right_2)
                dst[:, :, 0:512] = v[:, 0:512].astype(BF).reshape(4, 96, 512)
                dst[:, :, 512:640] = (v[:, 512:640] + v2[:, 0:128]).astype(BF).reshape(4, 96, 128)
                dst[:, :, 640:768] = v2[:, 128:256].astype(BF).reshape(4, 96, 128)
            if other:
                out_core(g, q).start()

    def put_t(dst, i, v):
        dst[:, :, :, block(i)] = v.T.reshape(4, 2, 96, BLOCK)

    def add(i, value):
        @pl.when(i == 0)
        def _():
            acc[...] = value

        @pl.when(i > 0)
        def _():
            acc[...] += value

    own_start(0)
    for i in range(1, 8):
        to = lax.rem(dp + i, 8)
        send(gain_own, gain_all.at[dp], gs.at[to], gr.at[dp], (to, z)).start()
    gain_all[dp] = gain_own[...]
    loop(3, lambda k: z_step(0, k + 1))
    rows_start(0, x_in, x_ref)
    own_start(1)
    seg_row = seg_ref[pl.ds(z, 1)].astype(F32)
    seg_col = jnp.broadcast_to(seg_row, (8, LEN)).T[:, 0:1]
    bias[...] = jnp.where(seg_col == seg_row, 0.0, -1e30)
    gain_sum[...] = jnp.zeros_like(gain_sum)
    loop(4, lambda k: plane_step(0, k))
    loop(3, lambda k: z_step(1, k + 1))
    own_start(2)
    for i in range(1, 8):
        other = lax.rem(dp + i, 8)
        send(gain_own, gain_all.at[other], gs.at[other], gr.at[other], (other, z)).wait_recv()
    gain_a = gain_row(gain_all, 0)
    gain_f = gain_row(gain_all, 1)
    loop(4, lambda k: far_step(0, k))
    rows_wait(0, x_in, x_ref)

    def norm_a(i):
        xhat, _ = norm(x_ref[i].astype(F32))
        normed = (xhat * gain_a).astype(BF)
        nrm[block(i)] = normed
        put_t(na_t, i, normed)

    loop(4, norm_a)
    own_ready(0)

    def attend(i):
        q = nearest(z, i)
        core_ready(0, q)
        w = attn[q].reshape(D, D)
        p = natural(nrm[...], w[:, 0:640])
        q8 = p[:, 0:256].astype(BF) * jnp.asarray(0.125, BF)
        v = p[:, 128:384].astype(BF)
        k = p[:, 384:640].astype(BF)
        qb[q] = q8
        vb[q] = v
        kb[q] = k
        for h in range(3):
            for r in range(2):
                rs = slice(256 * r, 256 * (r + 1))
                s = against(between(q8[rs], 64 * h, 64), k) + bias[rs]
                m = jnp.max(s, axis=1, keepdims=True)
                e = jnp.exp(s - m)
                total = jnp.sum(e, axis=1, keepdims=True)
                probs = (e * (1.0 / total)).astype(BF)
                part = between(natural(probs, v), 64 + 64 * h, 64).astype(BF)
                if h == 0:
                    cb[q, rs] = part
                else:
                    cb[q, rs] += part
                lane = lax.broadcasted_iota(jnp.int32, (256, 128), 1)
                lse_ref[rs] = jnp.where(lane == 3 * q + h, m + jnp.log(total), lse_ref[rs])
            if h == 0:
                plane_step(1, i)
            if h == 1:
                @pl.when(i < 3)
                def _():
                    z_step(2, i + 1)

    loop(4, attend)
    rows_start(1, ct_in, ct_ref)

    def attend_out(i):
        add(i, against(cb[i], attn[i].reshape(D, D)[:, 512:768]))
        far_step(1, i)

    loop(4, attend_out)
    own_ready(1)

    def norm_f(i):
        m = x_ref[i].astype(F32) + acc[block(i)]
        mid[block(i)] = m
        xhat, _ = norm(m)
        normed = (xhat * gain_f).astype(BF)
        nrm[block(i)] = normed
        put_t(nf_t, i, normed)

    loop(4, norm_f)
    q = nearest(z, 0)
    core_ready(1, q)
    hold(1, q, 0).start()

    def up(i):
        q = nearest(z, i)
        slot = lax.rem(i, 2)

        @pl.when(i < 3)
        def _():
            later = nearest(z, i + 1)
            core_ready(1, later)
            hold(1, later, 1 - slot).start()

        hold(1, q, slot).wait()
        w = held[slot].reshape(D, D)
        for r in range(2):
            rs = slice(256 * r, 256 * (r + 1))
            h = natural(nrm[rs], w)
            cdf = 0.5 + 0.5 * lax.erf(h * 0.7071067811865476)
            act[q, rs] = (h * cdf).astype(BF)
            gp[q, rs] = (cdf + h * (jnp.exp(-0.5 * h * h) * 0.3989422804014327)).astype(BF)
        plane_step(2, i)

    loop(4, up)
    rows_wait(1, ct_in, ct_ref)

    def turn_ct(i):
        put_t(ct_t, i, ct_ref[i])
        far_step(2, i)

    loop(4, turn_ct)
    own_ready(2)

    def grad_down(i):
        emit(2, i, ct_t, act[i])

        @pl.when(i > 0)
        def _():
            core_add(2, i - 1)

    loop(4, grad_down)
    core_add(2, 3)
    q = nearest(z, 0)
    core_ready(2, q)
    hold(2, q, 0).start()

    def down(i):
        q = nearest(z, i)
        slot = lax.rem(i, 2)

        @pl.when(i < 3)
        def _():
            later = nearest(z, i + 1)
            core_ready(2, later)
            hold(2, later, 1 - slot).start()

        hold(2, q, slot).wait()
        w = held[slot].reshape(D, D)
        gp[q] = (natural(ct_ref[...].reshape(LEN, D), w) * gp[q].astype(F32)).astype(BF)
        add(i, against(act[q], w))

    loop(4, down)
    hold(1, 0, 0).start()
    out_ref[...] = (mid[...] + acc[...]).astype(BF).reshape(4, BLOCK, D)
    rows_start(2, out_ref, outs_ref)
    loop(4, lambda k: corner_add(2, k))

    def up_back(i):
        slot = lax.rem(i, 2)

        @pl.when(i < 3)
        def _():
            hold(1, i + 1, 1 - slot).start()

        hold(1, i, slot).wait()
        add(i, against(gp[i], held[slot].reshape(D, D)))
        emit(1, i, nf_t, gp[i])

        @pl.when(i > 0)
        def _():
            core_add(1, i - 1)

    loop(4, up_back)
    core_add(1, 3)

    def norm_f_back(i):
        xhat, scale = norm(mid[block(i)])
        back, grad_gain = norm_back(acc[block(i)], xhat, scale, gain_f)
        gain_sum[1:2] += grad_gain[None]
        grad_middle = ct_ref[i].astype(F32) + back
        mid[block(i)] = grad_middle
        attended = grad_middle.astype(BF)
        nrm[block(i)] = attended
        put_t(ga_t, i, attended)

    loop(4, norm_f_back)

    def attend_back(i):
        w = attn[i].reshape(D, D)
        dctx = between(natural(nrm[...], w[:, 512:768]), 64, 192).astype(BF)
        q8, v, k, cx = qb[i], vb[i], kb[i], cb[i]
        dq = jnp.zeros((LEN, 256), F32)
        dk = jnp.zeros((LEN, 256), F32)
        dv = jnp.zeros((LEN, 256), F32)
        for h in range(3):
            lane = lax.broadcasted_iota(jnp.int32, (LEN, 128), 1)
            lse = jnp.sum(jnp.where(lane == 3 * i + h, lse_ref[...], 0.0), axis=1, keepdims=True)
            p = jnp.exp(against(between(q8, 64 * h, 64), k) + bias[...] - lse)
            dm = between(dctx, 64 + 64 * h, 64)
            delta = jnp.sum(dm.astype(F32) * cx.astype(F32), axis=1, keepdims=True)
            ds_ = (p * (against(dm, v) - delta)).astype(BF)
            dq += between(natural(ds_, k), 64 * h, 64)
            dk += between(inner(ds_, q8), 64 * h, 64)
            dv += between(inner(p.astype(BF), dctx), 64 + 64 * h, 64)
            if h == 0:
                plane_add(2, i)
            if h == 1:
                corner_add(1, i)
        dq = dq * 0.125
        d = jnp.concatenate(
            [dq[:, 0:128], dq[:, 128:256] + dv[:, 0:128], dv[:, 128:256], dk], axis=1
        ).astype(BF)
        add(i, against(d, w[:, 0:640]))
        emit(0, i, na_t, d, ga_t, cx)

        @pl.when(i > 0)
        def _():
            core_add(0, i - 1)

    loop(4, attend_back)
    core_add(0, 3)

    def norm_a_back(i):
        xhat, scale = norm(x_ref[i].astype(F32))
        back, grad_gain = norm_back(acc[block(i)], xhat, scale, gain_a)
        gain_sum[0:1] += grad_gain[None]
        dx_ref[i] = (mid[block(i)] + back).astype(BF)

    loop(4, norm_a_back)
    rows_start(3, dx_ref, dxs_ref)
    last_add(2)

    def small_copy(i):
        return send(gain_sum, small.at[i], egs.at[i], egr.at[i], ((nc, nx, ny)[i], z))

    def small_add(i):
        small_copy(i).wait()
        gain_sum[...] += small[i]

    small_copy(0).start()
    loop(4, lambda k: corner_add(0, k))
    small_add(0)
    small_copy(1).start()
    loop(4, lambda k: plane_add(1, k))
    small_add(1)
    small_copy(2).start()
    last_add(1)
    small_add(2)
    for j in range(1, 4):
        q = lax.rem(z + j, 4)
        send(gain_sum, small_z.at[z], egzs.at[q], egzr.at[z], (dp, q)).start()
    loop(4, lambda k: plane_add(0, k))
    total = gain_sum[...]
    for j in range(1, 4):
        q = lax.rem(z + j, 4)
        cp = send(gain_sum, small_z.at[q], egzs.at[q], egzr.at[q], (dp, q))
        cp.wait()
        total = total + small_z[q]
    gain_ref[...] = total
    last_add(0)

    for i in range(1, 8):
        other = lax.rem(dp + i, 8)
        send(gain_own, gain_all.at[other], gs.at[other], gr.at[other], (other, z)).wait_send()
    for g in range(3):
        weights_sent(g)
        grads_sent(g)
    loop(4, lambda q: out_core(0, q).wait_send())
    rows_wait(2, out_ref, outs_ref)
    rows_wait(3, dx_ref, dxs_ref)


def layer(x, ct, segment_ids, w_query, w_key, w_value, w_output, w_up, w_down, gain_attn, gain_ffn):
    sem = pltpu.SemaphoreType.DMA
    vm = pltpu.VMEM
    anywhere = pl.BlockSpec(memory_space=pl.ANY)
    vmem = pl.BlockSpec(memory_space=pltpu.VMEM)
    return pl.pallas_call(
        layer_kernel,
        out_shape=(
            jax.ShapeDtypeStruct((3, 96, D), F32),
            jax.ShapeDtypeStruct((8, D), F32),
            jax.ShapeDtypeStruct(x.shape, BF),
            jax.ShapeDtypeStruct(x.shape, BF),
            jax.ShapeDtypeStruct((2, 4, 8, 96, D), BF),
        ),
        in_specs=[anywhere] * 2 + [vmem] * 9,
        out_specs=(vmem, vmem, anywhere, anywhere, anywhere),
        scratch_shapes=[
            vm((3, 96, D), BF), vm((16, 128), BF), vm((8, 16, 128), BF),
            vm((4, 8, 96, D), BF), vm((2, 8, 96, D), BF),
            vm((4, BLOCK, D), BF), vm((4, BLOCK, D), BF), vm((4, BLOCK, D), BF), vm((4, BLOCK, D), BF),
            vm((LEN, D), BF),
            vm((4, 2, 96, LEN), BF), vm((4, 2, 96, LEN), BF), vm((4, 2, 96, LEN), BF), vm((4, 2, 96, LEN), BF),
            vm((4, LEN, 256), BF), vm((4, LEN, 256), BF), vm((4, LEN, 256), BF), vm((4, LEN, 256), BF),
            vm((LEN, 128), F32), vm((LEN, LEN), F32), vm((LEN, D), F32), vm((LEN, D), F32),
            vm((4, LEN, D), BF), vm((4, LEN, D), BF),
            vm((4, 4, 96, D), BF), vm((3, 4, 4, 96, D), BF), vm((3, 4, 4, 96, D), BF),
            vm((3, 4, 96, D), BF), vm((3, 4, 2, 96, D), BF), vm((3, 4, 96, D), BF),
            vm((3, 8, D), F32), vm((4, 8, D), F32), vm((8, D), F32),
            sem((7,)), sem((2,)),
            sem((3, 4, 2)), sem((3, 4)),
            sem((3, 4)), sem((3, 4)),
            sem((3, 4)), sem((3, 4)),
            sem((3, 4)), sem((3, 4)),
            sem((3, 4, 4)), sem((3, 4, 4)),
            sem((8,)), sem((8,)),
            sem((4, 4)), sem((4, 4)),
            sem((3, 4)), sem((3, 4)),
            sem((3, 4)), sem((3, 4)),
            sem((3, 4, 2)), sem((3, 4, 2)),
            sem((3, 4)), sem((3, 4)),
            sem((3,)), sem((3,)),
            sem((4,)), sem((4,)),
        ],
        compiler_params=pltpu.CompilerParams(
            collective_id=0, has_side_effects=True, vmem_limit_bytes=VMEM_LIMIT
        ),
        name="layer_with_copies",
    )(x, ct, segment_ids, w_query, w_key, w_value, w_output, w_up, w_down, gain_attn, gain_ffn)


VMEM_LIMIT = 62 * 2**20


def shards(
    inputs, segment_ids, w_query, w_key, w_value, w_output, w_up, w_down, gain_attn, gain_ffn, cotangent,
    *, parts, quarters,
):
    depth, width = w_query.shape
    index = lax.axis_index("dp")
    if parts == 8 and quarters == 4:
        total, gg, out, dx, _ = layer(
            inputs, cotangent, segment_ids, w_query, w_key, w_value, w_output, w_up, w_down,
            gain_attn.reshape(1, depth), gain_ffn.reshape(1, depth),
        )
        gg = lax.dynamic_slice_in_dim(gg, index * depth, depth, 1)
    else:
        z = lax.axis_index("mp")
        segment = lax.dynamic_index_in_dim(segment_ids, z, 0, keepdims=False)
        own = jnp.stack(
            [jnp.concatenate([w_query, w_value, w_key, w_output.T], axis=1), w_up, w_down.T]
        )
        weights = lax.all_gather(own, ("dp", "mp"), axis=0).reshape(parts, quarters, 3, depth, D)
        weights = weights.transpose(2, 1, 0, 3, 4).reshape(3, quarters, D, D)
        gains = jnp.stack(
            [lax.all_gather(g, "dp", axis=0, tiled=True) for g in (gain_attn, gain_ffn)]
        ).astype(F32)
        x, ct = (
            lax.all_to_all(a, "mp", split_axis=0, concat_axis=0, tiled=True) for a in (inputs, cotangent)
        )
        out, dx, grads, gg = row_layer(
            x.reshape(-1, D), ct.reshape(-1, D), segment, weights, gains[0], gains[1]
        )
        grads = grads.reshape(3, quarters, parts, depth, D).transpose(2, 1, 0, 3, 4)
        grads = grads.reshape(parts * quarters, 3, depth, D)
        total = lax.psum_scatter(grads, ("dp", "mp"), scatter_dimension=0).astype(F32)
        gg = lax.psum(lax.psum_scatter(gg, "dp", scatter_dimension=1, tiled=True), "mp")
        out, dx = (
            lax.all_to_all(a.reshape(inputs.shape), "mp", split_axis=0, concat_axis=0, tiled=True)
            for a in (out, dx)
        )
    return (
        out,
        dx,
        total[0, :, :width],
        total[0, :, 2 * width : 3 * width],
        total[0, :, width : 2 * width],
        total[0, :, 3 * width :].T,
        total[1],
        total[2].T,
        gg[0],
        gg[1],
    )


def solution(mesh):
    by_row = P("dp", "mp", None)
    grids = (P("dp", "mp"), P("dp", "mp"), P("dp", "mp"), P("mp", "dp"), P("dp", "mp"), P("mp", "dp"))
    gains = (P("dp"), P("dp"))
    return jax.shard_map(
        functools.partial(shards, parts=mesh.shape["dp"], quarters=mesh.shape["mp"]),
        mesh=mesh,
        in_specs=(by_row, P("dp", None)) + grids + gains + (by_row,),
        out_specs=(by_row, by_row) + grids + gains,
        check_vma=False,
    )
```

```python
import functools

import jax
import jax.numpy as jnp
from jax import lax
from jax.experimental import pallas as pl
from jax.experimental.pallas import tpu as pltpu
from jax.sharding import PartitionSpec as P

D = 768
HEADS = 12
HEAD = 64
EPS = 1e-05
MESH = pl.DeviceIdType.MESH
BF = jnp.bfloat16
F32 = jnp.float32


def dot(left, right, dims):
    return lax.dot_general(left, right, (dims, ((), ())), preferred_element_type=F32)


def natural(left, right):
    return dot(left, right, ((1,), (0,)))


def against(left, right):
    return dot(left, right, ((1,), (1,)))


def inner(left, right):
    return dot(left, right, ((0,), (0,)))


def norm(values):
    shifted = values - jnp.mean(values, axis=1, keepdims=True)
    scale = lax.rsqrt(jnp.mean(shifted * shifted, axis=1, keepdims=True) + EPS)
    return shifted * scale, scale


def norm_back(grad, xhat, scale, gain):
    e = grad * gain
    back = scale * (
        e - jnp.mean(e, axis=1, keepdims=True) - xhat * jnp.mean(e * xhat, axis=1, keepdims=True)
    )
    return back, jnp.sum(grad * xhat, axis=0)


def columns(w, first, count):
    part = w[:, :, first : first + count]
    return jnp.swapaxes(part, 0, 1).reshape(D, -1)


def row_layer(x, cotangent, segment, weights, gain_attn, gain_ffn):
    length = x.shape[0]
    quarters = weights.shape[1]
    width = D // quarters
    attn, up, down = weights[0], weights[1], weights[2]
    w_query, w_value, w_key, w_out = (columns(attn, i * width, width) for i in range(4))
    w_up, w_down = columns(up, 0, D), columns(down, 0, D)
    x = x.astype(F32)
    xhat_a, scale_a = norm(x)
    normed_a = (xhat_a * gain_attn).astype(BF)
    query, keys, values = (
        natural(normed_a, w).astype(BF).reshape(length, HEADS, HEAD) for w in (w_query, w_key, w_value)
    )
    same = segment[:, None] == segment[None, :]
    scores = jnp.einsum("qhd,khd->hqk", query, keys, preferred_element_type=F32) * HEAD**-0.5
    scores = jnp.where(same[None], scores, -1e30)
    exponent = jnp.exp(scores - jnp.max(scores, axis=2, keepdims=True))
    probs = exponent / jnp.sum(exponent, axis=2, keepdims=True)
    context = jnp.einsum("hqk,khd->qhd", probs.astype(BF), values, preferred_element_type=F32)
    context = context.reshape(length, D).astype(BF)
    middle = x + against(context, w_out)
    xhat_f, scale_f = norm(middle)
    normed_f = (xhat_f * gain_ffn).astype(BF)
    hidden = natural(normed_f, w_up)
    activated, gelu_back = jax.vjp(lambda v: jax.nn.gelu(v, approximate=False), hidden)
    activated = activated.astype(BF)
    output = (middle + against(activated, w_down)).astype(BF)

    grad_down = inner(cotangent, activated)
    grad_hidden = gelu_back(natural(cotangent, w_down))[0].astype(BF)
    grad_up = inner(normed_f, grad_hidden)
    back, grad_gain_ffn = norm_back(against(grad_hidden, w_up), xhat_f, scale_f, gain_ffn)
    grad_middle = cotangent.astype(F32) + back
    grad_attended = grad_middle.astype(BF)
    grad_out = inner(grad_attended, context)
    grad_context = natural(grad_attended, w_out).astype(BF).reshape(length, HEADS, HEAD)
    grad_probs = jnp.einsum("qhd,khd->hqk", grad_context, values, preferred_element_type=F32)
    grad_scores = (
        probs * (grad_probs - jnp.sum(probs * grad_probs, axis=2, keepdims=True))
    ).astype(BF)
    query_grad = jnp.einsum("hqk,khd->qhd", grad_scores, keys, preferred_element_type=F32) * HEAD**-0.5
    key_grad = jnp.einsum("hqk,qhd->khd", grad_scores, query, preferred_element_type=F32) * HEAD**-0.5
    value_grad = jnp.einsum(
        "hqk,qhd->khd", probs.astype(BF), grad_context, preferred_element_type=F32
    )
    query_grad, key_grad, value_grad = (
        g.reshape(length, D).astype(BF) for g in (query_grad, key_grad, value_grad)
    )
    grad_normed_a = (
        against(query_grad, w_query) + against(key_grad, w_key) + against(value_grad, w_value)
    )
    back, grad_gain_attn = norm_back(grad_normed_a, xhat_a, scale_a, gain_attn)
    input_grad = (grad_middle + back).astype(BF)

    def quarter(g, count):
        return g.astype(BF).reshape(D, quarters, count).swapaxes(0, 1)

    grads_attn = jnp.concatenate(
        [
            quarter(g, width)
            for g in (
                inner(normed_a, query_grad),
                inner(normed_a, value_grad),
                inner(normed_a, key_grad),
                grad_out,
            )
        ],
        axis=2,
    )
    grads = jnp.stack([grads_attn, quarter(grad_up, D), quarter(grad_down, D)])
    return output, input_grad, grads, jnp.stack([grad_gain_attn, grad_gain_ffn])


def between(value, first, count):
    lane = lax.broadcasted_iota(jnp.int32, value.shape, 1)
    return jnp.where((lane >= first) & (lane < first + count), value, jnp.zeros_like(value))


def place():
    dp, z = lax.axis_index("dp"), lax.axis_index("mp")
    c, x, y = lax.rem(dp, 2), lax.rem(dp // 2, 2), dp // 4
    return dp, z, c, dp + 2 - 4 * x, dp + 4 - 8 * y, dp + 1 - 2 * c


def send(src, dst, ssem, rsem, device):
    return pltpu.make_async_remote_copy(
        src_ref=src, dst_ref=dst, send_sem=ssem, recv_sem=rsem, device_id=device, device_id_type=MESH
    )


def nearest(z, k):
    inner_place = lax.rem((z + 1) // 2, 2)
    first_two = 1 - k // 2
    base = k + inner_place * first_two * (1 - 2 * k)
    return base + (z // 2) * (3 - 2 * base)


def gain_row(parts_ref, index):
    r = lax.broadcasted_iota(jnp.int32, (128, D), 0)
    col = lax.broadcasted_iota(jnp.int32, (128, D), 1)
    spread = jnp.where(lax.rem(col, 96) == r, 1.0, 0.0).astype(BF)
    total = jnp.zeros((1, D), F32)
    col = lax.broadcasted_iota(jnp.int32, (16, D), 1)
    row = lax.broadcasted_iota(jnp.int32, (16, D), 0)
    for p in range(8):
        full = natural(parts_ref[p], spread)
        keep = (row == index) & (col >= 96 * p) & (col < 96 * (p + 1))
        total = total + jnp.sum(jnp.where(keep, full, 0.0), axis=0, keepdims=True)
    return total


BLOCK = 128
LEN = 512


def block(i):
    return pl.ds(pl.multiple_of(i * BLOCK, BLOCK), BLOCK)


def loop(count, step):
    def body(i, _):
        step(i)
        return 0

    lax.fori_loop(0, count, body, 0)


def layer_kernel(
    x_in, ct_in, seg_ref, wq_ref, wk_ref, wv_ref, wo_ref, wup_ref, wdown_ref, ga_ref, gf_ref,
    total_ref, gain_ref, outs_ref, dxs_ref, wide_ref,
    own, gain_own, gain_all, attn, held, x_ref, ct_ref, out_ref, dx_ref,
    nrm, na_t, nf_t, ct_t, ga_t, qb, kb, vb, cb, lse_ref, bias, mid, acc, act, gp,
    staged, sums, from_core, corner, from_plane, from_z, small, small_z, gain_sum, gain_parts,
    local_sem, held_sem, zs, zr, xs, xr, ys, yr, ds, dr, cs, cr, gs, gr, as_, ar,
    ecs, ecr, eks, ekr, eps, epr, ezs, ezr, egs, egr, egzs, egzr,
):
    dp, z, c, nx, ny, nc = place()
    yx, yx_x, yx_y, yx_d = dp // 2, nx // 2, ny // 2, 3 - dp // 2

    barrier = pltpu.get_barrier_semaphore()
    for i in range(1, 8):
        pl.semaphore_signal(barrier, inc=1, device_id=(lax.rem(dp + i, 8), z), device_id_type=MESH)
    for i in range(1, 4):
        pl.semaphore_signal(barrier, inc=1, device_id=(dp, lax.rem(z + i, 4)), device_id_type=MESH)

    own[0] = jnp.concatenate(
        [wq_ref[...], wv_ref[...], wk_ref[...], wo_ref[...].T], axis=1
    )
    own[1] = wup_ref[...]
    own[2] = wdown_ref[...]
    gain_own[...] = jnp.zeros_like(gain_own)
    gain_own[0:1, 0:96] = ga_ref[...]
    gain_own[1:2, 0:96] = gf_ref[...]
    pl.semaphore_wait(barrier, 10)

    def rows_start(i, src, dst):
        for j in range(1, 4):
            q = lax.rem(z + j, 4)
            send(src.at[q], dst.at[z], as_.at[i, q], ar.at[i, z], (dp, q)).start()
        pltpu.make_async_copy(src.at[z], dst.at[z], local_sem.at[i]).start()

    def rows_wait(i, src, dst):
        for j in range(1, 4):
            q = lax.rem(z + j, 4)
            cp = send(src.at[q], dst.at[q], as_.at[i, q], ar.at[i, q], (dp, q))
            cp.wait_send()
            cp.wait_recv()
        pltpu.make_async_copy(src.at[z], dst.at[z], local_sem.at[i]).wait()

    def tile(g, q, d):
        return attn.at[q, d] if g == 0 else wide_ref.at[g - 1, q, d]

    def z_copy(g, q, side):
        to = z + (1 if side else -1)
        src = own.at[g] if q is None else tile(g, q, dp)
        q = z if q is None else q
        return send(src, tile(g, q, dp), zs.at[g, q, side], zr.at[g, q], (dp, to))

    def z_pass(g, q):
        origin = z if q is None else q

        @pl.when((origin <= z) & (z < 3))
        def _():
            z_copy(g, q, 1).start()

        @pl.when((origin >= z) & (z > 0))
        def _():
            z_copy(g, q, 0).start()

    def z_done(g, q):
        @pl.when((q <= z) & (z < 3))
        def _():
            z_copy(g, q, 1).wait_send()

        @pl.when((q >= z) & (z > 0))
        def _():
            z_copy(g, q, 0).wait_send()

    def x_copy(g, q, src=None):
        src = tile(g, q, dp) if src is None else src
        return send(src, tile(g, q, dp), xs.at[g, q], xr.at[g, q], (nx, z))

    def y_copy(g, q, src=None):
        src = tile(g, q, dp) if src is None else src
        return send(src, tile(g, q, dp), ys.at[g, q], yr.at[g, q], (ny, z))

    def core_copy(g, q, pos, src=None):
        d = 2 * pos + c
        src = tile(g, q, d) if src is None else src
        return send(src, tile(g, q, d), cs.at[g, q, pos], cr.at[g, q, pos], (nc, z))

    def forward(g, q, along_y):
        src, to = (nx, ny) if along_y else (ny, nx)
        return send(tile(g, q, src), tile(g, q, src), ds.at[g, q], dr.at[g, q], (to, z))

    def own_start(g):
        z_pass(g, None)
        x_copy(g, z, own.at[g]).start()
        y_copy(g, z, own.at[g]).start()
        core_copy(g, z, yx, own.at[g]).start()
        pltpu.make_async_copy(own.at[g], tile(g, z, dp), local_sem.at[4 + g]).start()

    def z_step(g, k):
        q = nearest(z, k)
        send(tile(g, q, dp), tile(g, q, dp), zs.at[g, q, 0], zr.at[g, q], (dp, z)).wait_recv()
        z_pass(g, q)
        x_copy(g, q).start()
        y_copy(g, q).start()
        core_copy(g, q, yx).start()

    def plane_step(g, k):
        q = nearest(z, k)
        x_copy(g, q).wait_recv()

        @pl.when(lax.rem(q, 2) == 0)
        def _():
            forward(g, q, True).start()

        core_copy(g, q, yx_x).start()
        y_copy(g, q).wait_recv()

        @pl.when(lax.rem(q, 2) == 1)
        def _():
            forward(g, q, False).start()

        core_copy(g, q, yx_y).start()

    def far_step(g, k):
        q = nearest(z, k)
        d = 2 * yx_d + c
        send(tile(g, q, d), tile(g, q, d), ds.at[g, q], dr.at[g, q], (nx, z)).wait_recv()
        core_copy(g, q, yx_d).start()

    def core_ready(g, q):
        for pos in range(4):
            d = 2 * pos + 1 - c
            send(
                tile(g, q, d), tile(g, q, d), cs.at[g, q, pos], cr.at[g, q, pos], (nc, z)
            ).wait_recv()

    def weights_sent(g):
        def step(q):
            z_done(g, q)
            x_copy(g, q).wait_send()
            y_copy(g, q).wait_send()

            @pl.when(lax.rem(q, 2) == 0)
            def _():
                forward(g, q, True).wait_send()

            @pl.when(lax.rem(q, 2) == 1)
            def _():
                forward(g, q, False).wait_send()

            for pos in range(4):
                core_copy(g, q, pos).wait_send()

        loop(4, step)

    def own_ready(g):
        pltpu.make_async_copy(own.at[g], tile(g, z, dp), local_sem.at[4 + g]).wait()

    def hold(g, q, slot):
        return pltpu.make_async_copy(wide_ref.at[g - 1, q], held.at[slot], held_sem.at[slot])

    def out_core(g, q):
        return send(staged.at[q], from_core.at[g, q], ecs.at[g, q], ecr.at[g, q], (nc, z))

    def out_corner(g, q):
        to = nx + (ny - nx) * lax.rem(q, 2)
        return send(sums.at[g, q, yx_d], corner.at[g, q], eks.at[g, q], ekr.at[g, q], (to, z))

    def out_plane(g, q, side):
        to = nx + (ny - nx) * side
        pos = yx_x + (yx_y - yx_x) * side
        return send(
            sums.at[g, q, pos], from_plane.at[g, q, side], eps.at[g, q, side], epr.at[g, q, side], (to, z)
        )

    def out_z(g, q):
        return send(sums.at[g, q, yx], from_z.at[g, z], ezs.at[g, q], ezr.at[g, z], (dp, q))

    def core_add(g, q):
        out_core(g, q).wait_recv()

        def step(pos):
            sums[g, q, pos] = (
                sums[g, q, pos].astype(F32) + from_core[g, q, pos].astype(F32)
            ).astype(BF)

        loop(4, step)
        out_corner(g, q).start()

        @pl.when(q >= 2)
        def _():
            out_plane(g, q - 2, lax.rem(q, 2)).start()

    def corner_add(g, q):
        @pl.when(q < 2)
        def _():
            out_plane(g, q + 2, lax.rem(q, 2)).start()

        side = 1 - lax.rem(q, 2)
        pos = yx_x + (yx_y - yx_x) * side
        out_corner(g, q).wait_recv()
        sums[g, q, pos] = (sums[g, q, pos].astype(F32) + corner[g, q].astype(F32)).astype(BF)
        out_plane(g, q, side).start()

    def plane_add(g, q):
        out_plane(g, q, 0).wait_recv()
        out_plane(g, q, 1).wait_recv()
        sums[g, q, yx] = (
            sums[g, q, yx].astype(F32)
            + from_plane[g, q, 0].astype(F32)
            + from_plane[g, q, 1].astype(F32)
        ).astype(BF)

        @pl.when(z != q)
        def _():
            out_z(g, q).start()

    def last_add(g):
        total = sums[g, z, yx].astype(F32)
        for j in range(1, 4):
            q = lax.rem(z + j, 4)
            send(sums.at[g, q, yx], from_z.at[g, q], ezs.at[g, q], ezr.at[g, q], (dp, q)).wait_recv()
            total = total + from_z[g, q].astype(F32)
        total_ref[g] = total

    def grads_sent(g):
        def step(q):
            out_corner(g, q).wait_send()
            out_plane(g, q, 0).wait_send()
            out_plane(g, q, 1).wait_send()

            @pl.when(z != q)
            def _():
                out_z(g, q).wait_send()

        loop(4, step)

    def emit(g, q, left, right, left_2=None, right_2=None):
        if g < 2:
            out_core(g + 1, q).wait_send()
        for other in (True, False):
            half = 1 - c if other else c
            dst = staged.at[q] if other else sums.at[g, q]
            v = natural(left[:, half].reshape(384, LEN), right)
            if right_2 is None:
                dst[...] = v.astype(BF).reshape(4, 96, D)
            else:
                v2 = natural(left_2[:, half].reshape(384, LEN), right_2)
                dst[:, :, 0:512] = v[:, 0:512].astype(BF).reshape(4, 96, 512)
                dst[:, :, 512:640] = (v[:, 512:640] + v2[:, 0:128]).astype(BF).reshape(4, 96, 128)
                dst[:, :, 640:768] = v2[:, 128:256].astype(BF).reshape(4, 96, 128)
            if other:
                out_core(g, q).start()

    def put_t(dst, i, v):
        dst[:, :, :, block(i)] = v.T.reshape(4, 2, 96, BLOCK)

    def add(i, value):
        @pl.when(i == 0)
        def _():
            acc[...] = value

        @pl.when(i > 0)
        def _():
            acc[...] += value

    own_start(0)
    for i in range(1, 8):
        to = lax.rem(dp + i, 8)
        send(gain_own, gain_all.at[dp], gs.at[to], gr.at[dp], (to, z)).start()
    gain_all[dp] = gain_own[...]
    own_start(1)
    loop(3, lambda k: z_step(0, k + 1))
    loop(3, lambda k: z_step(1, k + 1))
    own_start(2)
    loop(4, lambda k: plane_step(0, k))
    rows_start(0, x_in, x_ref)
    seg_row = seg_ref[pl.ds(z, 1)].astype(F32)
    seg_col = jnp.broadcast_to(seg_row, (8, LEN)).T[:, 0:1]
    bias[...] = jnp.where(seg_col == seg_row, 0.0, -1e30)
    gain_sum[...] = jnp.zeros_like(gain_sum)
    gain_parts[...] = jnp.zeros_like(gain_parts)
    for i in range(1, 8):
        other = lax.rem(dp + i, 8)
        send(gain_own, gain_all.at[other], gs.at[other], gr.at[other], (other, z)).wait_recv()
    gain_a = gain_row(gain_all, 0)
    gain_f = gain_row(gain_all, 1)
    loop(3, lambda k: z_step(2, k + 1))
    rows_start(1, ct_in, ct_ref)
    loop(4, lambda k: plane_step(1, k))
    loop(4, lambda k: far_step(0, k))
    rows_wait(0, x_in, x_ref)

    def norm_a(i):
        xhat, _ = norm(x_ref[i].astype(F32))
        normed = (xhat * gain_a).astype(BF)
        nrm[block(i)] = normed
        put_t(na_t, i, normed)

    loop(4, norm_a)
    own_ready(0)

    def attend(i):
        q = nearest(z, i)
        core_ready(0, q)
        w = attn[q].reshape(D, D)
        p = natural(nrm[...], w[:, 0:640])
        q8 = p[:, 0:256].astype(BF) * jnp.asarray(0.125, BF)
        v = p[:, 128:384].astype(BF)
        k = p[:, 384:640].astype(BF)
        qb[q] = q8
        vb[q] = v
        kb[q] = k
        for h in range(3):
            for r in range(2):
                rs = slice(256 * r, 256 * (r + 1))
                s = against(between(q8[rs], 64 * h, 64), k) + bias[rs]
                m = jnp.max(s, axis=1, keepdims=True)
                e = jnp.exp(s - m)
                total = jnp.sum(e, axis=1, keepdims=True)
                probs = (e * (1.0 / total)).astype(BF)
                part = between(natural(probs, v), 64 + 64 * h, 64).astype(BF)
                if h == 0:
                    cb[q, rs] = part
                else:
                    cb[q, rs] += part
                lane = lax.broadcasted_iota(jnp.int32, (256, 128), 1)
                lse_ref[rs] = jnp.where(lane == 3 * q + h, m + jnp.log(total), lse_ref[rs])
            if h == 0:
                far_step(1, i)
            if h == 2:
                plane_step(2, i)

    loop(4, attend)

    def attend_out(i):
        add(i, against(cb[i], attn[i].reshape(D, D)[:, 512:768]))

    loop(4, attend_out)
    own_ready(1)

    def norm_f(i):
        m = x_ref[i].astype(F32) + acc[block(i)]
        mid[block(i)] = m
        xhat, _ = norm(m)
        normed = (xhat * gain_f).astype(BF)
        nrm[block(i)] = normed
        put_t(nf_t, i, normed)

    loop(4, norm_f)
    q = nearest(z, 0)
    core_ready(1, q)
    hold(1, q, 0).start()

    def up(i):
        q = nearest(z, i)
        slot = lax.rem(i, 2)

        @pl.when(i < 3)
        def _():
            later = nearest(z, i + 1)
            core_ready(1, later)
            hold(1, later, 1 - slot).start()

        hold(1, q, slot).wait()
        w = held[slot].reshape(D, D)
        for r in range(2):
            rs = slice(256 * r, 256 * (r + 1))
            h = natural(nrm[rs], w)
            cdf = 0.5 + 0.5 * lax.erf(h * 0.7071067811865476)
            act[q, rs] = (h * cdf).astype(BF)
            gp[q, rs] = (cdf + h * (jnp.exp(-0.5 * h * h) * 0.3989422804014327)).astype(BF)
        far_step(2, i)

    loop(4, up)
    rows_wait(1, ct_in, ct_ref)

    def turn_ct(i):
        put_t(ct_t, i, ct_ref[i])

    loop(4, turn_ct)
    own_ready(2)

    def grad_down(i):
        emit(2, i, ct_t, act[i])

        @pl.when(i > 0)
        def _():
            core_add(2, i - 1)

    loop(4, grad_down)
    core_add(2, 3)
    q = nearest(z, 0)
    core_ready(2, q)
    hold(2, q, 0).start()

    def down(i):
        q = nearest(z, i)
        slot = lax.rem(i, 2)

        @pl.when(i < 3)
        def _():
            later = nearest(z, i + 1)
            core_ready(2, later)
            hold(2, later, 1 - slot).start()

        hold(2, q, slot).wait()
        w = held[slot].reshape(D, D)
        gp[q] = (natural(ct_ref[...].reshape(LEN, D), w) * gp[q].astype(F32)).astype(BF)
        add(i, against(act[q], w))
        corner_add(2, i)

    loop(4, down)
    hold(1, 0, 0).start()
    out_ref[...] = (mid[...] + acc[...]).astype(BF).reshape(4, BLOCK, D)
    rows_start(2, out_ref, outs_ref)

    def up_back(i):
        slot = lax.rem(i, 2)

        @pl.when(i < 3)
        def _():
            hold(1, i + 1, 1 - slot).start()

        hold(1, i, slot).wait()
        add(i, against(gp[i], held[slot].reshape(D, D)))
        emit(1, i, nf_t, gp[i])

        @pl.when(i > 0)
        def _():
            core_add(1, i - 1)

    loop(4, up_back)
    core_add(1, 3)

    def norm_f_back(i):
        xhat, scale = norm(mid[block(i)])
        back, grad_gain = norm_back(acc[block(i)], xhat, scale, gain_f)
        gain_sum[1:2] += grad_gain[None]
        grad_middle = ct_ref[i].astype(F32) + back
        mid[block(i)] = grad_middle
        attended = grad_middle.astype(BF)
        nrm[block(i)] = attended
        put_t(ga_t, i, attended)

    loop(4, norm_f_back)

    def attend_back(i):
        w = attn[i].reshape(D, D)
        dctx = between(natural(nrm[...], w[:, 512:768]), 64, 192).astype(BF)
        q8, v, k, cx = qb[i], vb[i], kb[i], cb[i]
        dq = jnp.zeros((LEN, 256), F32)
        dk = jnp.zeros((LEN, 256), F32)
        dv = jnp.zeros((LEN, 256), F32)
        for h in range(3):
            lane = lax.broadcasted_iota(jnp.int32, (LEN, 128), 1)
            lse = jnp.sum(jnp.where(lane == 3 * i + h, lse_ref[...], 0.0), axis=1, keepdims=True)
            p = jnp.exp(against(between(q8, 64 * h, 64), k) + bias[...] - lse)
            dm = between(dctx, 64 + 64 * h, 64)
            delta = jnp.sum(dm.astype(F32) * cx.astype(F32), axis=1, keepdims=True)
            ds_ = (p * (against(dm, v) - delta)).astype(BF)
            dq += between(natural(ds_, k), 64 * h, 64)
            dk += between(inner(ds_, q8), 64 * h, 64)
            dv += between(inner(p.astype(BF), dctx), 64 + 64 * h, 64)
            if h == 0:
                @pl.when(i < 2)
                def _():
                    plane_add(2, 2 * i)
                    plane_add(2, 2 * i + 1)
            if h == 1:
                @pl.when(i < 2)
                def _():
                    corner_add(1, 2 * i)
                    corner_add(1, 2 * i + 1)

                @pl.when(i >= 2)
                def _():
                    plane_add(1, 2 * i - 4)
                    plane_add(1, 2 * i - 3)
        dq = dq * 0.125
        d = jnp.concatenate(
            [dq[:, 0:128], dq[:, 128:256] + dv[:, 0:128], dv[:, 128:256], dk], axis=1
        ).astype(BF)
        add(i, against(d, w[:, 0:640]))
        emit(0, i, na_t, d, ga_t, cx)

        @pl.when(i > 0)
        def _():
            core_add(0, i - 1)

    loop(4, attend_back)
    core_add(0, 3)

    def norm_a_back(i):
        xhat, scale = norm(x_ref[i].astype(F32))
        back, grad_gain = norm_back(acc[block(i)], xhat, scale, gain_a)
        gain_sum[0:1] += grad_gain[None]
        dx_ref[i] = (mid[block(i)] + back).astype(BF)

    loop(4, norm_a_back)
    rows_start(3, dx_ref, dxs_ref)

    def small_copy(i):
        return send(gain_parts, small.at[i], egs.at[i], egr.at[i], ((nc, nx, ny)[i], z))

    def small_add(i):
        small_copy(i).wait()
        gain_parts[...] += small[i]

    for i in range(2):
        for p in range(8):
            gain_parts[8 * i + p : 8 * i + p + 1, 0:96] = gain_sum[i : i + 1, 96 * p : 96 * (p + 1)]
    small_copy(0).start()
    corner_add(0, 0)
    small_add(0)
    small_copy(1).start()
    corner_add(0, 1)
    corner_add(0, 2)
    small_add(1)
    small_copy(2).start()
    corner_add(0, 3)
    last_add(2)
    last_add(1)
    small_add(2)
    for j in range(1, 4):
        q = lax.rem(z + j, 4)
        send(gain_parts, small_z.at[z], egzs.at[q], egzr.at[z], (dp, q)).start()
    loop(4, lambda k: plane_add(0, k))
    total = gain_parts[...]
    for j in range(1, 4):
        q = lax.rem(z + j, 4)
        cp = send(gain_parts, small_z.at[q], egzs.at[q], egzr.at[q], (dp, q))
        cp.wait()
        total = total + small_z[q]
    gain_parts[...] = total
    gain_ref[0:1] = gain_parts[pl.ds(dp, 1)]
    gain_ref[1:2] = gain_parts[pl.ds(dp + 8, 1)]
    last_add(0)

    for i in range(1, 8):
        other = lax.rem(dp + i, 8)
        send(gain_own, gain_all.at[other], gs.at[other], gr.at[other], (other, z)).wait_send()
    for g in range(3):
        weights_sent(g)
        grads_sent(g)
    loop(4, lambda q: out_core(0, q).wait_send())
    rows_wait(2, out_ref, outs_ref)
    rows_wait(3, dx_ref, dxs_ref)


def layer(x, ct, segment_ids, w_query, w_key, w_value, w_output, w_up, w_down, gain_attn, gain_ffn):
    sem = pltpu.SemaphoreType.DMA
    vm = pltpu.VMEM
    anywhere = pl.BlockSpec(memory_space=pl.ANY)
    vmem = pl.BlockSpec(memory_space=pltpu.VMEM)
    return pl.pallas_call(
        layer_kernel,
        out_shape=(
            jax.ShapeDtypeStruct((3, 96, D), F32),
            jax.ShapeDtypeStruct((8, 128), F32),
            jax.ShapeDtypeStruct(x.shape, BF),
            jax.ShapeDtypeStruct(x.shape, BF),
            jax.ShapeDtypeStruct((2, 4, 8, 96, D), BF),
        ),
        in_specs=[anywhere] * 2 + [vmem] * 9,
        out_specs=(vmem, vmem, anywhere, anywhere, anywhere),
        scratch_shapes=[
            vm((3, 96, D), BF), vm((16, 128), BF), vm((8, 16, 128), BF),
            vm((4, 8, 96, D), BF), vm((2, 8, 96, D), BF),
            vm((4, BLOCK, D), BF), vm((4, BLOCK, D), BF), vm((4, BLOCK, D), BF), vm((4, BLOCK, D), BF),
            vm((LEN, D), BF),
            vm((4, 2, 96, LEN), BF), vm((4, 2, 96, LEN), BF), vm((4, 2, 96, LEN), BF), vm((4, 2, 96, LEN), BF),
            vm((4, LEN, 256), BF), vm((4, LEN, 256), BF), vm((4, LEN, 256), BF), vm((4, LEN, 256), BF),
            vm((LEN, 128), F32), vm((LEN, LEN), F32), vm((LEN, D), F32), vm((LEN, D), F32),
            vm((4, LEN, D), BF), vm((4, LEN, D), BF),
            vm((4, 4, 96, D), BF), vm((3, 4, 4, 96, D), BF), vm((3, 4, 4, 96, D), BF),
            vm((3, 4, 96, D), BF), vm((3, 4, 2, 96, D), BF), vm((3, 4, 96, D), BF),
            vm((3, 16, 128), F32), vm((4, 16, 128), F32), vm((8, D), F32), vm((16, 128), F32),
            sem((7,)), sem((2,)),
            sem((3, 4, 2)), sem((3, 4)),
            sem((3, 4)), sem((3, 4)),
            sem((3, 4)), sem((3, 4)),
            sem((3, 4)), sem((3, 4)),
            sem((3, 4, 4)), sem((3, 4, 4)),
            sem((8,)), sem((8,)),
            sem((4, 4)), sem((4, 4)),
            sem((3, 4)), sem((3, 4)),
            sem((3, 4)), sem((3, 4)),
            sem((3, 4, 2)), sem((3, 4, 2)),
            sem((3, 4)), sem((3, 4)),
            sem((3,)), sem((3,)),
            sem((4,)), sem((4,)),
        ],
        compiler_params=pltpu.CompilerParams(
            collective_id=0, has_side_effects=True, vmem_limit_bytes=VMEM_LIMIT
        ),
        name="layer_with_copies",
    )(x, ct, segment_ids, w_query, w_key, w_value, w_output, w_up, w_down, gain_attn, gain_ffn)


VMEM_LIMIT = 62 * 2**20


def part_kernel(
    total_ref, gain_ref, out_ref, dx_ref,
    outs_ref, dxs_ref, q_ref, k_ref, v_ref, o_ref, up_ref, down_ref, ga_ref, gf_ref,
):
    outs_ref[...] = out_ref[...]
    dxs_ref[...] = dx_ref[...]
    attn = total_ref[0]
    q_ref[...] = attn[:, 0:192]
    v_ref[...] = attn[:, 192:384]
    k_ref[...] = attn[:, 384:576]
    o_ref[...] = attn[:, 576:768].T
    up_ref[...] = total_ref[1]
    down_ref[...] = total_ref[2]
    ga_ref[...] = gain_ref[0:1, 0:96]
    gf_ref[...] = gain_ref[1:2, 0:96]


def part(total, gain, out, dx):
    vmem = pl.BlockSpec(memory_space=pltpu.VMEM)
    shapes = [(96, 192)] * 3 + [(192, 96), (96, D), (96, D), (1, 96), (1, 96)]
    return pl.pallas_call(
        part_kernel,
        out_shape=[jax.ShapeDtypeStruct(out.shape, BF)] * 2 + [jax.ShapeDtypeStruct(n, F32) for n in shapes],
        in_specs=[vmem] * 4,
        out_specs=[vmem] * 10,
        name="part_outputs",
    )(total, gain, out, dx)


def shards(
    inputs, segment_ids, w_query, w_key, w_value, w_output, w_up, w_down, gain_attn, gain_ffn, cotangent,
    *, parts, quarters,
):
    depth, width = w_query.shape
    if parts == 8 and quarters == 4:
        total, gg, out, dx, _ = layer(
            inputs, cotangent, segment_ids, w_query, w_key, w_value, w_output, w_up, w_down.T,
            gain_attn.reshape(1, depth), gain_ffn.reshape(1, depth),
        )
        *outs, grad_down, grad_gain_attn, grad_gain_ffn = part(total, gg, out, dx)
        return (*outs, grad_down.T, grad_gain_attn.reshape(depth), grad_gain_ffn.reshape(depth))
    else:
        z = lax.axis_index("mp")
        segment = lax.dynamic_index_in_dim(segment_ids, z, 0, keepdims=False)
        own = jnp.stack(
            [jnp.concatenate([w_query, w_value, w_key, w_output.T], axis=1), w_up, w_down.T]
        )
        weights = lax.all_gather(own, ("dp", "mp"), axis=0).reshape(parts, quarters, 3, depth, D)
        weights = weights.transpose(2, 1, 0, 3, 4).reshape(3, quarters, D, D)
        gains = jnp.stack(
            [lax.all_gather(g, "dp", axis=0, tiled=True) for g in (gain_attn, gain_ffn)]
        ).astype(F32)
        x, ct = (
            lax.all_to_all(a, "mp", split_axis=0, concat_axis=0, tiled=True) for a in (inputs, cotangent)
        )
        out, dx, grads, gg = row_layer(
            x.reshape(-1, D), ct.reshape(-1, D), segment, weights, gains[0], gains[1]
        )
        grads = grads.reshape(3, quarters, parts, depth, D).transpose(2, 1, 0, 3, 4)
        grads = grads.reshape(parts * quarters, 3, depth, D)
        total = lax.psum_scatter(grads, ("dp", "mp"), scatter_dimension=0).astype(F32)
        gg = lax.psum(lax.psum_scatter(gg, "dp", scatter_dimension=1, tiled=True), "mp")
        out, dx = (
            lax.all_to_all(a.reshape(inputs.shape), "mp", split_axis=0, concat_axis=0, tiled=True)
            for a in (out, dx)
        )
    return (
        out,
        dx,
        total[0, :, :width],
        total[0, :, 2 * width : 3 * width],
        total[0, :, width : 2 * width],
        total[0, :, 3 * width :].T,
        total[1],
        total[2].T,
        gg[0],
        gg[1],
    )


def solution(mesh):
    by_row = P("dp", "mp", None)
    grids = (P("dp", "mp"), P("dp", "mp"), P("dp", "mp"), P("mp", "dp"), P("dp", "mp"), P("mp", "dp"))
    gains = (P("dp"), P("dp"))
    return jax.shard_map(
        functools.partial(shards, parts=mesh.shape["dp"], quarters=mesh.shape["mp"]),
        mesh=mesh,
        in_specs=(by_row, P("dp", None)) + grids + gains + (by_row,),
        out_specs=(by_row, by_row) + grids + gains,
        check_vma=False,
    )
```

```python
import functools

import jax
import jax.numpy as jnp
from jax import lax
from jax.experimental import pallas as pl
from jax.experimental.pallas import tpu as pltpu
from jax.sharding import PartitionSpec as P

D = 768
HEADS = 12
HEAD = 64
EPS = 1e-05
MESH = pl.DeviceIdType.MESH
BF = jnp.bfloat16
F32 = jnp.float32


def dot(left, right, dims):
    return lax.dot_general(left, right, (dims, ((), ())), preferred_element_type=F32)


def natural(left, right):
    return dot(left, right, ((1,), (0,)))


def against(left, right):
    return dot(left, right, ((1,), (1,)))


def inner(left, right):
    return dot(left, right, ((0,), (0,)))


def norm(values):
    shifted = values - jnp.mean(values, axis=1, keepdims=True)
    scale = lax.rsqrt(jnp.mean(shifted * shifted, axis=1, keepdims=True) + EPS)
    return shifted * scale, scale


def norm_back(grad, xhat, scale, gain):
    e = grad * gain
    back = scale * (
        e - jnp.mean(e, axis=1, keepdims=True) - xhat * jnp.mean(e * xhat, axis=1, keepdims=True)
    )
    return back, jnp.sum(grad * xhat, axis=0)


def columns(w, first, count):
    part = w[:, :, first : first + count]
    return jnp.swapaxes(part, 0, 1).reshape(D, -1)


def row_layer(x, cotangent, segment, weights, gain_attn, gain_ffn):
    length = x.shape[0]
    quarters = weights.shape[1]
    width = D // quarters
    attn, up, down = weights[0], weights[1], weights[2]
    w_query, w_value, w_key, w_out = (columns(attn, i * width, width) for i in range(4))
    w_up, w_down = columns(up, 0, D), columns(down, 0, D)
    x = x.astype(F32)
    xhat_a, scale_a = norm(x)
    normed_a = (xhat_a * gain_attn).astype(BF)
    query, keys, values = (
        natural(normed_a, w).astype(BF).reshape(length, HEADS, HEAD) for w in (w_query, w_key, w_value)
    )
    same = segment[:, None] == segment[None, :]
    scores = jnp.einsum("qhd,khd->hqk", query, keys, preferred_element_type=F32) * HEAD**-0.5
    scores = jnp.where(same[None], scores, -1e30)
    exponent = jnp.exp(scores - jnp.max(scores, axis=2, keepdims=True))
    probs = exponent / jnp.sum(exponent, axis=2, keepdims=True)
    context = jnp.einsum("hqk,khd->qhd", probs.astype(BF), values, preferred_element_type=F32)
    context = context.reshape(length, D).astype(BF)
    middle = x + against(context, w_out)
    xhat_f, scale_f = norm(middle)
    normed_f = (xhat_f * gain_ffn).astype(BF)
    hidden = natural(normed_f, w_up)
    activated, gelu_back = jax.vjp(lambda v: jax.nn.gelu(v, approximate=False), hidden)
    activated = activated.astype(BF)
    output = (middle + against(activated, w_down)).astype(BF)

    grad_down = inner(cotangent, activated)
    grad_hidden = gelu_back(natural(cotangent, w_down))[0].astype(BF)
    grad_up = inner(normed_f, grad_hidden)
    back, grad_gain_ffn = norm_back(against(grad_hidden, w_up), xhat_f, scale_f, gain_ffn)
    grad_middle = cotangent.astype(F32) + back
    grad_attended = grad_middle.astype(BF)
    grad_out = inner(grad_attended, context)
    grad_context = natural(grad_attended, w_out).astype(BF).reshape(length, HEADS, HEAD)
    grad_probs = jnp.einsum("qhd,khd->hqk", grad_context, values, preferred_element_type=F32)
    grad_scores = (
        probs * (grad_probs - jnp.sum(probs * grad_probs, axis=2, keepdims=True))
    ).astype(BF)
    query_grad = jnp.einsum("hqk,khd->qhd", grad_scores, keys, preferred_element_type=F32) * HEAD**-0.5
    key_grad = jnp.einsum("hqk,qhd->khd", grad_scores, query, preferred_element_type=F32) * HEAD**-0.5
    value_grad = jnp.einsum(
        "hqk,qhd->khd", probs.astype(BF), grad_context, preferred_element_type=F32
    )
    query_grad, key_grad, value_grad = (
        g.reshape(length, D).astype(BF) for g in (query_grad, key_grad, value_grad)
    )
    grad_normed_a = (
        against(query_grad, w_query) + against(key_grad, w_key) + against(value_grad, w_value)
    )
    back, grad_gain_attn = norm_back(grad_normed_a, xhat_a, scale_a, gain_attn)
    input_grad = (grad_middle + back).astype(BF)

    def quarter(g, count):
        return g.astype(BF).reshape(D, quarters, count).swapaxes(0, 1)

    grads_attn = jnp.concatenate(
        [
            quarter(g, width)
            for g in (
                inner(normed_a, query_grad),
                inner(normed_a, value_grad),
                inner(normed_a, key_grad),
                grad_out,
            )
        ],
        axis=2,
    )
    grads = jnp.stack([grads_attn, quarter(grad_up, D), quarter(grad_down, D)])
    return output, input_grad, grads, jnp.stack([grad_gain_attn, grad_gain_ffn])


def between(value, first, count):
    lane = lax.broadcasted_iota(jnp.int32, value.shape, 1)
    return jnp.where((lane >= first) & (lane < first + count), value, jnp.zeros_like(value))


def place():
    dp, z = lax.axis_index("dp"), lax.axis_index("mp")
    c, x, y = lax.rem(dp, 2), lax.rem(dp // 2, 2), dp // 4
    return dp, z, c, dp + 2 - 4 * x, dp + 4 - 8 * y, dp + 1 - 2 * c


def send(src, dst, ssem, rsem, device):
    return pltpu.make_async_remote_copy(
        src_ref=src, dst_ref=dst, send_sem=ssem, recv_sem=rsem, device_id=device, device_id_type=MESH
    )


def nearest(z, k):
    inner_place = lax.rem((z + 1) // 2, 2)
    first_two = 1 - k // 2
    base = k + inner_place * first_two * (1 - 2 * k)
    return base + (z // 2) * (3 - 2 * base)


def gain_row(parts_ref, index):
    r = lax.broadcasted_iota(jnp.int32, (128, D), 0)
    col = lax.broadcasted_iota(jnp.int32, (128, D), 1)
    spread = jnp.where(lax.rem(col, 96) == r, 1.0, 0.0).astype(BF)
    total = jnp.zeros((1, D), F32)
    col = lax.broadcasted_iota(jnp.int32, (16, D), 1)
    row = lax.broadcasted_iota(jnp.int32, (16, D), 0)
    for p in range(8):
        full = natural(parts_ref[p], spread)
        keep = (row == index) & (col >= 96 * p) & (col < 96 * (p + 1))
        total = total + jnp.sum(jnp.where(keep, full, 0.0), axis=0, keepdims=True)
    return total


BLOCK = 128
LEN = 512

FIRST = ('b1','a1','z01','z02','z03','x')
SECOND = ('p00','p10','p01','iz11','f00','p02','iz12','p03','f01','iz13','a2','oz11','f02','oz12','oz13','b2','f03')
THIRD = ()
ATTEND = {0: ("p11","z21","iz22"), 1: ("iz23",), 2: ("p12",), 3: ("f10",), 4: ("c","p20"), 5: ("p13",), 6: ("f11", "oz22"), 7: ("p21",), 8: ("oz23",), 9: ("f12",), 10: ("p22","f13")}
AFTER_NORM = ("p23","f20")
UP = {0: ("f21",), 1: ("f22",), 3: ("f23",)}
TURN = {}
GRAD_DOWN = {}
AFTER_GRAD_DOWN = ()
DOWN = {0: ("e20",), 1: ("e21",), 2: ("e22",), 3: ("e23",)}
UP_BACK = {}
AFTER_NORM_BACK = ()
ATTEND_BACK = {
    0: ("l20", "l21", "l22", "l23"), 1: ("e10", "e11"), 2: ("e12", "e13"), 5: ("l10", "l11"),
    6: ("r2",), 7: ("l12",), 8: ("l13",), 10: ("e00", "r1"), 11: ("e01", "t2"),
}
AFTER_ROWS = ("e02", "e03", "t1")
LAST = ("l00", "l01", "l02", "l03", "r0")


def block(i):
    return pl.ds(pl.multiple_of(i * BLOCK, BLOCK), BLOCK)


def loop(count, step):
    def body(i, _):
        step(i)
        return 0

    lax.fori_loop(0, count, body, 0)


def layer_kernel(
    x_in, ct_in, seg_ref, wq_ref, wk_ref, wv_ref, wo_ref, wup_ref, wdown_ref, ga_ref, gf_ref,
    outs_ref, dxs_ref, q_ref, k_ref, v_ref, o_ref, up_ref, down_ref, gain_a_ref, gain_f_ref,
    gain_own, gain_all, weights, x_ref, ct_ref, out_ref,
    nrm, na_t, nf_t, ct_t, qb, kb, vb, cb, lse_ref, bias, mid, acc, act, gp,
    staged, sums, from_core, corner, from_plane, from_z, small, small_z, gain_sum, gain_parts, gain_own_sum,
    local_sem, zs, zr, xs, xr, ys, yr, ds, dr, cs, cr, gs, gr, as_, ar,
    ecs, ecr, eks, ekr, eps, epr, ezs, ezr, egs, egr, egzs, egzr,
):
    dp, z, c, nx, ny, nc = place()
    yx, yx_x, yx_y, yx_d = dp // 2, nx // 2, ny // 2, 3 - dp // 2

    barrier = pltpu.get_barrier_semaphore()
    for i in range(1, 8):
        pl.semaphore_signal(barrier, inc=1, device_id=(lax.rem(dp + i, 8), z), device_id_type=MESH)
    for i in range(1, 4):
        pl.semaphore_signal(barrier, inc=1, device_id=(dp, lax.rem(z + i, 4)), device_id_type=MESH)

    weights[0, z, dp] = jnp.concatenate(
        [wq_ref[...], wv_ref[...], wk_ref[...], wo_ref[...].T], axis=1
    )
    weights[1, z, dp] = wup_ref[...]
    weights[2, z, dp] = wdown_ref[...]
    gain_own[...] = jnp.zeros_like(gain_own)
    gain_own[0:1, 0:96] = ga_ref[...]
    gain_own[1:2, 0:96] = gf_ref[...]
    pl.semaphore_wait(barrier, 10)

    def rows_start(i, src, dst):
        for j in range(1, 4):
            q = lax.rem(z + j, 4)
            send(src.at[q], dst.at[z], as_.at[i, q], ar.at[i, z], (dp, q)).start()
        pltpu.make_async_copy(src.at[z], dst.at[z], local_sem.at[i]).start()

    def rows_wait(i, src, dst):
        for j in range(1, 4):
            q = lax.rem(z + j, 4)
            cp = send(src.at[q], dst.at[q], as_.at[i, q], ar.at[i, q], (dp, q))
            cp.wait_send()
            cp.wait_recv()
        pltpu.make_async_copy(src.at[z], dst.at[z], local_sem.at[i]).wait()

    def tile(g, q, d):
        return weights.at[g, q, d]

    mate = z + 1 - 2 * lax.rem(z, 2)
    far_inner = 2 - z // 2
    outer = (z == 0) | (z == 3)
    other_side = 2 * (1 - z // 2)

    def z_copy(g, q, side, to):
        return send(tile(g, q, dp), tile(g, q, dp), zs.at[g, q, side], zr.at[g, q], (dp, to))

    def passes_on(q):
        return jnp.logical_not(outer) & (q // 2 != z // 2)

    def own_z(g):
        z_copy(g, z, 0, mate).start()
        z_copy(g, z, 1, far_inner).start()

    def z_done(g, q):
        @pl.when(q == z)
        def _():
            z_copy(g, q, 0, mate).wait_send()
            z_copy(g, q, 1, far_inner).wait_send()

        @pl.when(passes_on(q))
        def _():
            z_copy(g, q, 0, mate).wait_send()

    def x_copy(g, q):
        return send(tile(g, q, dp), tile(g, q, dp), xs.at[g, q], xr.at[g, q], (nx, z))

    def y_copy(g, q):
        return send(tile(g, q, dp), tile(g, q, dp), ys.at[g, q], yr.at[g, q], (ny, z))

    def core_copy(g, q, pos):
        d = 2 * pos + c
        return send(tile(g, q, d), tile(g, q, d), cs.at[g, q, pos], cr.at[g, q, pos], (nc, z))

    def forward(g, q, along_y):
        src, to = (nx, ny) if along_y else (ny, nx)
        return send(tile(g, q, src), tile(g, q, src), ds.at[g, q], dr.at[g, q], (to, z))

    def own_plane(g):
        x_copy(g, z).start()
        y_copy(g, z).start()
        core_copy(g, z, yx).start()

    def z_step(g, k):
        q = nearest(z, k)
        z_copy(g, q, 0, mate).wait_recv()

        @pl.when(passes_on(q))
        def _():
            z_copy(g, q, 0, mate).start()

        x_copy(g, q).start()
        y_copy(g, q).start()
        core_copy(g, q, yx).start()

    def plane_step(g, k):
        q = nearest(z, k)
        x_copy(g, q).wait_recv()

        @pl.when(lax.rem(q, 2) == 0)
        def _():
            forward(g, q, True).start()

        core_copy(g, q, yx_x).start()
        y_copy(g, q).wait_recv()

        @pl.when(lax.rem(q, 2) == 1)
        def _():
            forward(g, q, False).start()

        core_copy(g, q, yx_y).start()

    def far_step(g, k):
        q = nearest(z, k)
        d = 2 * yx_d + c
        send(tile(g, q, d), tile(g, q, d), ds.at[g, q], dr.at[g, q], (nx, z)).wait_recv()
        core_copy(g, q, yx_d).start()

    def core_ready(g, q):
        for pos in range(4):
            d = 2 * pos + 1 - c
            send(
                tile(g, q, d), tile(g, q, d), cs.at[g, q, pos], cr.at[g, q, pos], (nc, z)
            ).wait_recv()

    def weights_sent(g):
        def step(q):
            z_done(g, q)
            x_copy(g, q).wait_send()
            y_copy(g, q).wait_send()

            @pl.when(lax.rem(q, 2) == 0)
            def _():
                forward(g, q, True).wait_send()

            @pl.when(lax.rem(q, 2) == 1)
            def _():
                forward(g, q, False).wait_send()

            for pos in range(4):
                core_copy(g, q, pos).wait_send()

        loop(4, step)

    def out_core(g, q):
        return send(staged.at[q], from_core.at[g % 2, q], ecs.at[g, q], ecr.at[g, q], (nc, z))

    def out_corner(g, q):
        to = nx + (ny - nx) * lax.rem(q, 2)
        return send(sums.at[g, q, yx_d], corner.at[g, q], eks.at[g, q], ekr.at[g, q], (to, z))

    def out_plane(g, q, side):
        to = nx + (ny - nx) * side
        pos = yx_x + (yx_y - yx_x) * side
        return send(
            sums.at[g, q, pos], from_plane.at[g, q, side], eps.at[g, q, side], epr.at[g, q, side], (to, z)
        )

    def out_z(g, q, slot, to):
        return send(sums.at[g, q, yx], from_z.at[g, slot], ezs.at[g, q], ezr.at[g, slot], (dp, to))

    def in_z(g, slot):
        return send(sums.at[g, 0, yx], from_z.at[g, slot], ezs.at[g, 0], ezr.at[g, slot], (dp, mate))

    def corner_add(g, q):
        side = 1 - lax.rem(q, 2)
        pos = yx_x + (yx_y - yx_x) * side
        out_corner(g, q).wait_recv()
        sums[g, q, pos] = (sums[g, q, pos].astype(F32) + corner[g, q].astype(F32)).astype(BF)
        out_plane(g, q, side).start()

    def plane_add(g, q):
        out_plane(g, q, 0).wait_recv()
        out_plane(g, q, 1).wait_recv()
        sums[g, q, yx] = (
            sums[g, q, yx].astype(F32)
            + from_plane[g, q, 0].astype(F32)
            + from_plane[g, q, 1].astype(F32)
        ).astype(BF)

        @pl.when(q == mate)
        def _():
            out_z(g, q, 0, mate).start()

        @pl.when(outer & (q // 2 != z // 2))
        def _():
            out_z(g, q, 2 + lax.rem(q, 2), mate).start()

    def relay(g):
        @pl.when(jnp.logical_not(outer))
        def _():
            for j in range(2):
                q = other_side + j
                in_z(g, 2 + j).wait_recv()
                sums[g, q, yx] = (
                    sums[g, q, yx].astype(F32) + from_z[g, 2 + j].astype(F32)
                ).astype(BF)
                out_z(g, q, 1, q).start()

    def last_add(g):
        in_z(g, 0).wait_recv()
        in_z(g, 1).wait_recv()
        total = sums[g, z, yx].astype(F32) + from_z[g, 0].astype(F32) + from_z[g, 1].astype(F32)
        if g == 0:
            q_ref[...] = total[:, 0:192]
            v_ref[...] = total[:, 192:384]
            k_ref[...] = total[:, 384:576]
            o_ref[...] = total[:, 576:768].T
        else:
            (up_ref if g == 1 else down_ref)[...] = total

    def grads_sent(g):
        def step(q):
            out_corner(g, q).wait_send()
            out_plane(g, q, 0).wait_send()
            out_plane(g, q, 1).wait_send()

            @pl.when(z != q)
            def _():
                out_z(g, q, 0, mate).wait_send()

        loop(4, step)

    def grad_rows(half, left, right, more):
        v = natural(left[:, half].reshape(384, LEN), right)
        if more is None:
            return ((0, v),)
        v2 = natural(more[0][:, half].reshape(384, LEN), more[1])
        return ((0, v[:, 0:512]), (512, v[:, 512:640] + v2[:, 0:128]), (640, v2[:, 128:256]))

    def emit_other(g, q, left, right, more=None):
        if g < 2:
            out_core(g + 1, q).wait_send()
        for first, v in grad_rows(1 - c, left, right, more):
            staged[q, :, :, first : first + v.shape[1]] = v.astype(BF).reshape(4, 96, v.shape[1])
        out_core(g, q).start()

    def emit_own(g, q, left, right, more=None):
        pieces = grad_rows(c, left, right, more)
        out_core(g, q).wait_recv()
        for first, v in pieces:
            lanes = slice(first, first + v.shape[1])
            theirs = from_core[g % 2, q, :, :, lanes].astype(F32)
            sums[g, q, :, :, lanes] = (v.reshape(4, 96, v.shape[1]) + theirs).astype(BF)
        out_corner(g, q).start()

        @pl.when(q >= 1)
        def _():
            out_plane(g, q - 1, lax.rem(q - 1, 2)).start()

        @pl.when(q == 3)
        def _():
            out_plane(g, q, lax.rem(q, 2)).start()

    def put_t(dst, i, v):
        dst[:, :, :, block(i)] = v.T.reshape(4, 2, 96, BLOCK)

    def add(i, value):
        @pl.when(i == 0)
        def _():
            acc[...] = value

        @pl.when(i > 0)
        def _():
            acc[...] += value

    steps = {
        "a": own_z, "b": own_plane, "z": z_step, "p": plane_step, "f": far_step,
        "x": lambda: rows_start(0, x_in, x_ref), "c": lambda: rows_start(1, ct_in, ct_ref),
        "e": corner_add, "l": plane_add, "r": relay, "t": last_add,
    }

    def take(names):
        for name in names:
            act_on = functools.partial(steps[name.lstrip("io")[0]], *map(int, name.lstrip("io")[1:]))
            if name[0] in "io":
                pl.when(outer if name[0] == "o" else jnp.logical_not(outer))(act_on)
            else:
                act_on()

    def serve(now, table):
        for due, names in table.items():
            pl.when(now == due)(functools.partial(take, names))

    own_z(0)
    own_plane(0)
    for i in range(1, 8):
        to = lax.rem(dp + i, 8)
        send(gain_own, gain_all.at[dp], gs.at[to], gr.at[dp], (to, z)).start()
    gain_all[dp] = gain_own[...]
    take(FIRST)
    seg_row = seg_ref[pl.ds(z, 1)].astype(F32)
    seg_col = jnp.broadcast_to(seg_row, (8, LEN)).T[:, 0:1]
    bias[...] = jnp.where(seg_col == seg_row, 0.0, -1e30)
    gain_sum[...] = jnp.zeros_like(gain_sum)
    gain_parts[...] = jnp.zeros_like(gain_parts)
    take(SECOND)
    for i in range(1, 8):
        other = lax.rem(dp + i, 8)
        send(gain_own, gain_all.at[other], gs.at[other], gr.at[other], (other, z)).wait_recv()
    gain_a = gain_row(gain_all, 0)
    gain_f = gain_row(gain_all, 1)
    take(THIRD)
    rows_wait(0, x_in, x_ref)

    def norm_a(i):
        xhat, _ = norm(x_ref[i].astype(F32))
        normed = (xhat * gain_a).astype(BF)
        nrm[block(i)] = normed
        put_t(na_t, i, normed)

    loop(4, norm_a)

    def attend(i):
        q = nearest(z, i)
        core_ready(0, q)
        w = weights[0, q].reshape(D, D)
        p = natural(nrm[...], w[:, 0:640])
        q8 = p[:, 0:256].astype(BF) * jnp.asarray(0.125, BF)
        v = p[:, 128:384].astype(BF)
        k = p[:, 384:640].astype(BF)
        qb[q] = q8
        vb[q] = v
        kb[q] = k
        for h in range(3):
            for r in range(2):
                rs = slice(256 * r, 256 * (r + 1))
                s = against(between(q8[rs], 64 * h, 64), k) + bias[rs]
                m = jnp.max(s, axis=1, keepdims=True)
                e = jnp.exp(s - m)
                total = jnp.sum(e, axis=1, keepdims=True)
                probs = (e * (1.0 / total)).astype(BF)
                part = between(natural(probs, v), 64 + 64 * h, 64).astype(BF)
                if h == 0:
                    cb[q, rs] = part
                else:
                    cb[q, rs] += part
                lane = lax.broadcasted_iota(jnp.int32, (256, 128), 1)
                lse_ref[rs] = jnp.where(lane == 3 * q + h, m + jnp.log(total), lse_ref[rs])
            serve(3 * i + h, ATTEND)

    loop(4, attend)

    def attend_out(i):
        add(i, against(cb[i], weights[0, i].reshape(D, D)[:, 512:768]))

    loop(4, attend_out)

    def norm_f(i):
        m = x_ref[i].astype(F32) + acc[block(i)]
        mid[block(i)] = m
        xhat, _ = norm(m)
        normed = (xhat * gain_f).astype(BF)
        nrm[block(i)] = normed
        put_t(nf_t, i, normed)

    loop(4, norm_f)
    take(AFTER_NORM)
    def up(i):
        q = nearest(z, i)
        core_ready(1, q)
        w = weights[1, q].reshape(D, D)
        for r in range(2):
            rs = slice(256 * r, 256 * (r + 1))
            h = natural(nrm[rs], w)
            cdf = 0.5 + 0.5 * lax.erf(h * 0.7071067811865476)
            act[q, rs] = (h * cdf).astype(BF)
            gp[q, rs] = (cdf + h * (jnp.exp(-0.5 * h * h) * 0.3989422804014327)).astype(BF)
        serve(i, UP)

    loop(4, up)
    rows_wait(1, ct_in, ct_ref)

    def turn_ct(i):
        put_t(ct_t, i, ct_ref[i])
        serve(i, TURN)

    loop(4, turn_ct)

    def grad_down(i):
        emit_other(2, i, ct_t, act[i])

        @pl.when(i > 0)
        def _():
            emit_own(2, i - 1, ct_t, act[i - 1])

        serve(i, GRAD_DOWN)

    loop(4, grad_down)
    emit_own(2, 3, ct_t, act[3])
    take(AFTER_GRAD_DOWN)

    def down(i):
        q = nearest(z, i)
        core_ready(2, q)
        w = weights[2, q].reshape(D, D)
        gp[q] = (natural(ct_ref[...].reshape(LEN, D), w) * gp[q].astype(F32)).astype(BF)
        add(i, against(act[q], w))
        serve(i, DOWN)

    loop(4, down)
    out_ref[...] = (mid[...] + acc[...]).astype(BF).reshape(4, BLOCK, D)
    rows_start(2, out_ref, outs_ref)

    def up_back(i):
        emit_other(1, i, nf_t, gp[i])
        add(i, against(gp[i], weights[1, i].reshape(D, D)))
        emit_own(1, i, nf_t, gp[i])

        serve(i, UP_BACK)

    loop(4, up_back)

    def norm_f_back(i):
        xhat, scale = norm(mid[block(i)])
        back, grad_gain = norm_back(acc[block(i)], xhat, scale, gain_f)
        gain_sum[1:2] += grad_gain[None]
        grad_middle = ct_ref[i].astype(F32) + back
        mid[block(i)] = grad_middle
        attended = grad_middle.astype(BF)
        nrm[block(i)] = attended
        put_t(ct_t, i, attended)

    loop(4, norm_f_back)
    take(AFTER_NORM_BACK)

    def attend_back(i):
        w = weights[0, i].reshape(D, D)
        dctx = between(natural(nrm[...], w[:, 512:768]), 64, 192).astype(BF)
        q8, v, k, cx = qb[i], vb[i], kb[i], cb[i]
        dq = jnp.zeros((LEN, 256), F32)
        dk = jnp.zeros((LEN, 256), F32)
        dv = jnp.zeros((LEN, 256), F32)
        for h in range(3):
            lane = lax.broadcasted_iota(jnp.int32, (LEN, 128), 1)
            lse = jnp.sum(jnp.where(lane == 3 * i + h, lse_ref[...], 0.0), axis=1, keepdims=True)
            p = jnp.exp(against(between(q8, 64 * h, 64), k) + bias[...] - lse)
            dm = between(dctx, 64 + 64 * h, 64)
            delta = jnp.sum(dm.astype(F32) * cx.astype(F32), axis=1, keepdims=True)
            ds_ = (p * (against(dm, v) - delta)).astype(BF)
            dq += between(natural(ds_, k), 64 * h, 64)
            dk += between(inner(ds_, q8), 64 * h, 64)
            dv += between(inner(p.astype(BF), dctx), 64 + 64 * h, 64)
            serve(3 * i + h, ATTEND_BACK)
        dq = dq * 0.125
        d = jnp.concatenate(
            [dq[:, 0:128], dq[:, 128:256] + dv[:, 0:128], dv[:, 128:256], dk], axis=1
        ).astype(BF)

        @pl.when(i < 3)
        def _():
            emit_other(0, i, na_t, d, (ct_t, cx))

        add(i, against(d, w[:, 0:640]))

        @pl.when(i < 3)
        def _():
            emit_own(0, i, na_t, d, (ct_t, cx))

        @pl.when(i == 3)
        def _():
            nrm[:, 0:640] = d

    loop(4, attend_back)

    def norm_a_back(i):
        xhat, scale = norm(x_ref[i].astype(F32))
        back, grad_gain = norm_back(acc[block(i)], xhat, scale, gain_a)
        gain_sum[0:1] += grad_gain[None]
        ct_ref[i] = (mid[block(i)] + back).astype(BF)

    loop(4, norm_a_back)
    rows_start(3, ct_ref, dxs_ref)
    emit_other(0, 3, na_t, nrm[:, 0:640], (ct_t, cb[3]))
    for i in range(2):
        for p in range(8):
            gain_parts[p, i : i + 1, 0:96] = gain_sum[i : i + 1, 96 * p : 96 * (p + 1)]

    def small_copy(i):
        to = lax.rem(dp + i, 8)
        return send(gain_parts.at[to], small.at[dp], egs.at[to], egr.at[dp], (to, z))

    def small_in(i):
        other = lax.rem(dp + i, 8)
        return send(gain_parts.at[other], small.at[other], egs.at[other], egr.at[other], (other, z))

    for i in range(1, 8):
        small_copy(i).start()
    emit_own(0, 3, na_t, nrm[:, 0:640], (ct_t, cb[3]))
    take(AFTER_ROWS)
    total = gain_parts[dp]
    for i in range(1, 8):
        small_in(i).wait_recv()
        total = total + small[lax.rem(dp + i, 8)]
    gain_own_sum[...] = total
    for j in range(1, 4):
        q = lax.rem(z + j, 4)
        send(gain_own_sum, small_z.at[z], egzs.at[q], egzr.at[z], (dp, q)).start()
    take(LAST)
    for i in range(1, 8):
        other = lax.rem(dp + i, 8)
        send(gain_own, gain_all.at[other], gs.at[other], gr.at[other], (other, z)).wait_send()
        small_copy(i).wait_send()
    for g in range(3):
        weights_sent(g)
    grads_sent(2)
    grads_sent(1)
    loop(4, lambda q: out_core(0, q).wait_send())
    rows_wait(2, out_ref, outs_ref)
    total = gain_own_sum[...]
    for j in range(1, 4):
        q = lax.rem(z + j, 4)
        cp = send(gain_own_sum, small_z.at[q], egzs.at[q], egzr.at[q], (dp, q))
        cp.wait()
        total = total + small_z[q]
    gain_a_ref[...] = total[0:1, 0:96]
    gain_f_ref[...] = total[1:2, 0:96]
    rows_wait(3, ct_ref, dxs_ref)
    last_add(0)
    grads_sent(0)


def layer(x, ct, segment_ids, w_query, w_key, w_value, w_output, w_up, w_down, gain_attn, gain_ffn):
    sem = pltpu.SemaphoreType.DMA
    vm = pltpu.VMEM
    anywhere = pl.BlockSpec(memory_space=pl.ANY)
    vmem = pl.BlockSpec(memory_space=pltpu.VMEM)
    return pl.pallas_call(
        layer_kernel,
        out_shape=(
            jax.ShapeDtypeStruct(x.shape, BF),
            jax.ShapeDtypeStruct(x.shape, BF),
            *(jax.ShapeDtypeStruct(n, F32) for n in [(96, 192)] * 3 + [(192, 96)] + [(96, D)] * 2 + [(1, 96)] * 2),
        ),
        in_specs=[anywhere] * 2 + [vmem] * 9,
        out_specs=[anywhere] * 2 + [vmem] * 8,
        scratch_shapes=[
            vm((16, 128), BF), vm((8, 16, 128), BF),
            vm((3, 4, 8, 96, D), BF),
            vm((4, BLOCK, D), BF), vm((4, BLOCK, D), BF), vm((4, BLOCK, D), BF),
            vm((LEN, D), BF),
            vm((4, 2, 96, LEN), BF), vm((4, 2, 96, LEN), BF), vm((4, 2, 96, LEN), BF),
            vm((4, LEN, 256), BF), vm((4, LEN, 256), BF), vm((4, LEN, 256), BF), vm((4, LEN, 256), BF),
            vm((LEN, 128), F32), vm((LEN, LEN), F32), vm((LEN, D), F32), vm((LEN, D), F32),
            vm((4, LEN, D), BF), vm((4, LEN, D), BF),
            vm((4, 4, 96, D), BF), vm((3, 4, 4, 96, D), BF), vm((2, 4, 4, 96, D), BF),
            vm((3, 4, 96, D), BF), vm((3, 4, 2, 96, D), BF), vm((3, 4, 96, D), BF),
            vm((8, 8, 128), F32), vm((4, 8, 128), F32), vm((8, D), F32), vm((8, 8, 128), F32), vm((8, 128), F32),
            sem((4,)),
            sem((3, 4, 2)), sem((3, 4)),
            sem((3, 4)), sem((3, 4)),
            sem((3, 4)), sem((3, 4)),
            sem((3, 4)), sem((3, 4)),
            sem((3, 4, 4)), sem((3, 4, 4)),
            sem((8,)), sem((8,)),
            sem((4, 4)), sem((4, 4)),
            sem((3, 4)), sem((3, 4)),
            sem((3, 4)), sem((3, 4)),
            sem((3, 4, 2)), sem((3, 4, 2)),
            sem((3, 4)), sem((3, 4)),
            sem((8,)), sem((8,)),
            sem((4,)), sem((4,)),
        ],
        compiler_params=pltpu.CompilerParams(
            collective_id=0, has_side_effects=True, vmem_limit_bytes=VMEM_LIMIT
        ),
        name="layer_with_copies",
    )(x, ct, segment_ids, w_query, w_key, w_value, w_output, w_up, w_down, gain_attn, gain_ffn)


VMEM_LIMIT = 62 * 2**20


def part_kernel(*refs):
    count = (len(refs) - 2) // 3
    sources, targets, held, (arrive, leave) = (
        refs[:count], refs[count : 2 * count], refs[2 * count : 3 * count], refs[3 * count :]
    )
    coming = [pltpu.make_async_copy(sources[i], held[i], arrive.at[i]) for i in range(count)]
    going = [pltpu.make_async_copy(held[i], targets[i], leave.at[i]) for i in range(count)]
    for copy in coming:
        copy.start()
    for copy_in, copy_out in zip(coming, going):
        copy_in.wait()
        copy_out.start()
    for copy in going:
        copy.wait()


def part(*results):
    anywhere = pl.BlockSpec(memory_space=pl.ANY)
    return pl.pallas_call(
        part_kernel,
        out_shape=[jax.ShapeDtypeStruct(r.shape, r.dtype) for r in results],
        in_specs=[anywhere] * len(results),
        out_specs=[anywhere] * len(results),
        scratch_shapes=[pltpu.VMEM(r.shape, r.dtype) for r in results]
        + [pltpu.SemaphoreType.DMA((len(results),))] * 2,
        name="part_outputs",
    )(*results)


def shards(
    inputs, segment_ids, w_query, w_key, w_value, w_output, w_up, w_down, gain_attn, gain_ffn, cotangent,
    *, parts, quarters,
):
    depth, width = w_query.shape
    if parts == 8 and quarters == 4:
        results = layer(
            inputs, cotangent, segment_ids, w_query, w_key, w_value, w_output, w_up, w_down.T,
            gain_attn.reshape(1, depth), gain_ffn.reshape(1, depth),
        )
        *outs, grad_down, grad_gain_attn, grad_gain_ffn = part(*results)
        return (*outs, grad_down.T, grad_gain_attn.reshape(depth), grad_gain_ffn.reshape(depth))
    else:
        z = lax.axis_index("mp")
        segment = lax.dynamic_index_in_dim(segment_ids, z, 0, keepdims=False)
        own = jnp.stack(
            [jnp.concatenate([w_query, w_value, w_key, w_output.T], axis=1), w_up, w_down.T]
        )
        weights = lax.all_gather(own, ("dp", "mp"), axis=0).reshape(parts, quarters, 3, depth, D)
        weights = weights.transpose(2, 1, 0, 3, 4).reshape(3, quarters, D, D)
        gains = jnp.stack(
            [lax.all_gather(g, "dp", axis=0, tiled=True) for g in (gain_attn, gain_ffn)]
        ).astype(F32)
        x, ct = (
            lax.all_to_all(a, "mp", split_axis=0, concat_axis=0, tiled=True) for a in (inputs, cotangent)
        )
        out, dx, grads, gg = row_layer(
            x.reshape(-1, D), ct.reshape(-1, D), segment, weights, gains[0], gains[1]
        )
        grads = grads.reshape(3, quarters, parts, depth, D).transpose(2, 1, 0, 3, 4)
        grads = grads.reshape(parts * quarters, 3, depth, D)
        total = lax.psum_scatter(grads, ("dp", "mp"), scatter_dimension=0).astype(F32)
        gg = lax.psum(lax.psum_scatter(gg, "dp", scatter_dimension=1, tiled=True), "mp")
        out, dx = (
            lax.all_to_all(a.reshape(inputs.shape), "mp", split_axis=0, concat_axis=0, tiled=True)
            for a in (out, dx)
        )
    return (
        out,
        dx,
        total[0, :, :width],
        total[0, :, 2 * width : 3 * width],
        total[0, :, width : 2 * width],
        total[0, :, 3 * width :].T,
        total[1],
        total[2].T,
        gg[0],
        gg[1],
    )


def solution(mesh):
    by_row = P("dp", "mp", None)
    grids = (P("dp", "mp"), P("dp", "mp"), P("dp", "mp"), P("mp", "dp"), P("dp", "mp"), P("mp", "dp"))
    gains = (P("dp"), P("dp"))
    return jax.shard_map(
        functools.partial(shards, parts=mesh.shape["dp"], quarters=mesh.shape["mp"]),
        mesh=mesh,
        in_specs=(by_row, P("dp", None)) + grids + gains + (by_row,),
        out_specs=(by_row, by_row) + grids + gains,
        check_vma=False,
    )
```

```python
import functools

import jax
import jax.numpy as jnp
from jax import lax
from jax.experimental import pallas as pl
from jax.experimental.pallas import tpu as pltpu
from jax.sharding import PartitionSpec as P

D = 768
HEADS = 12
HEAD = 64
EPS = 1e-05
MESH = pl.DeviceIdType.MESH
BF = jnp.bfloat16
F32 = jnp.float32


def dot(left, right, dims):
    return lax.dot_general(left, right, (dims, ((), ())), preferred_element_type=F32)


def natural(left, right):
    return dot(left, right, ((1,), (0,)))


def against(left, right):
    return dot(left, right, ((1,), (1,)))


def inner(left, right):
    return dot(left, right, ((0,), (0,)))


def norm(values):
    shifted = values - jnp.mean(values, axis=1, keepdims=True)
    scale = lax.rsqrt(jnp.mean(shifted * shifted, axis=1, keepdims=True) + EPS)
    return shifted * scale, scale


def norm_back(grad, xhat, scale, gain):
    e = grad * gain
    back = scale * (
        e - jnp.mean(e, axis=1, keepdims=True) - xhat * jnp.mean(e * xhat, axis=1, keepdims=True)
    )
    return back, jnp.sum(grad * xhat, axis=0)


def columns(w, first, count):
    part = w[:, :, first : first + count]
    return jnp.swapaxes(part, 0, 1).reshape(D, -1)


def row_layer(x, cotangent, segment, weights, gain_attn, gain_ffn):
    length = x.shape[0]
    quarters = weights.shape[1]
    width = D // quarters
    attn, up, down = weights[0], weights[1], weights[2]
    w_query, w_value, w_key, w_out = (columns(attn, i * width, width) for i in range(4))
    w_up, w_down = columns(up, 0, D), columns(down, 0, D)
    x = x.astype(F32)
    xhat_a, scale_a = norm(x)
    normed_a = (xhat_a * gain_attn).astype(BF)
    query, keys, values = (
        natural(normed_a, w).astype(BF).reshape(length, HEADS, HEAD) for w in (w_query, w_key, w_value)
    )
    same = segment[:, None] == segment[None, :]
    scores = jnp.einsum("qhd,khd->hqk", query, keys, preferred_element_type=F32) * HEAD**-0.5
    scores = jnp.where(same[None], scores, -1e30)
    exponent = jnp.exp(scores - jnp.max(scores, axis=2, keepdims=True))
    probs = exponent / jnp.sum(exponent, axis=2, keepdims=True)
    context = jnp.einsum("hqk,khd->qhd", probs.astype(BF), values, preferred_element_type=F32)
    context = context.reshape(length, D).astype(BF)
    middle = x + against(context, w_out)
    xhat_f, scale_f = norm(middle)
    normed_f = (xhat_f * gain_ffn).astype(BF)
    hidden = natural(normed_f, w_up)
    activated, gelu_back = jax.vjp(lambda v: jax.nn.gelu(v, approximate=False), hidden)
    activated = activated.astype(BF)
    output = (middle + against(activated, w_down)).astype(BF)

    grad_down = inner(cotangent, activated)
    grad_hidden = gelu_back(natural(cotangent, w_down))[0].astype(BF)
    grad_up = inner(normed_f, grad_hidden)
    back, grad_gain_ffn = norm_back(against(grad_hidden, w_up), xhat_f, scale_f, gain_ffn)
    grad_middle = cotangent.astype(F32) + back
    grad_attended = grad_middle.astype(BF)
    grad_out = inner(grad_attended, context)
    grad_context = natural(grad_attended, w_out).astype(BF).reshape(length, HEADS, HEAD)
    grad_probs = jnp.einsum("qhd,khd->hqk", grad_context, values, preferred_element_type=F32)
    grad_scores = (
        probs * (grad_probs - jnp.sum(probs * grad_probs, axis=2, keepdims=True))
    ).astype(BF)
    query_grad = jnp.einsum("hqk,khd->qhd", grad_scores, keys, preferred_element_type=F32) * HEAD**-0.5
    key_grad = jnp.einsum("hqk,qhd->khd", grad_scores, query, preferred_element_type=F32) * HEAD**-0.5
    value_grad = jnp.einsum(
        "hqk,qhd->khd", probs.astype(BF), grad_context, preferred_element_type=F32
    )
    query_grad, key_grad, value_grad = (
        g.reshape(length, D).astype(BF) for g in (query_grad, key_grad, value_grad)
    )
    grad_normed_a = (
        against(query_grad, w_query) + against(key_grad, w_key) + against(value_grad, w_value)
    )
    back, grad_gain_attn = norm_back(grad_normed_a, xhat_a, scale_a, gain_attn)
    input_grad = (grad_middle + back).astype(BF)

    def quarter(g, count):
        return g.astype(BF).reshape(D, quarters, count).swapaxes(0, 1)

    grads_attn = jnp.concatenate(
        [
            quarter(g, width)
            for g in (
                inner(normed_a, query_grad),
                inner(normed_a, value_grad),
                inner(normed_a, key_grad),
                grad_out,
            )
        ],
        axis=2,
    )
    grads = jnp.stack([grads_attn, quarter(grad_up, D), quarter(grad_down, D)])
    return output, input_grad, grads, jnp.stack([grad_gain_attn, grad_gain_ffn])


def between(value, first, count):
    lane = lax.broadcasted_iota(jnp.int32, value.shape, 1)
    return jnp.where((lane >= first) & (lane < first + count), value, jnp.zeros_like(value))


def place():
    dp, z = lax.axis_index("dp"), lax.axis_index("mp")
    c, x, y = lax.rem(dp, 2), lax.rem(dp // 2, 2), dp // 4
    return dp, z, c, dp + 2 - 4 * x, dp + 4 - 8 * y, dp + 1 - 2 * c


def send(src, dst, ssem, rsem, device):
    return pltpu.make_async_remote_copy(
        src_ref=src, dst_ref=dst, send_sem=ssem, recv_sem=rsem, device_id=device, device_id_type=MESH
    )


def nearest(z, k):
    inner_place = lax.rem((z + 1) // 2, 2)
    first_two = 1 - k // 2
    base = k + inner_place * first_two * (1 - 2 * k)
    return base + (z // 2) * (3 - 2 * base)


def gain_row(parts_ref, index):
    r = lax.broadcasted_iota(jnp.int32, (128, D), 0)
    col = lax.broadcasted_iota(jnp.int32, (128, D), 1)
    spread = jnp.where(lax.rem(col, 96) == r, 1.0, 0.0).astype(BF)
    total = jnp.zeros((1, D), F32)
    col = lax.broadcasted_iota(jnp.int32, (16, D), 1)
    row = lax.broadcasted_iota(jnp.int32, (16, D), 0)
    for p in range(8):
        full = natural(parts_ref[p], spread)
        keep = (row == index) & (col >= 96 * p) & (col < 96 * (p + 1))
        total = total + jnp.sum(jnp.where(keep, full, 0.0), axis=0, keepdims=True)
    return total


BLOCK = 128
LEN = 512

FIRST = ("b1", "a1", "z01", "s01", "z02", "s02", "z03", "s03", "x")
SECOND = (
    "p00", "p10", "p01", "iz11", "is11", "f00", "p02", "iz12", "is12", "p03", "f01", "iz13", "is13", "a2",
    "oz11", "os11", "f02", "oz12", "os12", "oz13", "os13", "b2", "f03",
)
THIRD = ()
ATTEND = {
    0: ("p11", "z21", "s21", "iz22", "is22", "iz23", "is23"), 1: ("p12", "f10"), 2: ("c", "p20"),
    3: ("p13",), 4: ("f11", "oz22", "os22"), 5: ("p21", "oz23", "os23"), 6: ("f12",), 7: ("p22", "f13"),
}
AFTER_NORM = ("p23", "f20")
TURN = {}
UP = {0: ("f21",), 1: ("f22",), 3: ("f23",)}
AFTER_GRAD_DOWN = ()
DOWN = {0: ("e20",), 1: ("e21",), 2: ("e22",), 3: ("e23",)}
UP_BACK = {}
AFTER_NORM_BACK = ("l20", "l21", "l22", "l23")
ATTEND_BACK = {
    0: ("e10", "e11"), 1: ("e12", "e13", "r20", "r21"), 3: ("l10", "l11"), 5: ("l12", "l13", "r10", "r11", "e00"),
    7: ("t2", "e01"),
}
AFTER_ROWS = ("e02", "e03", "t1")
LAST = ("l00", "l01", "l02", "r00", "r01", "l03")


def block(i):
    return pl.ds(pl.multiple_of(i * BLOCK, BLOCK), BLOCK)


def loop(count, step):
    def body(i, _):
        step(i)
        return 0

    lax.fori_loop(0, count, body, 0)


def layer_kernel(
    x_in, ct_in, seg_ref, wq_ref, wk_ref, wv_ref, wo_ref, wup_ref, wdown_ref, ga_ref, gf_ref,
    outs_ref, dxs_ref, q_ref, k_ref, v_ref, o_ref, up_ref, down_ref, gain_a_ref, gain_f_ref,
    gain_own, gain_all, weights, x_ref, ct_ref, out_ref,
    nrm, na_t, nf_t, ct_t, qb, kb, vb, cb, lse_ref, bias, mid, acc, act, gp,
    staged, sums, from_core, corner, from_plane, from_z, small, small_z, gain_sum, gain_parts, gain_own_sum,
    local_sem, zs, zr, xs, xr, ys, yr, ds, dr, cs, cr, gs, gr, as_, ar,
    ecs, ecr, eks, ekr, eps, epr, ezs, ezr, egs, egr, egzs, egzr,
):
    dp, z, c, nx, ny, nc = place()
    yx, yx_x, yx_y, yx_d = dp // 2, nx // 2, ny // 2, 3 - dp // 2

    barrier = pltpu.get_barrier_semaphore()
    for i in range(1, 8):
        pl.semaphore_signal(barrier, inc=1, device_id=(lax.rem(dp + i, 8), z), device_id_type=MESH)
    for i in range(1, 4):
        pl.semaphore_signal(barrier, inc=1, device_id=(dp, lax.rem(z + i, 4)), device_id_type=MESH)

    weights[0, z, dp] = jnp.concatenate(
        [wq_ref[...], wv_ref[...], wk_ref[...], wo_ref[...].T], axis=1
    )
    weights[1, z, dp] = wup_ref[...]
    weights[2, z, dp] = wdown_ref[...]
    gain_own[...] = jnp.zeros_like(gain_own)
    gain_own[0:1, 0:96] = ga_ref[...]
    gain_own[1:2, 0:96] = gf_ref[...]
    pl.semaphore_wait(barrier, 10)

    def rows_start(i, src, dst):
        for j in range(1, 4):
            q = lax.rem(z + j, 4)
            send(src.at[q], dst.at[z], as_.at[i, q], ar.at[i, z], (dp, q)).start()
        pltpu.make_async_copy(src.at[z], dst.at[z], local_sem.at[i]).start()

    def rows_wait(i, src, dst):
        for j in range(1, 4):
            q = lax.rem(z + j, 4)
            cp = send(src.at[q], dst.at[q], as_.at[i, q], ar.at[i, q], (dp, q))
            cp.wait_send()
            cp.wait_recv()
        pltpu.make_async_copy(src.at[z], dst.at[z], local_sem.at[i]).wait()

    def tile(g, q, d):
        return weights.at[g, q, d]

    mate = z + 1 - 2 * lax.rem(z, 2)
    far_inner = 2 - z // 2
    outer = (z == 0) | (z == 3)
    other_side = 2 * (1 - z // 2)

    def z_copy(g, q, side, to):
        return send(tile(g, q, dp), tile(g, q, dp), zs.at[g, q, side], zr.at[g, q], (dp, to))

    def passes_on(q):
        return jnp.logical_not(outer) & (q // 2 != z // 2)

    def own_z(g):
        z_copy(g, z, 0, mate).start()
        z_copy(g, z, 1, far_inner).start()

    def z_done(g, q):
        @pl.when(q == z)
        def _():
            z_copy(g, q, 0, mate).wait_send()
            z_copy(g, q, 1, far_inner).wait_send()

        @pl.when(passes_on(q))
        def _():
            z_copy(g, q, 0, mate).wait_send()

    def x_copy(g, q):
        return send(tile(g, q, dp), tile(g, q, dp), xs.at[g, q], xr.at[g, q], (nx, z))

    def y_copy(g, q):
        return send(tile(g, q, dp), tile(g, q, dp), ys.at[g, q], yr.at[g, q], (ny, z))

    def core_copy(g, q, pos):
        d = 2 * pos + c
        return send(tile(g, q, d), tile(g, q, d), cs.at[g, q, pos], cr.at[g, q, pos], (nc, z))

    def forward(g, q, along_y):
        src, to = (nx, ny) if along_y else (ny, nx)
        return send(tile(g, q, src), tile(g, q, src), ds.at[g, q], dr.at[g, q], (to, z))

    def own_plane(g):
        x_copy(g, z).start()
        y_copy(g, z).start()
        core_copy(g, z, yx).start()

    def z_step(g, k):
        q = nearest(z, k)
        z_copy(g, q, 0, mate).wait_recv()

        @pl.when(passes_on(q))
        def _():
            z_copy(g, q, 0, mate).start()

    def spread_step(g, k):
        q = nearest(z, k)
        x_copy(g, q).start()
        y_copy(g, q).start()
        core_copy(g, q, yx).start()

    def plane_step(g, k):
        q = nearest(z, k)
        x_copy(g, q).wait_recv()

        @pl.when(lax.rem(q, 2) == 0)
        def _():
            forward(g, q, True).start()

        core_copy(g, q, yx_x).start()
        y_copy(g, q).wait_recv()

        @pl.when(lax.rem(q, 2) == 1)
        def _():
            forward(g, q, False).start()

        core_copy(g, q, yx_y).start()

    def far_step(g, k):
        q = nearest(z, k)
        d = 2 * yx_d + c
        send(tile(g, q, d), tile(g, q, d), ds.at[g, q], dr.at[g, q], (nx, z)).wait_recv()
        core_copy(g, q, yx_d).start()

    def core_ready(g, q):
        for pos in range(4):
            d = 2 * pos + 1 - c
            send(
                tile(g, q, d), tile(g, q, d), cs.at[g, q, pos], cr.at[g, q, pos], (nc, z)
            ).wait_recv()

    def weights_sent(g):
        def step(q):
            z_done(g, q)
            x_copy(g, q).wait_send()
            y_copy(g, q).wait_send()

            @pl.when(lax.rem(q, 2) == 0)
            def _():
                forward(g, q, True).wait_send()

            @pl.when(lax.rem(q, 2) == 1)
            def _():
                forward(g, q, False).wait_send()

            for pos in range(4):
                core_copy(g, q, pos).wait_send()

        loop(4, step)

    def out_core(g, q):
        return send(staged.at[q], from_core.at[q], ecs.at[g, q], ecr.at[g, q], (nc, z))

    def out_corner(g, q):
        to = nx + (ny - nx) * lax.rem(q, 2)
        return send(sums.at[g, q, yx_d], corner.at[g, q], eks.at[g, q], ekr.at[g, q], (to, z))

    def out_plane(g, q, side):
        to = nx + (ny - nx) * side
        pos = yx_x + (yx_y - yx_x) * side
        return send(
            sums.at[g, q, pos], from_plane.at[g, q, side], eps.at[g, q, side], epr.at[g, q, side], (to, z)
        )

    def out_z(g, q, slot, to):
        return send(sums.at[g, q, yx], from_z.at[g, slot], ezs.at[g, q], ezr.at[g, slot], (dp, to))

    def in_z(g, slot):
        return send(sums.at[g, 0, yx], from_z.at[g, slot], ezs.at[g, 0], ezr.at[g, slot], (dp, mate))

    def corner_add(g, q):
        side = 1 - lax.rem(q, 2)
        pos = yx_x + (yx_y - yx_x) * side
        out_corner(g, q).wait_recv()
        sums[g, q, pos] = (sums[g, q, pos].astype(F32) + corner[g, q].astype(F32)).astype(BF)
        out_plane(g, q, side).start()

    def plane_add(g, q):
        out_plane(g, q, 0).wait_recv()
        out_plane(g, q, 1).wait_recv()
        sums[g, q, yx] = (
            sums[g, q, yx].astype(F32)
            + from_plane[g, q, 0].astype(F32)
            + from_plane[g, q, 1].astype(F32)
        ).astype(BF)

        @pl.when(q == mate)
        def _():
            out_z(g, q, 0, mate).start()

        @pl.when(outer & (q // 2 != z // 2))
        def _():
            out_z(g, q, 2 + lax.rem(q, 2), mate).start()

    def relay(g, k):
        q = quarter(k)

        @pl.when(jnp.logical_not(outer))
        def _():
            slot = 2 + lax.rem(q, 2)
            in_z(g, slot).wait_recv()
            sums[g, q, yx] = (sums[g, q, yx].astype(F32) + from_z[g, slot].astype(F32)).astype(BF)
            out_z(g, q, 1, q).start()

    def last_add(g):
        in_z(g, 0).wait_recv()
        in_z(g, 1).wait_recv()
        total = sums[g, z, yx].astype(F32) + from_z[g, 0].astype(F32) + from_z[g, 1].astype(F32)
        if g == 0:
            q_ref[...] = total[:, 0:192]
            v_ref[...] = total[:, 192:384]
            k_ref[...] = total[:, 384:576]
            o_ref[...] = total[:, 576:768].T
        else:
            (up_ref if g == 1 else down_ref)[...] = total

    def grads_sent(g):
        def step(q):
            out_corner(g, q).wait_send()
            out_plane(g, q, 0).wait_send()
            out_plane(g, q, 1).wait_send()

            @pl.when(z != q)
            def _():
                out_z(g, q, 0, mate).wait_send()

        loop(4, step)

    def quarter(k):
        return nearest(z, 3 - k)

    def grad_rows(half, left, right, more):
        v = natural(left[:, half].reshape(384, LEN), right)
        if more is None:
            return ((0, v),)
        v2 = natural(more[0][:, half].reshape(384, LEN), more[1])
        return ((0, v[:, 0:512]), (512, v[:, 512:640] + v2[:, 0:128]), (640, v2[:, 128:256]))

    def emit_other(g, q, left, right, more=None):
        if g < 2:
            out_core(g + 1, q).wait_send()
        for first, v in grad_rows(1 - c, left, right, more):
            staged[q, :, :, first : first + v.shape[1]] = v.astype(BF).reshape(4, 96, v.shape[1])
        out_core(g, q).start()

    def emit_own(g, k, left, right, more=None):
        q = quarter(k)
        pieces = grad_rows(c, left, right, more)
        out_core(g, q).wait_recv()
        for first, v in pieces:
            lanes = slice(first, first + v.shape[1])
            theirs = from_core[q, :, :, lanes].astype(F32)
            sums[g, q, :, :, lanes] = (v.reshape(4, 96, v.shape[1]) + theirs).astype(BF)
        out_corner(g, q).start()

        @pl.when(k >= 1)
        def _():
            before = quarter(k - 1)
            out_plane(g, before, lax.rem(before, 2)).start()

        @pl.when(k == 3)
        def _():
            out_plane(g, q, lax.rem(q, 2)).start()

    def put_t(dst, i, v):
        dst[:, :, :, block(i)] = v.T.reshape(4, 2, 96, BLOCK)

    def add(i, value):
        @pl.when(i == 0)
        def _():
            acc[...] = value

        @pl.when(i > 0)
        def _():
            acc[...] += value

    steps = {
        "a": own_z, "b": own_plane, "z": z_step, "s": spread_step, "p": plane_step, "f": far_step,
        "x": lambda: rows_start(0, x_in, x_ref), "c": lambda: rows_start(1, ct_in, ct_ref),
        "e": lambda g, k: corner_add(g, quarter(k)), "l": lambda g, k: plane_add(g, quarter(k)), "r": relay, "t": last_add,
    }

    def take(names):
        for name in names:
            act_on = functools.partial(steps[name.lstrip("io")[0]], *map(int, name.lstrip("io")[1:]))
            if name[0] in "io":
                pl.when(outer if name[0] == "o" else jnp.logical_not(outer))(act_on)
            else:
                act_on()

    def serve(now, table):
        for due, names in table.items():
            pl.when(now == due)(functools.partial(take, names))

    own_z(0)
    own_plane(0)
    for i in range(1, 8):
        to = lax.rem(dp + i, 8)
        send(gain_own, gain_all.at[dp], gs.at[to], gr.at[dp], (to, z)).start()
    gain_all[dp] = gain_own[...]
    take(FIRST)
    seg_row = seg_ref[pl.ds(z, 1)].astype(F32)
    seg_col = jnp.broadcast_to(seg_row, (8, LEN)).T[:, 0:1]
    bias[...] = jnp.where(seg_col == seg_row, 0.0, -1e30)
    gain_sum[...] = jnp.zeros_like(gain_sum)
    gain_parts[...] = jnp.zeros_like(gain_parts)
    take(SECOND)
    for i in range(1, 8):
        other = lax.rem(dp + i, 8)
        send(gain_own, gain_all.at[other], gs.at[other], gr.at[other], (other, z)).wait_recv()
    gain_a = gain_row(gain_all, 0)
    gain_f = gain_row(gain_all, 1)
    take(THIRD)
    rows_wait(0, x_in, x_ref)

    def norm_a(i):
        xhat, _ = norm(x_ref[i].astype(F32))
        normed = (xhat * gain_a).astype(BF)
        nrm[block(i)] = normed
        put_t(na_t, i, normed)

    loop(4, norm_a)

    def attend(i):
        q = nearest(z, i)
        core_ready(0, q)
        w = weights[0, q].reshape(D, D)
        p = natural(nrm[...], w[:, 0:640])
        q8 = p[:, 0:256].astype(BF) * jnp.asarray(0.125, BF)
        v = p[:, 128:384].astype(BF)
        k = p[:, 384:640].astype(BF)
        qb[q] = q8
        vb[q] = v
        kb[q] = k
        for r in range(2):
            rs = slice(256 * r, 256 * (r + 1))
            ctx = jnp.zeros((256, 256), F32)
            lane = lax.broadcasted_iota(jnp.int32, (256, 128), 1)
            lse = lse_ref[rs]
            for h in range(3):
                s = against(between(q8[rs], 64 * h, 64), k) + bias[rs]
                m = jnp.max(s, axis=1, keepdims=True)
                e = jnp.exp(s - m)
                total = jnp.sum(e, axis=1, keepdims=True)
                ctx += natural(e.astype(BF), between(v, 64 + 64 * h, 64)) * (1.0 / total)
                lse = jnp.where(lane == 3 * q + h, m + jnp.log(total), lse)
            lse_ref[rs] = lse
            cb[q, rs] = ctx.astype(BF)
            serve(2 * i + r, ATTEND)

    loop(4, attend)

    def attend_out(i):
        add(i, against(cb[i], weights[0, i].reshape(D, D)[:, 512:768]))

    loop(4, attend_out)

    def norm_f(i):
        m = x_ref[i].astype(F32) + acc[block(i)]
        mid[block(i)] = m
        xhat, _ = norm(m)
        normed = (xhat * gain_f).astype(BF)
        nrm[block(i)] = normed
        put_t(nf_t, i, normed)

    loop(4, norm_f)
    take(AFTER_NORM)
    rows_wait(1, ct_in, ct_ref)

    def turn_ct(i):
        put_t(ct_t, i, ct_ref[i])
        serve(i, TURN)

    loop(4, turn_ct)

    def up(i):
        q = quarter(i)
        core_ready(1, q)
        w = weights[1, q].reshape(D, D)
        for r in range(2):
            rs = slice(256 * r, 256 * (r + 1))
            h = natural(nrm[rs], w)
            cdf = 0.5 + 0.5 * lax.erf(h * 0.7071067811865476)
            act[q, rs] = (h * cdf).astype(BF)
            gp[q, rs] = (cdf + h * (jnp.exp(-0.5 * h * h) * 0.3989422804014327)).astype(BF)
        emit_other(2, q, ct_t, act[q])

        @pl.when(i > 0)
        def _():
            emit_own(2, i - 1, ct_t, act[quarter(i - 1)])

        serve(i, UP)

    loop(4, up)
    emit_own(2, 3, ct_t, act[quarter(3)])
    take(AFTER_GRAD_DOWN)

    def down(i):
        q = nearest(z, i)
        core_ready(2, q)
        w = weights[2, q].reshape(D, D)
        gp[q] = (natural(ct_ref[...].reshape(LEN, D), w) * gp[q].astype(F32)).astype(BF)
        add(i, against(act[q], w))
        serve(i, DOWN)

    loop(4, down)
    out_ref[...] = (mid[...] + acc[...]).astype(BF).reshape(4, BLOCK, D)
    rows_start(2, out_ref, outs_ref)

    def up_back(i):
        q = quarter(i)
        emit_other(1, q, nf_t, gp[q])
        add(i, against(gp[q], weights[1, q].reshape(D, D)))
        emit_own(1, i, nf_t, gp[q])

        serve(i, UP_BACK)

    loop(4, up_back)

    def norm_f_back(i):
        xhat, scale = norm(mid[block(i)])
        back, grad_gain = norm_back(acc[block(i)], xhat, scale, gain_f)
        gain_sum[1:2] += grad_gain[None]
        grad_middle = ct_ref[i].astype(F32) + back
        mid[block(i)] = grad_middle
        attended = grad_middle.astype(BF)
        nrm[block(i)] = attended
        put_t(ct_t, i, attended)

    loop(4, norm_f_back)
    take(AFTER_NORM_BACK)

    def attend_back(i):
        q = quarter(i)
        w = weights[0, q].reshape(D, D)
        dctx = between(natural(nrm[...], w[:, 512:768]), 64, 192).astype(BF)
        q8, v, k, cx = qb[q], vb[q], kb[q], cb[q]
        dq = jnp.zeros((LEN, 256), F32)
        dk = jnp.zeros((LEN, 256), F32)
        dv = jnp.zeros((LEN, 256), F32)
        for h in range(3):
            lane = lax.broadcasted_iota(jnp.int32, (LEN, 128), 1)
            lse = jnp.sum(jnp.where(lane == 3 * q + h, lse_ref[...], 0.0), axis=1, keepdims=True)
            p = jnp.exp(against(between(q8, 64 * h, 64), k) + bias[...] - lse)
            dm = between(dctx, 64 + 64 * h, 64)
            delta = jnp.sum(dm.astype(F32) * cx.astype(F32), axis=1, keepdims=True)
            ds_ = (p * (against(dm, v) - delta)).astype(BF)
            dq += between(natural(ds_, k), 64 * h, 64)
            dk += between(inner(ds_, q8), 64 * h, 64)
            dv += between(inner(p.astype(BF), dctx), 64 + 64 * h, 64)
        dq = dq * 0.125
        d = jnp.concatenate(
            [dq[:, 0:128], dq[:, 128:256] + dv[:, 0:128], dv[:, 128:256], dk], axis=1
        ).astype(BF)

        serve(2 * i, ATTEND_BACK)
        emit_other(0, q, na_t, d, (ct_t, cx))
        add(i, against(d, w[:, 0:640]))
        emit_own(0, i, na_t, d, (ct_t, cx))
        serve(2 * i + 1, ATTEND_BACK)

    loop(4, attend_back)

    def norm_a_back(i):
        xhat, scale = norm(x_ref[i].astype(F32))
        back, grad_gain = norm_back(acc[block(i)], xhat, scale, gain_a)
        gain_sum[0:1] += grad_gain[None]
        ct_ref[i] = (mid[block(i)] + back).astype(BF)

    loop(4, norm_a_back)
    rows_start(3, ct_ref, dxs_ref)
    for i in range(2):
        for p in range(8):
            gain_parts[p, i : i + 1, 0:96] = gain_sum[i : i + 1, 96 * p : 96 * (p + 1)]

    def small_copy(i):
        to = lax.rem(dp + i, 8)
        return send(gain_parts.at[to], small.at[dp], egs.at[to], egr.at[dp], (to, z))

    def small_in(i):
        other = lax.rem(dp + i, 8)
        return send(gain_parts.at[other], small.at[other], egs.at[other], egr.at[other], (other, z))

    for i in range(1, 8):
        small_copy(i).start()
    take(AFTER_ROWS)
    total = gain_parts[dp]
    for i in range(1, 8):
        small_in(i).wait_recv()
        total = total + small[lax.rem(dp + i, 8)]
    gain_own_sum[...] = total
    for j in range(1, 4):
        q = lax.rem(z + j, 4)
        send(gain_own_sum, small_z.at[z], egzs.at[q], egzr.at[z], (dp, q)).start()
    take(LAST)
    for i in range(1, 8):
        other = lax.rem(dp + i, 8)
        send(gain_own, gain_all.at[other], gs.at[other], gr.at[other], (other, z)).wait_send()
        small_copy(i).wait_send()
    for g in range(3):
        weights_sent(g)
    grads_sent(2)
    grads_sent(1)
    loop(4, lambda q: out_core(0, q).wait_send())
    rows_wait(2, out_ref, outs_ref)
    total = gain_own_sum[...]
    for j in range(1, 4):
        q = lax.rem(z + j, 4)
        cp = send(gain_own_sum, small_z.at[q], egzs.at[q], egzr.at[q], (dp, q))
        cp.wait()
        total = total + small_z[q]
    gain_a_ref[...] = total[0:1, 0:96]
    gain_f_ref[...] = total[1:2, 0:96]
    rows_wait(3, ct_ref, dxs_ref)
    last_add(0)
    grads_sent(0)


def layer(x, ct, segment_ids, w_query, w_key, w_value, w_output, w_up, w_down, gain_attn, gain_ffn):
    sem = pltpu.SemaphoreType.DMA
    vm = pltpu.VMEM
    anywhere = pl.BlockSpec(memory_space=pl.ANY)
    vmem = pl.BlockSpec(memory_space=pltpu.VMEM)
    return pl.pallas_call(
        layer_kernel,
        out_shape=(
            jax.ShapeDtypeStruct(x.shape, BF),
            jax.ShapeDtypeStruct(x.shape, BF),
            *(jax.ShapeDtypeStruct(n, F32) for n in [(96, 192)] * 3 + [(192, 96)] + [(96, D)] * 2 + [(1, 96)] * 2),
        ),
        in_specs=[anywhere] * 2 + [vmem] * 9,
        out_specs=[anywhere] * 2 + [vmem] * 8,
        scratch_shapes=[
            vm((16, 128), BF), vm((8, 16, 128), BF),
            vm((3, 4, 8, 96, D), BF),
            vm((4, BLOCK, D), BF), vm((4, BLOCK, D), BF), vm((4, BLOCK, D), BF),
            vm((LEN, D), BF),
            vm((4, 2, 96, LEN), BF), vm((4, 2, 96, LEN), BF), vm((4, 2, 96, LEN), BF),
            vm((4, LEN, 256), BF), vm((4, LEN, 256), BF), vm((4, LEN, 256), BF), vm((4, LEN, 256), BF),
            vm((LEN, 128), F32), vm((LEN, LEN), F32), vm((LEN, D), F32), vm((LEN, D), F32),
            vm((4, LEN, D), BF), vm((4, LEN, D), BF),
            vm((4, 4, 96, D), BF), vm((3, 4, 4, 96, D), BF), vm((4, 4, 96, D), BF),
            vm((3, 4, 96, D), BF), vm((3, 4, 2, 96, D), BF), vm((3, 4, 96, D), BF),
            vm((8, 8, 128), F32), vm((4, 8, 128), F32), vm((8, D), F32), vm((8, 8, 128), F32), vm((8, 128), F32),
            sem((4,)),
            sem((3, 4, 2)), sem((3, 4)),
            sem((3, 4)), sem((3, 4)),
            sem((3, 4)), sem((3, 4)),
            sem((3, 4)), sem((3, 4)),
            sem((3, 4, 4)), sem((3, 4, 4)),
            sem((8,)), sem((8,)),
            sem((4, 4)), sem((4, 4)),
            sem((3, 4)), sem((3, 4)),
            sem((3, 4)), sem((3, 4)),
            sem((3, 4, 2)), sem((3, 4, 2)),
            sem((3, 4)), sem((3, 4)),
            sem((8,)), sem((8,)),
            sem((4,)), sem((4,)),
        ],
        compiler_params=pltpu.CompilerParams(
            collective_id=0, has_side_effects=True, vmem_limit_bytes=VMEM_LIMIT
        ),
        name="layer_with_copies",
    )(x, ct, segment_ids, w_query, w_key, w_value, w_output, w_up, w_down, gain_attn, gain_ffn)


VMEM_LIMIT = 62 * 2**20


def part_kernel(*refs):
    count = (len(refs) - 2) // 3
    sources, targets, held, (arrive, leave) = (
        refs[:count], refs[count : 2 * count], refs[2 * count : 3 * count], refs[3 * count :]
    )
    coming = [pltpu.make_async_copy(sources[i], held[i], arrive.at[i]) for i in range(count)]
    going = [pltpu.make_async_copy(held[i], targets[i], leave.at[i]) for i in range(count)]
    for copy in coming:
        copy.start()
    for copy_in, copy_out in zip(coming, going):
        copy_in.wait()
        copy_out.start()
    for copy in going:
        copy.wait()


def part(*results):
    anywhere = pl.BlockSpec(memory_space=pl.ANY)
    return pl.pallas_call(
        part_kernel,
        out_shape=[jax.ShapeDtypeStruct(r.shape, r.dtype) for r in results],
        in_specs=[anywhere] * len(results),
        out_specs=[anywhere] * len(results),
        scratch_shapes=[pltpu.VMEM(r.shape, r.dtype) for r in results]
        + [pltpu.SemaphoreType.DMA((len(results),))] * 2,
        name="part_outputs",
    )(*results)


def shards(
    inputs, segment_ids, w_query, w_key, w_value, w_output, w_up, w_down, gain_attn, gain_ffn, cotangent,
    *, parts, quarters,
):
    depth, width = w_query.shape
    if parts == 8 and quarters == 4:
        results = layer(
            inputs, cotangent, segment_ids, w_query, w_key, w_value, w_output, w_up, w_down.T,
            gain_attn.reshape(1, depth), gain_ffn.reshape(1, depth),
        )
        *outs, grad_down, grad_gain_attn, grad_gain_ffn = part(*results)
        return (*outs, grad_down.T, grad_gain_attn.reshape(depth), grad_gain_ffn.reshape(depth))
    else:
        z = lax.axis_index("mp")
        segment = lax.dynamic_index_in_dim(segment_ids, z, 0, keepdims=False)
        own = jnp.stack(
            [jnp.concatenate([w_query, w_value, w_key, w_output.T], axis=1), w_up, w_down.T]
        )
        weights = lax.all_gather(own, ("dp", "mp"), axis=0).reshape(parts, quarters, 3, depth, D)
        weights = weights.transpose(2, 1, 0, 3, 4).reshape(3, quarters, D, D)
        gains = jnp.stack(
            [lax.all_gather(g, "dp", axis=0, tiled=True) for g in (gain_attn, gain_ffn)]
        ).astype(F32)
        x, ct = (
            lax.all_to_all(a, "mp", split_axis=0, concat_axis=0, tiled=True) for a in (inputs, cotangent)
        )
        out, dx, grads, gg = row_layer(
            x.reshape(-1, D), ct.reshape(-1, D), segment, weights, gains[0], gains[1]
        )
        grads = grads.reshape(3, quarters, parts, depth, D).transpose(2, 1, 0, 3, 4)
        grads = grads.reshape(parts * quarters, 3, depth, D)
        total = lax.psum_scatter(grads, ("dp", "mp"), scatter_dimension=0).astype(F32)
        gg = lax.psum(lax.psum_scatter(gg, "dp", scatter_dimension=1, tiled=True), "mp")
        out, dx = (
            lax.all_to_all(a.reshape(inputs.shape), "mp", split_axis=0, concat_axis=0, tiled=True)
            for a in (out, dx)
        )
    return (
        out,
        dx,
        total[0, :, :width],
        total[0, :, 2 * width : 3 * width],
        total[0, :, width : 2 * width],
        total[0, :, 3 * width :].T,
        total[1],
        total[2].T,
        gg[0],
        gg[1],
    )


def solution(mesh):
    by_row = P("dp", "mp", None)
    grids = (P("dp", "mp"), P("dp", "mp"), P("dp", "mp"), P("mp", "dp"), P("dp", "mp"), P("mp", "dp"))
    gains = (P("dp"), P("dp"))
    return jax.shard_map(
        functools.partial(shards, parts=mesh.shape["dp"], quarters=mesh.shape["mp"]),
        mesh=mesh,
        in_specs=(by_row, P("dp", None)) + grids + gains + (by_row,),
        out_specs=(by_row, by_row) + grids + gains,
        check_vma=False,
    )
```

```python
import functools

import jax
import jax.numpy as jnp
from jax import lax
from jax.experimental import pallas as pl
from jax.experimental.pallas import tpu as pltpu
from jax.sharding import PartitionSpec as P

D = 768
HEADS = 12
HEAD = 64
EPS = 1e-05
MESH = pl.DeviceIdType.MESH
BF = jnp.bfloat16
F32 = jnp.float32


def dot(left, right, dims):
    return lax.dot_general(left, right, (dims, ((), ())), preferred_element_type=F32)


def natural(left, right):
    return dot(left, right, ((1,), (0,)))


def against(left, right):
    return dot(left, right, ((1,), (1,)))


def inner(left, right):
    return dot(left, right, ((0,), (0,)))


def norm(values):
    shifted = values - jnp.mean(values, axis=1, keepdims=True)
    scale = lax.rsqrt(jnp.mean(shifted * shifted, axis=1, keepdims=True) + EPS)
    return shifted * scale, scale


def norm_back(grad, xhat, scale, gain):
    e = grad * gain
    back = scale * (
        e - jnp.mean(e, axis=1, keepdims=True) - xhat * jnp.mean(e * xhat, axis=1, keepdims=True)
    )
    return back, jnp.sum(grad * xhat, axis=0)


def columns(w, first, count):
    part = w[:, :, first : first + count]
    return jnp.swapaxes(part, 0, 1).reshape(D, -1)


def row_layer(x, cotangent, segment, weights, gain_attn, gain_ffn):
    length = x.shape[0]
    quarters = weights.shape[1]
    width = D // quarters
    attn, up, down = weights[0], weights[1], weights[2]
    w_query, w_value, w_key, w_out = (columns(attn, i * width, width) for i in range(4))
    w_up, w_down = columns(up, 0, D), columns(down, 0, D)
    x = x.astype(F32)
    xhat_a, scale_a = norm(x)
    normed_a = (xhat_a * gain_attn).astype(BF)
    query, keys, values = (
        natural(normed_a, w).astype(BF).reshape(length, HEADS, HEAD) for w in (w_query, w_key, w_value)
    )
    same = segment[:, None] == segment[None, :]
    scores = jnp.einsum("qhd,khd->hqk", query, keys, preferred_element_type=F32) * HEAD**-0.5
    scores = jnp.where(same[None], scores, -1e30)
    exponent = jnp.exp(scores - jnp.max(scores, axis=2, keepdims=True))
    probs = exponent / jnp.sum(exponent, axis=2, keepdims=True)
    context = jnp.einsum("hqk,khd->qhd", probs.astype(BF), values, preferred_element_type=F32)
    context = context.reshape(length, D).astype(BF)
    middle = x + against(context, w_out)
    xhat_f, scale_f = norm(middle)
    normed_f = (xhat_f * gain_ffn).astype(BF)
    hidden = natural(normed_f, w_up)
    activated, gelu_back = jax.vjp(lambda v: jax.nn.gelu(v, approximate=False), hidden)
    activated = activated.astype(BF)
    output = (middle + against(activated, w_down)).astype(BF)

    grad_down = inner(cotangent, activated)
    grad_hidden = gelu_back(natural(cotangent, w_down))[0].astype(BF)
    grad_up = inner(normed_f, grad_hidden)
    back, grad_gain_ffn = norm_back(against(grad_hidden, w_up), xhat_f, scale_f, gain_ffn)
    grad_middle = cotangent.astype(F32) + back
    grad_attended = grad_middle.astype(BF)
    grad_out = inner(grad_attended, context)
    grad_context = natural(grad_attended, w_out).astype(BF).reshape(length, HEADS, HEAD)
    grad_probs = jnp.einsum("qhd,khd->hqk", grad_context, values, preferred_element_type=F32)
    grad_scores = (
        probs * (grad_probs - jnp.sum(probs * grad_probs, axis=2, keepdims=True))
    ).astype(BF)
    query_grad = jnp.einsum("hqk,khd->qhd", grad_scores, keys, preferred_element_type=F32) * HEAD**-0.5
    key_grad = jnp.einsum("hqk,qhd->khd", grad_scores, query, preferred_element_type=F32) * HEAD**-0.5
    value_grad = jnp.einsum(
        "hqk,qhd->khd", probs.astype(BF), grad_context, preferred_element_type=F32
    )
    query_grad, key_grad, value_grad = (
        g.reshape(length, D).astype(BF) for g in (query_grad, key_grad, value_grad)
    )
    grad_normed_a = (
        against(query_grad, w_query) + against(key_grad, w_key) + against(value_grad, w_value)
    )
    back, grad_gain_attn = norm_back(grad_normed_a, xhat_a, scale_a, gain_attn)
    input_grad = (grad_middle + back).astype(BF)

    def quarter(g, count):
        return g.astype(BF).reshape(D, quarters, count).swapaxes(0, 1)

    grads_attn = jnp.concatenate(
        [
            quarter(g, width)
            for g in (
                inner(normed_a, query_grad),
                inner(normed_a, value_grad),
                inner(normed_a, key_grad),
                grad_out,
            )
        ],
        axis=2,
    )
    grads = jnp.stack([grads_attn, quarter(grad_up, D), quarter(grad_down, D)])
    return output, input_grad, grads, jnp.stack([grad_gain_attn, grad_gain_ffn])


def between(value, first, count):
    lane = lax.broadcasted_iota(jnp.int32, value.shape, 1)
    return jnp.where((lane >= first) & (lane < first + count), value, jnp.zeros_like(value))


def place():
    dp, z = lax.axis_index("dp"), lax.axis_index("mp")
    c, x, y = lax.rem(dp, 2), lax.rem(dp // 2, 2), dp // 4
    return dp, z, c, dp + 2 - 4 * x, dp + 4 - 8 * y, dp + 1 - 2 * c


def send(src, dst, ssem, rsem, device):
    return pltpu.make_async_remote_copy(
        src_ref=src, dst_ref=dst, send_sem=ssem, recv_sem=rsem, device_id=device, device_id_type=MESH
    )


def nearest(z, k):
    inner_place = lax.rem((z + 1) // 2, 2)
    first_two = 1 - k // 2
    base = k + inner_place * first_two * (1 - 2 * k)
    return base + (z // 2) * (3 - 2 * base)


def gain_row(parts_ref, index):
    r = lax.broadcasted_iota(jnp.int32, (128, D), 0)
    col = lax.broadcasted_iota(jnp.int32, (128, D), 1)
    spread = jnp.where(lax.rem(col, 96) == r, 1.0, 0.0).astype(BF)
    total = jnp.zeros((1, D), F32)
    col = lax.broadcasted_iota(jnp.int32, (16, D), 1)
    row = lax.broadcasted_iota(jnp.int32, (16, D), 0)
    for p in range(8):
        full = natural(parts_ref[p], spread)
        keep = (row == index) & (col >= 96 * p) & (col < 96 * (p + 1))
        total = total + jnp.sum(jnp.where(keep, full, 0.0), axis=0, keepdims=True)
    return total


BLOCK = 128
LEN = 512

FIRST = ("b1", "a1", "z01", "s01", "z02", "s02", "z03", "s03", "x")
SECOND = (
    "p00", "p10", "p01", "iz11", "is11", "f00", "p02", "iz12", "is12", "p03", "f01", "iz13", "is13", "a2",
    "oz11", "os11", "f02", "oz12", "os12", "oz13", "os13", "b2", "f03",
)
THIRD = ()
ATTEND = {0: ('p11','z21','s21','iz22','is22','iz23','is23'), 1: ('p12','f10'), 2: ('c',), 3: ('p13',), 4: ('f11','p20'), 5: ('oz22','os22'), 6: ('p21',), 7: ('oz23','os23','f12')}
AFTER_NORM = ('f13',)
TURN = {}
UP = {0:('p22','f20'),1:('p23','f21',),2:('f22',),3:('f23',)}
AFTER_GRAD_DOWN = ()
DOWN = {0: ("e20",), 1: ("e21",), 2: ("e22",), 3: ("e23",)}
UP_BACK = {}
AFTER_NORM_BACK = ("l20", "l21", "l22", "l23")
ATTEND_BACK = {
    0: ("e10", "e11"), 1: ("e12", "e13", "r20", "r21"), 3: ("l10", "l11"), 5: ("l12", "l13", "r10", "r11", "e00"),
    7: ("t2", "e01"),
}
AFTER_ROWS = ("e02", "e03", "t1")
LAST = ("l00", "l01")
END = ("l02", "r00", "r01", "l03")


def block(i):
    return pl.ds(pl.multiple_of(i * BLOCK, BLOCK), BLOCK)


def loop(count, step):
    def body(i, _):
        step(i)
        return 0

    lax.fori_loop(0, count, body, 0)


def layer_kernel(
    x_in, ct_in, seg_ref, wq_ref, wk_ref, wv_ref, wo_ref, wup_ref, wdown_ref, ga_ref, gf_ref,
    outs_ref, dxs_ref, q_ref, k_ref, v_ref, o_ref, up_ref, down_ref, gain_a_ref, gain_f_ref,
    gain_own, gain_all, weights, x_ref, ct_ref, out_ref,
    nrm, na_t, nf_t, ct_t, qb, kb, vb, cb, lse_ref, bias, mid, acc, act, gp,
    staged, sums, from_core, corner, from_plane, from_z, small, small_z, gain_sum, gain_parts, gain_own_sum,
    local_sem, zs, zr, xs, xr, ys, yr, ds, dr, cs, cr, gs, gr, as_, ar,
    ecs, ecr, eks, ekr, eps, epr, ezs, ezr, egs, egr, egzs, egzr,
):
    dp, z, c, nx, ny, nc = place()
    yx, yx_x, yx_y, yx_d = dp // 2, nx // 2, ny // 2, 3 - dp // 2

    barrier = pltpu.get_barrier_semaphore()
    for i in range(1, 8):
        pl.semaphore_signal(barrier, inc=1, device_id=(lax.rem(dp + i, 8), z), device_id_type=MESH)
    for i in range(1, 4):
        pl.semaphore_signal(barrier, inc=1, device_id=(dp, lax.rem(z + i, 4)), device_id_type=MESH)

    weights[0, z, dp] = jnp.concatenate(
        [wq_ref[...], wv_ref[...], wk_ref[...], wo_ref[...].T], axis=1
    )
    weights[1, z, dp] = wup_ref[...]
    weights[2, z, dp] = wdown_ref[...]
    gain_own[...] = jnp.zeros_like(gain_own)
    gain_own[0:1, 0:96] = ga_ref[...]
    gain_own[1:2, 0:96] = gf_ref[...]
    pl.semaphore_wait(barrier, 10)

    def rows_start(i, src, dst):
        for j in range(1, 4):
            q = lax.rem(z + j, 4)
            send(src.at[q], dst.at[z], as_.at[i, q], ar.at[i, z], (dp, q)).start()
        pltpu.make_async_copy(src.at[z], dst.at[z], local_sem.at[i]).start()

    def rows_wait(i, src, dst):
        for j in range(1, 4):
            q = lax.rem(z + j, 4)
            cp = send(src.at[q], dst.at[q], as_.at[i, q], ar.at[i, q], (dp, q))
            cp.wait_send()
            cp.wait_recv()
        pltpu.make_async_copy(src.at[z], dst.at[z], local_sem.at[i]).wait()

    def tile(g, q, d):
        return weights.at[g, q, d]

    mate = z + 1 - 2 * lax.rem(z, 2)
    far_inner = 2 - z // 2
    outer = (z == 0) | (z == 3)
    other_side = 2 * (1 - z // 2)

    def z_copy(g, q, side, to):
        return send(tile(g, q, dp), tile(g, q, dp), zs.at[g, q, side], zr.at[g, q], (dp, to))

    def passes_on(q):
        return jnp.logical_not(outer) & (q // 2 != z // 2)

    def own_z(g):
        z_copy(g, z, 0, mate).start()
        z_copy(g, z, 1, far_inner).start()

    def z_done(g, q):
        @pl.when(q == z)
        def _():
            z_copy(g, q, 0, mate).wait_send()
            z_copy(g, q, 1, far_inner).wait_send()

        @pl.when(passes_on(q))
        def _():
            z_copy(g, q, 0, mate).wait_send()

    def x_copy(g, q):
        return send(tile(g, q, dp), tile(g, q, dp), xs.at[g, q], xr.at[g, q], (nx, z))

    def y_copy(g, q):
        return send(tile(g, q, dp), tile(g, q, dp), ys.at[g, q], yr.at[g, q], (ny, z))

    def core_copy(g, q, pos):
        d = 2 * pos + c
        return send(tile(g, q, d), tile(g, q, d), cs.at[g, q, pos], cr.at[g, q, pos], (nc, z))

    def forward(g, q, along_y):
        src, to = (nx, ny) if along_y else (ny, nx)
        return send(tile(g, q, src), tile(g, q, src), ds.at[g, q], dr.at[g, q], (to, z))

    def own_plane(g):
        x_copy(g, z).start()
        y_copy(g, z).start()
        core_copy(g, z, yx).start()

    def z_step(g, k):
        q = nearest(z, k)
        z_copy(g, q, 0, mate).wait_recv()

        @pl.when(passes_on(q))
        def _():
            z_copy(g, q, 0, mate).start()

    def spread_step(g, k):
        q = nearest(z, k)
        x_copy(g, q).start()
        y_copy(g, q).start()
        core_copy(g, q, yx).start()

    def plane_step(g, k):
        q = nearest(z, k)
        x_copy(g, q).wait_recv()

        @pl.when(lax.rem(q, 2) == 0)
        def _():
            forward(g, q, True).start()

        core_copy(g, q, yx_x).start()
        y_copy(g, q).wait_recv()

        @pl.when(lax.rem(q, 2) == 1)
        def _():
            forward(g, q, False).start()

        core_copy(g, q, yx_y).start()

    def far_step(g, k):
        q = nearest(z, k)
        d = 2 * yx_d + c
        send(tile(g, q, d), tile(g, q, d), ds.at[g, q], dr.at[g, q], (nx, z)).wait_recv()
        core_copy(g, q, yx_d).start()

    def core_ready(g, q):
        for pos in range(4):
            d = 2 * pos + 1 - c
            send(
                tile(g, q, d), tile(g, q, d), cs.at[g, q, pos], cr.at[g, q, pos], (nc, z)
            ).wait_recv()

    def weights_sent(g):
        def step(q):
            z_done(g, q)
            x_copy(g, q).wait_send()
            y_copy(g, q).wait_send()

            @pl.when(lax.rem(q, 2) == 0)
            def _():
                forward(g, q, True).wait_send()

            @pl.when(lax.rem(q, 2) == 1)
            def _():
                forward(g, q, False).wait_send()

            for pos in range(4):
                core_copy(g, q, pos).wait_send()

        loop(4, step)

    def out_core(g, q):
        return send(staged.at[q], from_core.at[q], ecs.at[g, q], ecr.at[g, q], (nc, z))

    def out_corner(g, q):
        to = nx + (ny - nx) * lax.rem(q, 2)
        return send(sums.at[g, q, yx_d], corner.at[g, q], eks.at[g, q], ekr.at[g, q], (to, z))

    def out_plane(g, q, side):
        to = nx + (ny - nx) * side
        pos = yx_x + (yx_y - yx_x) * side
        return send(
            sums.at[g, q, pos], from_plane.at[g, q, side], eps.at[g, q, side], epr.at[g, q, side], (to, z)
        )

    def out_z(g, q, slot, to):
        return send(sums.at[g, q, yx], from_z.at[g, slot], ezs.at[g, q], ezr.at[g, slot], (dp, to))

    def in_z(g, slot):
        return send(sums.at[g, 0, yx], from_z.at[g, slot], ezs.at[g, 0], ezr.at[g, slot], (dp, mate))

    def corner_add(g, q):
        side = 1 - lax.rem(q, 2)
        pos = yx_x + (yx_y - yx_x) * side
        out_corner(g, q).wait_recv()
        sums[g, q, pos] = (sums[g, q, pos].astype(F32) + corner[g, q].astype(F32)).astype(BF)
        out_plane(g, q, side).start()

    def plane_add(g, q):
        out_plane(g, q, 0).wait_recv()
        out_plane(g, q, 1).wait_recv()
        sums[g, q, yx] = (
            sums[g, q, yx].astype(F32)
            + from_plane[g, q, 0].astype(F32)
            + from_plane[g, q, 1].astype(F32)
        ).astype(BF)

        @pl.when(q == mate)
        def _():
            out_z(g, q, 0, mate).start()

        @pl.when(outer & (q // 2 != z // 2))
        def _():
            out_z(g, q, 2 + lax.rem(q, 2), mate).start()

    def relay(g, k):
        q = quarter(k)

        @pl.when(jnp.logical_not(outer))
        def _():
            slot = 2 + lax.rem(q, 2)
            in_z(g, slot).wait_recv()
            sums[g, q, yx] = (sums[g, q, yx].astype(F32) + from_z[g, slot].astype(F32)).astype(BF)
            out_z(g, q, 1, q).start()

    def last_add(g):
        in_z(g, 0).wait_recv()
        in_z(g, 1).wait_recv()
        total = sums[g, z, yx].astype(F32) + from_z[g, 0].astype(F32) + from_z[g, 1].astype(F32)
        if g == 0:
            q_ref[...] = total[:, 0:192]
            v_ref[...] = total[:, 192:384]
            k_ref[...] = total[:, 384:576]
            o_ref[...] = total[:, 576:768].T
        else:
            (up_ref if g == 1 else down_ref)[...] = total

    def grads_sent(g):
        def step(q):
            out_corner(g, q).wait_send()
            out_plane(g, q, 0).wait_send()
            out_plane(g, q, 1).wait_send()

            @pl.when(z != q)
            def _():
                out_z(g, q, 0, mate).wait_send()

        loop(4, step)

    def quarter(k):
        return nearest(z, 3 - k)

    def grad_rows(half, left, right, more):
        v = natural(left[:, half].reshape(384, LEN), right)
        if more is None:
            return ((0, v),)
        v2 = natural(more[0][:, half].reshape(384, LEN), more[1])
        return ((0, v[:, 0:512]), (512, v[:, 512:640] + v2[:, 0:128]), (640, v2[:, 128:256]))

    def emit_other(g, q, left, right, more=None):
        if g < 2:
            out_core(g + 1, q).wait_send()
        for first, v in grad_rows(1 - c, left, right, more):
            staged[q, :, :, first : first + v.shape[1]] = v.astype(BF).reshape(4, 96, v.shape[1])
        out_core(g, q).start()

    def emit_own(g, k, left, right, more=None):
        q = quarter(k)
        pieces = grad_rows(c, left, right, more)
        out_core(g, q).wait_recv()
        for first, v in pieces:
            lanes = slice(first, first + v.shape[1])
            theirs = from_core[q, :, :, lanes].astype(F32)
            sums[g, q, :, :, lanes] = (v.reshape(4, 96, v.shape[1]) + theirs).astype(BF)
        out_corner(g, q).start()

        @pl.when(k >= 1)
        def _():
            before = quarter(k - 1)
            out_plane(g, before, lax.rem(before, 2)).start()

        @pl.when(k == 3)
        def _():
            out_plane(g, q, lax.rem(q, 2)).start()

    def put_t(dst, i, v):
        dst[:, :, :, block(i)] = v.T.reshape(4, 2, 96, BLOCK)

    def add(i, value):
        @pl.when(i == 0)
        def _():
            acc[...] = value

        @pl.when(i > 0)
        def _():
            acc[...] += value

    steps = {
        "a": own_z, "b": own_plane, "z": z_step, "s": spread_step, "p": plane_step, "f": far_step,
        "x": lambda: rows_start(0, x_in, x_ref), "c": lambda: rows_start(1, ct_in, ct_ref),
        "e": lambda g, k: corner_add(g, quarter(k)), "l": lambda g, k: plane_add(g, quarter(k)), "r": relay, "t": last_add,
    }

    def take(names):
        for name in names:
            act_on = functools.partial(steps[name.lstrip("io")[0]], *map(int, name.lstrip("io")[1:]))
            if name[0] in "io":
                pl.when(outer if name[0] == "o" else jnp.logical_not(outer))(act_on)
            else:
                act_on()

    def serve(now, table):
        for due, names in table.items():
            pl.when(now == due)(functools.partial(take, names))

    own_z(0)
    own_plane(0)
    for i in range(1, 8):
        to = lax.rem(dp + i, 8)
        send(gain_own, gain_all.at[dp], gs.at[to], gr.at[dp], (to, z)).start()
    gain_all[dp] = gain_own[...]
    take(FIRST)
    seg_row = seg_ref[pl.ds(z, 1)].astype(F32)
    seg_col = jnp.broadcast_to(seg_row, (8, LEN)).T[:, 0:1]
    bias[...] = jnp.where(seg_col == seg_row, 0.0, -1e30)
    gain_sum[...] = jnp.zeros_like(gain_sum)
    gain_parts[...] = jnp.zeros_like(gain_parts)
    take(SECOND)
    for i in range(1, 8):
        other = lax.rem(dp + i, 8)
        send(gain_own, gain_all.at[other], gs.at[other], gr.at[other], (other, z)).wait_recv()
    gain_a = gain_row(gain_all, 0)
    gain_f = gain_row(gain_all, 1)
    take(THIRD)
    rows_wait(0, x_in, x_ref)

    def norm_a(i):
        xhat, _ = norm(x_ref[i].astype(F32))
        normed = (xhat * gain_a).astype(BF)
        nrm[block(i)] = normed
        put_t(na_t, i, normed)

    loop(4, norm_a)

    def attend(i):
        q = nearest(z, i)
        core_ready(0, q)
        w = weights[0, q].reshape(D, D)
        p = natural(nrm[...], w[:, 0:640])
        q8 = p[:, 0:256].astype(BF) * jnp.asarray(0.125, BF)
        v = p[:, 128:384].astype(BF)
        k = p[:, 384:640].astype(BF)
        qb[q] = q8
        vb[q] = v
        kb[q] = k
        for r in range(2):
            rs = slice(256 * r, 256 * (r + 1))
            ctx = jnp.zeros((256, 256), F32)
            lane = lax.broadcasted_iota(jnp.int32, (256, 128), 1)
            lse = lse_ref[rs]
            for h in range(3):
                s = against(between(q8[rs], 64 * h, 64), k) + bias[rs]
                m = jnp.max(s, axis=1, keepdims=True)
                e = jnp.exp(s - m)
                total = jnp.sum(e, axis=1, keepdims=True)
                ctx += natural(e.astype(BF), between(v, 64 + 64 * h, 64)) * (1.0 / total)
                lse = jnp.where(lane == 3 * q + h, m + jnp.log(total), lse)
            lse_ref[rs] = lse
            cb[q, rs] = ctx.astype(BF)
            serve(2 * i + r, ATTEND)

    loop(4, attend)

    def attend_out(i):
        add(i, against(cb[i], weights[0, i].reshape(D, D)[:, 512:768]))

    loop(4, attend_out)

    def norm_f(i):
        m = x_ref[i].astype(F32) + acc[block(i)]
        mid[block(i)] = m
        xhat, _ = norm(m)
        normed = (xhat * gain_f).astype(BF)
        nrm[block(i)] = normed
        put_t(nf_t, i, normed)

    loop(4, norm_f)
    take(AFTER_NORM)
    rows_wait(1, ct_in, ct_ref)

    def turn_ct(i):
        put_t(ct_t, i, ct_ref[i])
        serve(i, TURN)

    loop(4, turn_ct)

    def up(i):
        q = quarter(i)
        core_ready(1, q)
        w = weights[1, q].reshape(D, D)
        for r in range(2):
            rs = slice(256 * r, 256 * (r + 1))
            h = natural(nrm[rs], w)
            cdf = 0.5 + 0.5 * lax.erf(h * 0.7071067811865476)
            act[q, rs] = (h * cdf).astype(BF)
            gp[q, rs] = (cdf + h * (jnp.exp(-0.5 * h * h) * 0.3989422804014327)).astype(BF)
        emit_other(2, q, ct_t, act[q])

        @pl.when(i > 0)
        def _():
            emit_own(2, i - 1, ct_t, act[quarter(i - 1)])

        serve(i, UP)

    loop(4, up)
    emit_own(2, 3, ct_t, act[quarter(3)])
    take(AFTER_GRAD_DOWN)

    def down(i):
        q = nearest(z, i)
        core_ready(2, q)
        w = weights[2, q].reshape(D, D)
        gp[q] = (natural(ct_ref[...].reshape(LEN, D), w) * gp[q].astype(F32)).astype(BF)
        add(i, against(act[q], w))
        serve(i, DOWN)

    loop(4, down)
    out_ref[...] = (mid[...] + acc[...]).astype(BF).reshape(4, BLOCK, D)
    rows_start(2, out_ref, outs_ref)

    def up_back(i):
        q = quarter(i)
        emit_other(1, q, nf_t, gp[q])
        add(i, against(gp[q], weights[1, q].reshape(D, D)))
        emit_own(1, i, nf_t, gp[q])

        serve(i, UP_BACK)

    loop(4, up_back)

    def norm_f_back(i):
        xhat, scale = norm(mid[block(i)])
        back, grad_gain = norm_back(acc[block(i)], xhat, scale, gain_f)
        gain_sum[1:2] += grad_gain[None]
        grad_middle = ct_ref[i].astype(F32) + back
        mid[block(i)] = grad_middle
        attended = grad_middle.astype(BF)
        nrm[block(i)] = attended
        put_t(ct_t, i, attended)

    loop(4, norm_f_back)
    take(AFTER_NORM_BACK)

    def attend_back(i):
        q = quarter(i)
        w = weights[0, q].reshape(D, D)
        dctx = between(natural(nrm[...], w[:, 512:768]), 64, 192).astype(BF)
        q8, v, k, cx = qb[q], vb[q], kb[q], cb[q]
        dq = jnp.zeros((LEN, 256), F32)
        dk = jnp.zeros((LEN, 256), F32)
        dv = jnp.zeros((LEN, 256), F32)
        for h in range(3):
            lane = lax.broadcasted_iota(jnp.int32, (LEN, 128), 1)
            lse = jnp.sum(jnp.where(lane == 3 * q + h, lse_ref[...], 0.0), axis=1, keepdims=True)
            p = jnp.exp(against(between(q8, 64 * h, 64), k) + bias[...] - lse)
            dm = between(dctx, 64 + 64 * h, 64)
            delta = jnp.sum(dm.astype(F32) * cx.astype(F32), axis=1, keepdims=True)
            ds_ = (p * (against(dm, v) - delta)).astype(BF)
            dq += between(natural(ds_, k), 64 * h, 64)
            dk += between(inner(ds_, q8), 64 * h, 64)
            dv += between(inner(p.astype(BF), dctx), 64 + 64 * h, 64)
        dq = dq * 0.125
        d = jnp.concatenate(
            [dq[:, 0:128], dq[:, 128:256] + dv[:, 0:128], dv[:, 128:256], dk], axis=1
        ).astype(BF)

        serve(2 * i, ATTEND_BACK)
        emit_other(0, q, na_t, d, (ct_t, cx))
        add(i, against(d, w[:, 0:640]))
        emit_own(0, i, na_t, d, (ct_t, cx))
        serve(2 * i + 1, ATTEND_BACK)

    loop(4, attend_back)

    def norm_a_back(i):
        xhat, scale = norm(x_ref[i].astype(F32))
        back, grad_gain = norm_back(acc[block(i)], xhat, scale, gain_a)
        gain_sum[0:1] += grad_gain[None]
        ct_ref[i] = (mid[block(i)] + back).astype(BF)

    loop(4, norm_a_back)
    rows_start(3, ct_ref, dxs_ref)
    for i in range(2):
        for p in range(8):
            gain_parts[p, i : i + 1, 0:96] = gain_sum[i : i + 1, 96 * p : 96 * (p + 1)]

    def small_copy(i):
        to = lax.rem(dp + i, 8)
        return send(gain_parts.at[to], small.at[dp], egs.at[to], egr.at[dp], (to, z))

    def small_in(i):
        other = lax.rem(dp + i, 8)
        return send(gain_parts.at[other], small.at[other], egs.at[other], egr.at[other], (other, z))

    for i in range(1, 8):
        small_copy(i).start()
    take(AFTER_ROWS)
    take(LAST)
    total = gain_parts[dp]
    for i in range(1, 8):
        small_in(i).wait_recv()
        total = total + small[lax.rem(dp + i, 8)]
    gain_own_sum[...] = total
    for j in range(1, 4):
        q = lax.rem(z + j, 4)
        send(gain_own_sum, small_z.at[z], egzs.at[q], egzr.at[z], (dp, q)).start()
    take(END)
    for i in range(1, 8):
        other = lax.rem(dp + i, 8)
        send(gain_own, gain_all.at[other], gs.at[other], gr.at[other], (other, z)).wait_send()
        small_copy(i).wait_send()
    for g in range(3):
        weights_sent(g)
    grads_sent(2)
    grads_sent(1)
    loop(4, lambda q: out_core(0, q).wait_send())
    rows_wait(2, out_ref, outs_ref)
    total = gain_own_sum[...]
    for j in range(1, 4):
        q = lax.rem(z + j, 4)
        cp = send(gain_own_sum, small_z.at[q], egzs.at[q], egzr.at[q], (dp, q))
        cp.wait()
        total = total + small_z[q]
    gain_a_ref[...] = total[0:1, 0:96]
    gain_f_ref[...] = total[1:2, 0:96]
    rows_wait(3, ct_ref, dxs_ref)
    last_add(0)
    grads_sent(0)


def layer(x, ct, segment_ids, w_query, w_key, w_value, w_output, w_up, w_down, gain_attn, gain_ffn):
    sem = pltpu.SemaphoreType.DMA
    vm = pltpu.VMEM
    anywhere = pl.BlockSpec(memory_space=pl.ANY)
    vmem = pl.BlockSpec(memory_space=pltpu.VMEM)
    return pl.pallas_call(
        layer_kernel,
        out_shape=(
            jax.ShapeDtypeStruct(x.shape, BF),
            jax.ShapeDtypeStruct(x.shape, BF),
            *(jax.ShapeDtypeStruct(n, F32) for n in [(96, 192)] * 3 + [(192, 96)] + [(96, D)] * 2 + [(1, 96)] * 2),
        ),
        in_specs=[anywhere] * 2 + [vmem] * 9,
        out_specs=[anywhere] * 2 + [vmem] * 8,
        scratch_shapes=[
            vm((16, 128), BF), vm((8, 16, 128), BF),
            vm((3, 4, 8, 96, D), BF),
            vm((4, BLOCK, D), BF), vm((4, BLOCK, D), BF), vm((4, BLOCK, D), BF),
            vm((LEN, D), BF),
            vm((4, 2, 96, LEN), BF), vm((4, 2, 96, LEN), BF), vm((4, 2, 96, LEN), BF),
            vm((4, LEN, 256), BF), vm((4, LEN, 256), BF), vm((4, LEN, 256), BF), vm((4, LEN, 256), BF),
            vm((LEN, 128), F32), vm((LEN, LEN), F32), vm((LEN, D), F32), vm((LEN, D), F32),
            vm((4, LEN, D), BF), vm((4, LEN, D), BF),
            vm((4, 4, 96, D), BF), vm((3, 4, 4, 96, D), BF), vm((4, 4, 96, D), BF),
            vm((3, 4, 96, D), BF), vm((3, 4, 2, 96, D), BF), vm((3, 4, 96, D), BF),
            vm((8, 8, 128), F32), vm((4, 8, 128), F32), vm((8, D), F32), vm((8, 8, 128), F32), vm((8, 128), F32),
            sem((4,)),
            sem((3, 4, 2)), sem((3, 4)),
            sem((3, 4)), sem((3, 4)),
            sem((3, 4)), sem((3, 4)),
            sem((3, 4)), sem((3, 4)),
            sem((3, 4, 4)), sem((3, 4, 4)),
            sem((8,)), sem((8,)),
            sem((4, 4)), sem((4, 4)),
            sem((3, 4)), sem((3, 4)),
            sem((3, 4)), sem((3, 4)),
            sem((3, 4, 2)), sem((3, 4, 2)),
            sem((3, 4)), sem((3, 4)),
            sem((8,)), sem((8,)),
            sem((4,)), sem((4,)),
        ],
        compiler_params=pltpu.CompilerParams(
            collective_id=0, has_side_effects=True, vmem_limit_bytes=VMEM_LIMIT
        ),
        name="layer_with_copies",
    )(x, ct, segment_ids, w_query, w_key, w_value, w_output, w_up, w_down, gain_attn, gain_ffn)


VMEM_LIMIT = 62 * 2**20


def part_kernel(*refs):
    count = (len(refs) - 2) // 3
    sources, targets, held, (arrive, leave) = (
        refs[:count], refs[count : 2 * count], refs[2 * count : 3 * count], refs[3 * count :]
    )
    coming = [pltpu.make_async_copy(sources[i], held[i], arrive.at[i]) for i in range(count)]
    going = [pltpu.make_async_copy(held[i], targets[i], leave.at[i]) for i in range(count)]
    for copy in coming:
        copy.start()
    for copy_in, copy_out in zip(coming, going):
        copy_in.wait()
        copy_out.start()
    for copy in going:
        copy.wait()


def part(*results):
    anywhere = pl.BlockSpec(memory_space=pl.ANY)
    return pl.pallas_call(
        part_kernel,
        out_shape=[jax.ShapeDtypeStruct(r.shape, r.dtype) for r in results],
        in_specs=[anywhere] * len(results),
        out_specs=[anywhere] * len(results),
        scratch_shapes=[pltpu.VMEM(r.shape, r.dtype) for r in results]
        + [pltpu.SemaphoreType.DMA((len(results),))] * 2,
        name="part_outputs",
    )(*results)


def shards(
    inputs, segment_ids, w_query, w_key, w_value, w_output, w_up, w_down, gain_attn, gain_ffn, cotangent,
    *, parts, quarters,
):
    depth, width = w_query.shape
    if parts == 8 and quarters == 4:
        results = layer(
            inputs, cotangent, segment_ids, w_query, w_key, w_value, w_output, w_up, w_down.T,
            gain_attn.reshape(1, depth), gain_ffn.reshape(1, depth),
        )
        *outs, grad_down, grad_gain_attn, grad_gain_ffn = part(*results)
        return (*outs, grad_down.T, grad_gain_attn.reshape(depth), grad_gain_ffn.reshape(depth))
    else:
        z = lax.axis_index("mp")
        segment = lax.dynamic_index_in_dim(segment_ids, z, 0, keepdims=False)
        own = jnp.stack(
            [jnp.concatenate([w_query, w_value, w_key, w_output.T], axis=1), w_up, w_down.T]
        )
        weights = lax.all_gather(own, ("dp", "mp"), axis=0).reshape(parts, quarters, 3, depth, D)
        weights = weights.transpose(2, 1, 0, 3, 4).reshape(3, quarters, D, D)
        gains = jnp.stack(
            [lax.all_gather(g, "dp", axis=0, tiled=True) for g in (gain_attn, gain_ffn)]
        ).astype(F32)
        x, ct = (
            lax.all_to_all(a, "mp", split_axis=0, concat_axis=0, tiled=True) for a in (inputs, cotangent)
        )
        out, dx, grads, gg = row_layer(
            x.reshape(-1, D), ct.reshape(-1, D), segment, weights, gains[0], gains[1]
        )
        grads = grads.reshape(3, quarters, parts, depth, D).transpose(2, 1, 0, 3, 4)
        grads = grads.reshape(parts * quarters, 3, depth, D)
        total = lax.psum_scatter(grads, ("dp", "mp"), scatter_dimension=0).astype(F32)
        gg = lax.psum(lax.psum_scatter(gg, "dp", scatter_dimension=1, tiled=True), "mp")
        out, dx = (
            lax.all_to_all(a.reshape(inputs.shape), "mp", split_axis=0, concat_axis=0, tiled=True)
            for a in (out, dx)
        )
    return (
        out,
        dx,
        total[0, :, :width],
        total[0, :, 2 * width : 3 * width],
        total[0, :, width : 2 * width],
        total[0, :, 3 * width :].T,
        total[1],
        total[2].T,
        gg[0],
        gg[1],
    )


def solution(mesh):
    by_row = P("dp", "mp", None)
    grids = (P("dp", "mp"), P("dp", "mp"), P("dp", "mp"), P("mp", "dp"), P("dp", "mp"), P("mp", "dp"))
    gains = (P("dp"), P("dp"))
    return jax.shard_map(
        functools.partial(shards, parts=mesh.shape["dp"], quarters=mesh.shape["mp"]),
        mesh=mesh,
        in_specs=(by_row, P("dp", None)) + grids + gains + (by_row,),
        out_specs=(by_row, by_row) + grids + gains,
        check_vma=False,
    )
```

```python
import functools

import jax
import jax.numpy as jnp
from jax import lax
from jax.experimental import pallas as pl
from jax.experimental.pallas import tpu as pltpu
from jax.sharding import PartitionSpec as P

D = 768
HEADS = 12
HEAD = 64
EPS = 1e-05
MESH = pl.DeviceIdType.MESH
BF = jnp.bfloat16
F32 = jnp.float32


def dot(left, right, dims):
    return lax.dot_general(left, right, (dims, ((), ())), preferred_element_type=F32)


def natural(left, right):
    return dot(left, right, ((1,), (0,)))


def against(left, right):
    return dot(left, right, ((1,), (1,)))


def inner(left, right):
    return dot(left, right, ((0,), (0,)))


def norm(values):
    shifted = values - jnp.mean(values, axis=1, keepdims=True)
    scale = lax.rsqrt(jnp.mean(shifted * shifted, axis=1, keepdims=True) + EPS)
    return shifted * scale, scale


def norm_back(grad, xhat, scale, gain):
    e = grad * gain
    back = scale * (
        e - jnp.mean(e, axis=1, keepdims=True) - xhat * jnp.mean(e * xhat, axis=1, keepdims=True)
    )
    return back, jnp.sum(grad * xhat, axis=0)


def columns(w, first, count):
    part = w[:, :, first : first + count]
    return jnp.swapaxes(part, 0, 1).reshape(D, -1)


def row_layer(x, cotangent, segment, weights, gain_attn, gain_ffn):
    length = x.shape[0]
    quarters = weights.shape[1]
    width = D // quarters
    attn, up, down = weights[0], weights[1], weights[2]
    w_query, w_value, w_key, w_out = (columns(attn, i * width, width) for i in range(4))
    w_up, w_down = columns(up, 0, D), columns(down, 0, D)
    x = x.astype(F32)
    xhat_a, scale_a = norm(x)
    normed_a = (xhat_a * gain_attn).astype(BF)
    query, keys, values = (
        natural(normed_a, w).astype(BF).reshape(length, HEADS, HEAD) for w in (w_query, w_key, w_value)
    )
    same = segment[:, None] == segment[None, :]
    scores = jnp.einsum("qhd,khd->hqk", query, keys, preferred_element_type=F32) * HEAD**-0.5
    scores = jnp.where(same[None], scores, -1e30)
    exponent = jnp.exp(scores - jnp.max(scores, axis=2, keepdims=True))
    probs = exponent / jnp.sum(exponent, axis=2, keepdims=True)
    context = jnp.einsum("hqk,khd->qhd", probs.astype(BF), values, preferred_element_type=F32)
    context = context.reshape(length, D).astype(BF)
    middle = x + against(context, w_out)
    xhat_f, scale_f = norm(middle)
    normed_f = (xhat_f * gain_ffn).astype(BF)
    hidden = natural(normed_f, w_up)
    activated, gelu_back = jax.vjp(lambda v: jax.nn.gelu(v, approximate=False), hidden)
    activated = activated.astype(BF)
    output = (middle + against(activated, w_down)).astype(BF)

    grad_down = inner(cotangent, activated)
    grad_hidden = gelu_back(natural(cotangent, w_down))[0].astype(BF)
    grad_up = inner(normed_f, grad_hidden)
    back, grad_gain_ffn = norm_back(against(grad_hidden, w_up), xhat_f, scale_f, gain_ffn)
    grad_middle = cotangent.astype(F32) + back
    grad_attended = grad_middle.astype(BF)
    grad_out = inner(grad_attended, context)
    grad_context = natural(grad_attended, w_out).astype(BF).reshape(length, HEADS, HEAD)
    grad_probs = jnp.einsum("qhd,khd->hqk", grad_context, values, preferred_element_type=F32)
    grad_scores = (
        probs * (grad_probs - jnp.sum(probs * grad_probs, axis=2, keepdims=True))
    ).astype(BF)
    query_grad = jnp.einsum("hqk,khd->qhd", grad_scores, keys, preferred_element_type=F32) * HEAD**-0.5
    key_grad = jnp.einsum("hqk,qhd->khd", grad_scores, query, preferred_element_type=F32) * HEAD**-0.5
    value_grad = jnp.einsum(
        "hqk,qhd->khd", probs.astype(BF), grad_context, preferred_element_type=F32
    )
    query_grad, key_grad, value_grad = (
        g.reshape(length, D).astype(BF) for g in (query_grad, key_grad, value_grad)
    )
    grad_normed_a = (
        against(query_grad, w_query) + against(key_grad, w_key) + against(value_grad, w_value)
    )
    back, grad_gain_attn = norm_back(grad_normed_a, xhat_a, scale_a, gain_attn)
    input_grad = (grad_middle + back).astype(BF)

    def quarter(g, count):
        return g.astype(BF).reshape(D, quarters, count).swapaxes(0, 1)

    grads_attn = jnp.concatenate(
        [
            quarter(g, width)
            for g in (
                inner(normed_a, query_grad),
                inner(normed_a, value_grad),
                inner(normed_a, key_grad),
                grad_out,
            )
        ],
        axis=2,
    )
    grads = jnp.stack([grads_attn, quarter(grad_up, D), quarter(grad_down, D)])
    return output, input_grad, grads, jnp.stack([grad_gain_attn, grad_gain_ffn])


def between(value, first, count):
    lane = lax.broadcasted_iota(jnp.int32, value.shape, 1)
    return jnp.where((lane >= first) & (lane < first + count), value, jnp.zeros_like(value))


def place():
    dp, z = lax.axis_index("dp"), lax.axis_index("mp")
    c, x, y = lax.rem(dp, 2), lax.rem(dp // 2, 2), dp // 4
    return dp, z, c, dp + 2 - 4 * x, dp + 4 - 8 * y, dp + 1 - 2 * c


def send(src, dst, ssem, rsem, device):
    return pltpu.make_async_remote_copy(
        src_ref=src, dst_ref=dst, send_sem=ssem, recv_sem=rsem, device_id=device, device_id_type=MESH
    )


def nearest(z, k):
    inner_place = lax.rem((z + 1) // 2, 2)
    first_two = 1 - k // 2
    base = k + inner_place * first_two * (1 - 2 * k)
    return base + (z // 2) * (3 - 2 * base)


def gain_row(parts_ref, index):
    r = lax.broadcasted_iota(jnp.int32, (128, D), 0)
    col = lax.broadcasted_iota(jnp.int32, (128, D), 1)
    spread = jnp.where(lax.rem(col, 96) == r, 1.0, 0.0).astype(BF)
    total = jnp.zeros((1, D), F32)
    col = lax.broadcasted_iota(jnp.int32, (16, D), 1)
    row = lax.broadcasted_iota(jnp.int32, (16, D), 0)
    for p in range(8):
        full = natural(parts_ref[p], spread)
        keep = (row == index) & (col >= 96 * p) & (col < 96 * (p + 1))
        total = total + jnp.sum(jnp.where(keep, full, 0.0), axis=0, keepdims=True)
    return total


BLOCK = 128
LEN = 512

FIRST = ("b1", "a1", "z01", "s01", "z02", "s02", "z03", "s03", "x")
SECOND = (
    "p00", "p10", "p01", "iz11", "is11", "f00", "p02", "iz12", "is12", "p03", "f01", "iz13", "is13", "a2",
    "oz11", "os11", "f02", "oz12", "os12", "oz13", "os13", "b2", "f03",
)
THIRD = ()
ATTEND = {0: ('p11','z21','s21','iz22','is22','iz23','is23'), 1: ('p12','f10'), 2: ('c',), 3: ('p13',), 4: ('f11','p20'), 5: ('oz22','os22'), 6: ('p21',), 7: ('oz23','os23','f12')}
AFTER_NORM = ('f13',)
TURN = {}
UP = {0:('p22','f20'),1:('p23','f21',),2:('f22',),3:('f23',)}
AFTER_GRAD_DOWN = ()
DOWN = {0: ("e20",), 1: ("e21",), 2: ("e22",), 3: ("e23",)}
UP_BACK = {}
AFTER_NORM_BACK = ("l20", "l21", "l22", "l23")
ATTEND_BACK = {
    0: ("e10", "e11"), 1: ("e12", "e13", "r20", "r21"), 3: ("l10", "l11"), 5: ("l12", "l13", "r10", "r11", "e00"),
    7: ("t2", "e01"),
}
AFTER_ROWS = ('e02','l00','e03','t1')
LAST = ('l01',)
END = ("l02", "r00", "r01", "l03")


def block(i):
    return pl.ds(pl.multiple_of(i * BLOCK, BLOCK), BLOCK)


def loop(count, step):
    def body(i, _):
        step(i)
        return 0

    lax.fori_loop(0, count, body, 0)


def layer_kernel(
    x_in, ct_in, seg_ref, wq_ref, wk_ref, wv_ref, wo_ref, wup_ref, wdown_ref, ga_ref, gf_ref,
    outs_ref, dxs_ref, q_ref, k_ref, v_ref, o_ref, up_ref, down_ref, gain_a_ref, gain_f_ref,
    gain_own, gain_all, weights, x_ref, ct_ref, out_ref,
    nrm, na_t, nf_t, ct_t, qb, kb, vb, cb, lse_ref, bias, mid, acc, act, gp,
    staged, sums, from_core, corner, from_plane, from_z, small, small_z, gain_sum, gain_parts, gain_own_sum,
    local_sem, zs, zr, xs, xr, ys, yr, ds, dr, cs, cr, gs, gr, as_, ar,
    ecs, ecr, eks, ekr, eps, epr, ezs, ezr, egs, egr, egzs, egzr,
):
    dp, z, c, nx, ny, nc = place()
    yx, yx_x, yx_y, yx_d = dp // 2, nx // 2, ny // 2, 3 - dp // 2

    barrier = pltpu.get_barrier_semaphore()
    for i in range(1, 8):
        pl.semaphore_signal(barrier, inc=1, device_id=(lax.rem(dp + i, 8), z), device_id_type=MESH)
    for i in range(1, 4):
        pl.semaphore_signal(barrier, inc=1, device_id=(dp, lax.rem(z + i, 4)), device_id_type=MESH)

    weights[0, z, dp] = jnp.concatenate(
        [wq_ref[...], wv_ref[...], wk_ref[...], wo_ref[...].T], axis=1
    )
    weights[1, z, dp] = wup_ref[...]
    weights[2, z, dp] = wdown_ref[...]
    gain_own[...] = jnp.zeros_like(gain_own)
    gain_own[0:1, 0:96] = ga_ref[...]
    gain_own[1:2, 0:96] = gf_ref[...]
    pl.semaphore_wait(barrier, 10)

    def rows_start(i, src, dst):
        for j in range(1, 4):
            q = lax.rem(z + j, 4)
            send(src.at[q], dst.at[z], as_.at[i, q], ar.at[i, z], (dp, q)).start()
        pltpu.make_async_copy(src.at[z], dst.at[z], local_sem.at[i]).start()

    def rows_wait(i, src, dst):
        for j in range(1, 4):
            q = lax.rem(z + j, 4)
            cp = send(src.at[q], dst.at[q], as_.at[i, q], ar.at[i, q], (dp, q))
            cp.wait_send()
            cp.wait_recv()
        pltpu.make_async_copy(src.at[z], dst.at[z], local_sem.at[i]).wait()

    def tile(g, q, d):
        return weights.at[g, q, d]

    mate = z + 1 - 2 * lax.rem(z, 2)
    far_inner = 2 - z // 2
    outer = (z == 0) | (z == 3)
    other_side = 2 * (1 - z // 2)

    def z_copy(g, q, side, to):
        return send(tile(g, q, dp), tile(g, q, dp), zs.at[g, q, side], zr.at[g, q], (dp, to))

    def passes_on(q):
        return jnp.logical_not(outer) & (q // 2 != z // 2)

    def own_z(g):
        z_copy(g, z, 0, mate).start()
        z_copy(g, z, 1, far_inner).start()

    def z_done(g, q):
        @pl.when(q == z)
        def _():
            z_copy(g, q, 0, mate).wait_send()
            z_copy(g, q, 1, far_inner).wait_send()

        @pl.when(passes_on(q))
        def _():
            z_copy(g, q, 0, mate).wait_send()

    def x_copy(g, q):
        return send(tile(g, q, dp), tile(g, q, dp), xs.at[g, q], xr.at[g, q], (nx, z))

    def y_copy(g, q):
        return send(tile(g, q, dp), tile(g, q, dp), ys.at[g, q], yr.at[g, q], (ny, z))

    def core_copy(g, q, pos):
        d = 2 * pos + c
        return send(tile(g, q, d), tile(g, q, d), cs.at[g, q, pos], cr.at[g, q, pos], (nc, z))

    def forward(g, q, along_y):
        src, to = (nx, ny) if along_y else (ny, nx)
        return send(tile(g, q, src), tile(g, q, src), ds.at[g, q], dr.at[g, q], (to, z))

    def own_plane(g):
        x_copy(g, z).start()
        y_copy(g, z).start()
        core_copy(g, z, yx).start()

    def z_step(g, k):
        q = nearest(z, k)
        z_copy(g, q, 0, mate).wait_recv()

        @pl.when(passes_on(q))
        def _():
            z_copy(g, q, 0, mate).start()

    def spread_step(g, k):
        q = nearest(z, k)
        x_copy(g, q).start()
        y_copy(g, q).start()
        core_copy(g, q, yx).start()

    def plane_step(g, k):
        q = nearest(z, k)
        x_copy(g, q).wait_recv()

        @pl.when(lax.rem(q, 2) == 0)
        def _():
            forward(g, q, True).start()

        core_copy(g, q, yx_x).start()
        y_copy(g, q).wait_recv()

        @pl.when(lax.rem(q, 2) == 1)
        def _():
            forward(g, q, False).start()

        core_copy(g, q, yx_y).start()

    def far_step(g, k):
        q = nearest(z, k)
        d = 2 * yx_d + c
        send(tile(g, q, d), tile(g, q, d), ds.at[g, q], dr.at[g, q], (nx, z)).wait_recv()
        core_copy(g, q, yx_d).start()

    def core_ready(g, q):
        for pos in range(4):
            d = 2 * pos + 1 - c
            send(
                tile(g, q, d), tile(g, q, d), cs.at[g, q, pos], cr.at[g, q, pos], (nc, z)
            ).wait_recv()

    def weights_sent(g):
        def step(q):
            z_done(g, q)
            x_copy(g, q).wait_send()
            y_copy(g, q).wait_send()

            @pl.when(lax.rem(q, 2) == 0)
            def _():
                forward(g, q, True).wait_send()

            @pl.when(lax.rem(q, 2) == 1)
            def _():
                forward(g, q, False).wait_send()

            for pos in range(4):
                core_copy(g, q, pos).wait_send()

        loop(4, step)

    def out_core(g, q):
        return send(staged.at[q], from_core.at[q], ecs.at[g, q], ecr.at[g, q], (nc, z))

    def out_corner(g, q):
        to = nx + (ny - nx) * lax.rem(q, 2)
        return send(sums.at[g, q, yx_d], corner.at[g, q], eks.at[g, q], ekr.at[g, q], (to, z))

    def out_plane(g, q, side):
        to = nx + (ny - nx) * side
        pos = yx_x + (yx_y - yx_x) * side
        return send(
            sums.at[g, q, pos], from_plane.at[g, q, side], eps.at[g, q, side], epr.at[g, q, side], (to, z)
        )

    def out_z(g, q, slot, to):
        return send(sums.at[g, q, yx], from_z.at[g, slot], ezs.at[g, q], ezr.at[g, slot], (dp, to))

    def in_z(g, slot):
        return send(sums.at[g, 0, yx], from_z.at[g, slot], ezs.at[g, 0], ezr.at[g, slot], (dp, mate))

    def corner_add(g, q):
        side = 1 - lax.rem(q, 2)
        pos = yx_x + (yx_y - yx_x) * side
        out_corner(g, q).wait_recv()
        sums[g, q, pos] = (sums[g, q, pos].astype(F32) + corner[g, q].astype(F32)).astype(BF)
        out_plane(g, q, side).start()

    def plane_add(g, q):
        out_plane(g, q, 0).wait_recv()
        out_plane(g, q, 1).wait_recv()
        sums[g, q, yx] = (
            sums[g, q, yx].astype(F32)
            + from_plane[g, q, 0].astype(F32)
            + from_plane[g, q, 1].astype(F32)
        ).astype(BF)

        @pl.when(q == mate)
        def _():
            out_z(g, q, 0, mate).start()

        @pl.when(outer & (q // 2 != z // 2))
        def _():
            out_z(g, q, 2 + lax.rem(q, 2), mate).start()

    def relay(g, k):
        q = quarter(k)

        @pl.when(jnp.logical_not(outer))
        def _():
            slot = 2 + lax.rem(q, 2)
            in_z(g, slot).wait_recv()
            sums[g, q, yx] = (sums[g, q, yx].astype(F32) + from_z[g, slot].astype(F32)).astype(BF)
            out_z(g, q, 1, q).start()

    def last_add(g):
        in_z(g, 0).wait_recv()
        in_z(g, 1).wait_recv()
        total = sums[g, z, yx].astype(F32) + from_z[g, 0].astype(F32) + from_z[g, 1].astype(F32)
        if g == 0:
            q_ref[...] = total[:, 0:192]
            v_ref[...] = total[:, 192:384]
            k_ref[...] = total[:, 384:576]
            o_ref[...] = total[:, 576:768].T
        else:
            (up_ref if g == 1 else down_ref)[...] = total

    def grads_sent(g):
        def step(q):
            out_corner(g, q).wait_send()
            out_plane(g, q, 0).wait_send()
            out_plane(g, q, 1).wait_send()

            @pl.when(z != q)
            def _():
                out_z(g, q, 0, mate).wait_send()

        loop(4, step)

    def quarter(k):
        return nearest(z, 3 - k)

    def grad_rows(half, left, right, more):
        v = natural(left[:, half].reshape(384, LEN), right)
        if more is None:
            return ((0, v),)
        v2 = natural(more[0][:, half].reshape(384, LEN), more[1])
        return ((0, v[:, 0:512]), (512, v[:, 512:640] + v2[:, 0:128]), (640, v2[:, 128:256]))

    def emit_other(g, q, left, right, more=None):
        if g < 2:
            out_core(g + 1, q).wait_send()
        for first, v in grad_rows(1 - c, left, right, more):
            staged[q, :, :, first : first + v.shape[1]] = v.astype(BF).reshape(4, 96, v.shape[1])
        out_core(g, q).start()

    def emit_own(g, k, left, right, more=None):
        q = quarter(k)
        pieces = grad_rows(c, left, right, more)
        out_core(g, q).wait_recv()
        for first, v in pieces:
            lanes = slice(first, first + v.shape[1])
            theirs = from_core[q, :, :, lanes].astype(F32)
            sums[g, q, :, :, lanes] = (v.reshape(4, 96, v.shape[1]) + theirs).astype(BF)
        out_corner(g, q).start()

        @pl.when(k >= 1)
        def _():
            before = quarter(k - 1)
            out_plane(g, before, lax.rem(before, 2)).start()

        @pl.when(k == 3)
        def _():
            out_plane(g, q, lax.rem(q, 2)).start()

    def put_t(dst, i, v):
        dst[:, :, :, block(i)] = v.T.reshape(4, 2, 96, BLOCK)

    def add(i, value):
        @pl.when(i == 0)
        def _():
            acc[...] = value

        @pl.when(i > 0)
        def _():
            acc[...] += value

    steps = {
        "a": own_z, "b": own_plane, "z": z_step, "s": spread_step, "p": plane_step, "f": far_step,
        "x": lambda: rows_start(0, x_in, x_ref), "c": lambda: rows_start(1, ct_in, ct_ref),
        "e": lambda g, k: corner_add(g, quarter(k)), "l": lambda g, k: plane_add(g, quarter(k)), "r": relay, "t": last_add,
    }

    def take(names):
        for name in names:
            act_on = functools.partial(steps[name.lstrip("io")[0]], *map(int, name.lstrip("io")[1:]))
            if name[0] in "io":
                pl.when(outer if name[0] == "o" else jnp.logical_not(outer))(act_on)
            else:
                act_on()

    def serve(now, table):
        for due, names in table.items():
            pl.when(now == due)(functools.partial(take, names))

    own_z(0)
    own_plane(0)
    for i in range(1, 8):
        to = lax.rem(dp + i, 8)
        send(gain_own, gain_all.at[dp], gs.at[to], gr.at[dp], (to, z)).start()
    gain_all[dp] = gain_own[...]
    take(FIRST)
    seg_row = seg_ref[pl.ds(z, 1)].astype(F32)
    seg_col = jnp.broadcast_to(seg_row, (8, LEN)).T[:, 0:1]
    bias[...] = jnp.where(seg_col == seg_row, 0.0, -1e30)
    gain_sum[...] = jnp.zeros_like(gain_sum)
    gain_parts[...] = jnp.zeros_like(gain_parts)
    take(SECOND)
    for i in range(1, 8):
        other = lax.rem(dp + i, 8)
        send(gain_own, gain_all.at[other], gs.at[other], gr.at[other], (other, z)).wait_recv()
    gain_a = gain_row(gain_all, 0)
    gain_f = gain_row(gain_all, 1)
    take(THIRD)
    rows_wait(0, x_in, x_ref)

    def norm_a(i):
        xhat, _ = norm(x_ref[i].astype(F32))
        normed = (xhat * gain_a).astype(BF)
        nrm[block(i)] = normed
        put_t(na_t, i, normed)

    loop(4, norm_a)

    def attend(i):
        q = nearest(z, i)
        core_ready(0, q)
        w = weights[0, q].reshape(D, D)
        p = natural(nrm[...], w[:, 0:640])
        q8 = p[:, 0:256].astype(BF) * jnp.asarray(0.125, BF)
        v = p[:, 128:384].astype(BF)
        k = p[:, 384:640].astype(BF)
        qb[q] = q8
        vb[q] = v
        kb[q] = k
        for r in range(2):
            rs = slice(256 * r, 256 * (r + 1))
            ctx = jnp.zeros((256, 256), F32)
            lane = lax.broadcasted_iota(jnp.int32, (256, 128), 1)
            lse = lse_ref[rs]
            for h in range(3):
                s = against(between(q8[rs], 64 * h, 64), k) + bias[rs]
                m = jnp.max(s, axis=1, keepdims=True)
                e = jnp.exp(s - m)
                total = jnp.sum(e, axis=1, keepdims=True)
                ctx += natural(e.astype(BF), between(v, 64 + 64 * h, 64)) * (1.0 / total)
                lse = jnp.where(lane == 3 * q + h, m + jnp.log(total), lse)
            lse_ref[rs] = lse
            cb[q, rs] = ctx.astype(BF)
            serve(2 * i + r, ATTEND)

    loop(4, attend)

    def attend_out(i):
        add(i, against(cb[i], weights[0, i].reshape(D, D)[:, 512:768]))

    loop(4, attend_out)

    def norm_f(i):
        m = x_ref[i].astype(F32) + acc[block(i)]
        mid[block(i)] = m
        xhat, _ = norm(m)
        normed = (xhat * gain_f).astype(BF)
        nrm[block(i)] = normed
        put_t(nf_t, i, normed)

    loop(4, norm_f)
    take(AFTER_NORM)
    rows_wait(1, ct_in, ct_ref)

    def turn_ct(i):
        put_t(ct_t, i, ct_ref[i])
        serve(i, TURN)

    loop(4, turn_ct)

    def up(i):
        q = quarter(i)
        core_ready(1, q)
        w = weights[1, q].reshape(D, D)
        for r in range(2):
            rs = slice(256 * r, 256 * (r + 1))
            h = natural(nrm[rs], w)
            cdf = 0.5 + 0.5 * lax.erf(h * 0.7071067811865476)
            act[q, rs] = (h * cdf).astype(BF)
            gp[q, rs] = (cdf + h * (jnp.exp(-0.5 * h * h) * 0.3989422804014327)).astype(BF)
        emit_other(2, q, ct_t, act[q])

        @pl.when(i > 0)
        def _():
            emit_own(2, i - 1, ct_t, act[quarter(i - 1)])

        serve(i, UP)

    loop(4, up)
    emit_own(2, 3, ct_t, act[quarter(3)])
    take(AFTER_GRAD_DOWN)

    def down(i):
        q = nearest(z, i)
        core_ready(2, q)
        w = weights[2, q].reshape(D, D)
        gp[q] = (natural(ct_ref[...].reshape(LEN, D), w) * gp[q].astype(F32)).astype(BF)
        add(i, against(act[q], w))
        serve(i, DOWN)

    loop(4, down)
    out_ref[...] = (mid[...] + acc[...]).astype(BF).reshape(4, BLOCK, D)
    rows_start(2, out_ref, outs_ref)

    def up_back(i):
        q = quarter(i)
        emit_other(1, q, nf_t, gp[q])
        add(i, against(gp[q], weights[1, q].reshape(D, D)))
        emit_own(1, i, nf_t, gp[q])

        serve(i, UP_BACK)

    loop(4, up_back)

    def norm_f_back(i):
        xhat, scale = norm(mid[block(i)])
        back, grad_gain = norm_back(acc[block(i)], xhat, scale, gain_f)
        gain_sum[1:2] += grad_gain[None]
        grad_middle = ct_ref[i].astype(F32) + back
        mid[block(i)] = grad_middle
        attended = grad_middle.astype(BF)
        nrm[block(i)] = attended
        put_t(ct_t, i, attended)

    loop(4, norm_f_back)
    take(AFTER_NORM_BACK)

    def own_attention(k):
        q = quarter(k)
        emit_own(0, k, na_t, act[q, :, 0:640], (ct_t, cb[q]))

    def attend_back(i):
        q = quarter(i)
        w = weights[0, q].reshape(D, D)
        dctx = between(natural(nrm[...], w[:, 512:768]), 64, 192).astype(BF)

        @pl.when(i > 0)
        def _():
            own_attention(i - 1)

        q8, v, k, cx = qb[q], vb[q], kb[q], cb[q]
        dq = jnp.zeros((LEN, 256), F32)
        dk = jnp.zeros((LEN, 256), F32)
        dv = jnp.zeros((LEN, 256), F32)
        for h in range(3):
            lane = lax.broadcasted_iota(jnp.int32, (LEN, 128), 1)
            lse = jnp.sum(jnp.where(lane == 3 * q + h, lse_ref[...], 0.0), axis=1, keepdims=True)
            p = jnp.exp(against(between(q8, 64 * h, 64), k) + bias[...] - lse)
            dm = between(dctx, 64 + 64 * h, 64)
            delta = jnp.sum(dm.astype(F32) * cx.astype(F32), axis=1, keepdims=True)
            ds_ = (p * (against(dm, v) - delta)).astype(BF)
            dq += between(natural(ds_, k), 64 * h, 64)
            dk += between(inner(ds_, q8), 64 * h, 64)
            dv += between(inner(p.astype(BF), dctx), 64 + 64 * h, 64)
        dq = dq * 0.125
        d = jnp.concatenate(
            [dq[:, 0:128], dq[:, 128:256] + dv[:, 0:128], dv[:, 128:256], dk], axis=1
        ).astype(BF)

        serve(2 * i, ATTEND_BACK)
        emit_other(0, q, na_t, d, (ct_t, cx))
        add(i, against(d, w[:, 0:640]))
        act[q, :, 0:640] = d
        serve(2 * i + 1, ATTEND_BACK)

    loop(4, attend_back)

    def norm_a_back(i):
        xhat, scale = norm(x_ref[i].astype(F32))
        back, grad_gain = norm_back(acc[block(i)], xhat, scale, gain_a)
        gain_sum[0:1] += grad_gain[None]
        ct_ref[i] = (mid[block(i)] + back).astype(BF)

    loop(4, norm_a_back)
    rows_start(3, ct_ref, dxs_ref)
    own_attention(3)
    for i in range(2):
        for p in range(8):
            gain_parts[p, i : i + 1, 0:96] = gain_sum[i : i + 1, 96 * p : 96 * (p + 1)]

    def small_copy(i):
        to = lax.rem(dp + i, 8)
        return send(gain_parts.at[to], small.at[dp], egs.at[to], egr.at[dp], (to, z))

    def small_in(i):
        other = lax.rem(dp + i, 8)
        return send(gain_parts.at[other], small.at[other], egs.at[other], egr.at[other], (other, z))

    for i in range(1, 8):
        small_copy(i).start()
    take(AFTER_ROWS)
    take(LAST)
    total = gain_parts[dp]
    for i in range(1, 8):
        small_in(i).wait_recv()
        total = total + small[lax.rem(dp + i, 8)]
    gain_own_sum[...] = total
    for j in range(1, 4):
        q = lax.rem(z + j, 4)
        send(gain_own_sum, small_z.at[z], egzs.at[q], egzr.at[z], (dp, q)).start()
    take(END)
    for i in range(1, 8):
        other = lax.rem(dp + i, 8)
        send(gain_own, gain_all.at[other], gs.at[other], gr.at[other], (other, z)).wait_send()
        small_copy(i).wait_send()
    for g in range(3):
        weights_sent(g)
    grads_sent(2)
    grads_sent(1)
    loop(4, lambda q: out_core(0, q).wait_send())
    rows_wait(2, out_ref, outs_ref)
    total = gain_own_sum[...]
    for j in range(1, 4):
        q = lax.rem(z + j, 4)
        cp = send(gain_own_sum, small_z.at[q], egzs.at[q], egzr.at[q], (dp, q))
        cp.wait()
        total = total + small_z[q]
    gain_a_ref[...] = total[0:1, 0:96]
    gain_f_ref[...] = total[1:2, 0:96]
    rows_wait(3, ct_ref, dxs_ref)
    last_add(0)
    grads_sent(0)


def layer(x, ct, segment_ids, w_query, w_key, w_value, w_output, w_up, w_down, gain_attn, gain_ffn):
    sem = pltpu.SemaphoreType.DMA
    vm = pltpu.VMEM
    anywhere = pl.BlockSpec(memory_space=pl.ANY)
    vmem = pl.BlockSpec(memory_space=pltpu.VMEM)
    return pl.pallas_call(
        layer_kernel,
        out_shape=(
            jax.ShapeDtypeStruct(x.shape, BF),
            jax.ShapeDtypeStruct(x.shape, BF),
            *(jax.ShapeDtypeStruct(n, F32) for n in [(96, 192)] * 3 + [(192, 96)] + [(96, D)] * 2 + [(1, 96)] * 2),
        ),
        in_specs=[anywhere] * 2 + [vmem] * 9,
        out_specs=[anywhere] * 2 + [vmem] * 8,
        scratch_shapes=[
            vm((16, 128), BF), vm((8, 16, 128), BF),
            vm((3, 4, 8, 96, D), BF),
            vm((4, BLOCK, D), BF), vm((4, BLOCK, D), BF), vm((4, BLOCK, D), BF),
            vm((LEN, D), BF),
            vm((4, 2, 96, LEN), BF), vm((4, 2, 96, LEN), BF), vm((4, 2, 96, LEN), BF),
            vm((4, LEN, 256), BF), vm((4, LEN, 256), BF), vm((4, LEN, 256), BF), vm((4, LEN, 256), BF),
            vm((LEN, 128), F32), vm((LEN, LEN), F32), vm((LEN, D), F32), vm((LEN, D), F32),
            vm((4, LEN, D), BF), vm((4, LEN, D), BF),
            vm((4, 4, 96, D), BF), vm((3, 4, 4, 96, D), BF), vm((4, 4, 96, D), BF),
            vm((3, 4, 96, D), BF), vm((3, 4, 2, 96, D), BF), vm((3, 4, 96, D), BF),
            vm((8, 8, 128), F32), vm((4, 8, 128), F32), vm((8, D), F32), vm((8, 8, 128), F32), vm((8, 128), F32),
            sem((4,)),
            sem((3, 4, 2)), sem((3, 4)),
            sem((3, 4)), sem((3, 4)),
            sem((3, 4)), sem((3, 4)),
            sem((3, 4)), sem((3, 4)),
            sem((3, 4, 4)), sem((3, 4, 4)),
            sem((8,)), sem((8,)),
            sem((4, 4)), sem((4, 4)),
            sem((3, 4)), sem((3, 4)),
            sem((3, 4)), sem((3, 4)),
            sem((3, 4, 2)), sem((3, 4, 2)),
            sem((3, 4)), sem((3, 4)),
            sem((8,)), sem((8,)),
            sem((4,)), sem((4,)),
        ],
        compiler_params=pltpu.CompilerParams(
            collective_id=0, has_side_effects=True, vmem_limit_bytes=VMEM_LIMIT
        ),
        name="layer_with_copies",
    )(x, ct, segment_ids, w_query, w_key, w_value, w_output, w_up, w_down, gain_attn, gain_ffn)


VMEM_LIMIT = 62 * 2**20


def part_kernel(*refs):
    count = (len(refs) - 2) // 3
    sources, targets, held, (arrive, leave) = (
        refs[:count], refs[count : 2 * count], refs[2 * count : 3 * count], refs[3 * count :]
    )
    coming = [pltpu.make_async_copy(sources[i], held[i], arrive.at[i]) for i in range(count)]
    going = [pltpu.make_async_copy(held[i], targets[i], leave.at[i]) for i in range(count)]
    for copy in coming:
        copy.start()
    for copy_in, copy_out in zip(coming, going):
        copy_in.wait()
        copy_out.start()
    for copy in going:
        copy.wait()


def part(*results):
    anywhere = pl.BlockSpec(memory_space=pl.ANY)
    return pl.pallas_call(
        part_kernel,
        out_shape=[jax.ShapeDtypeStruct(r.shape, r.dtype) for r in results],
        in_specs=[anywhere] * len(results),
        out_specs=[anywhere] * len(results),
        scratch_shapes=[pltpu.VMEM(r.shape, r.dtype) for r in results]
        + [pltpu.SemaphoreType.DMA((len(results),))] * 2,
        name="part_outputs",
    )(*results)


def shards(
    inputs, segment_ids, w_query, w_key, w_value, w_output, w_up, w_down, gain_attn, gain_ffn, cotangent,
    *, parts, quarters,
):
    depth, width = w_query.shape
    if parts == 8 and quarters == 4:
        results = layer(
            inputs, cotangent, segment_ids, w_query, w_key, w_value, w_output, w_up, w_down.T,
            gain_attn.reshape(1, depth), gain_ffn.reshape(1, depth),
        )
        *outs, grad_down, grad_gain_attn, grad_gain_ffn = part(*results)
        return (*outs, grad_down.T, grad_gain_attn.reshape(depth), grad_gain_ffn.reshape(depth))
    else:
        z = lax.axis_index("mp")
        segment = lax.dynamic_index_in_dim(segment_ids, z, 0, keepdims=False)
        own = jnp.stack(
            [jnp.concatenate([w_query, w_value, w_key, w_output.T], axis=1), w_up, w_down.T]
        )
        weights = lax.all_gather(own, ("dp", "mp"), axis=0).reshape(parts, quarters, 3, depth, D)
        weights = weights.transpose(2, 1, 0, 3, 4).reshape(3, quarters, D, D)
        gains = jnp.stack(
            [lax.all_gather(g, "dp", axis=0, tiled=True) for g in (gain_attn, gain_ffn)]
        ).astype(F32)
        x, ct = (
            lax.all_to_all(a, "mp", split_axis=0, concat_axis=0, tiled=True) for a in (inputs, cotangent)
        )
        out, dx, grads, gg = row_layer(
            x.reshape(-1, D), ct.reshape(-1, D), segment, weights, gains[0], gains[1]
        )
        grads = grads.reshape(3, quarters, parts, depth, D).transpose(2, 1, 0, 3, 4)
        grads = grads.reshape(parts * quarters, 3, depth, D)
        total = lax.psum_scatter(grads, ("dp", "mp"), scatter_dimension=0).astype(F32)
        gg = lax.psum(lax.psum_scatter(gg, "dp", scatter_dimension=1, tiled=True), "mp")
        out, dx = (
            lax.all_to_all(a.reshape(inputs.shape), "mp", split_axis=0, concat_axis=0, tiled=True)
            for a in (out, dx)
        )
    return (
        out,
        dx,
        total[0, :, :width],
        total[0, :, 2 * width : 3 * width],
        total[0, :, width : 2 * width],
        total[0, :, 3 * width :].T,
        total[1],
        total[2].T,
        gg[0],
        gg[1],
    )


def solution(mesh):
    by_row = P("dp", "mp", None)
    grids = (P("dp", "mp"), P("dp", "mp"), P("dp", "mp"), P("mp", "dp"), P("dp", "mp"), P("mp", "dp"))
    gains = (P("dp"), P("dp"))
    return jax.shard_map(
        functools.partial(shards, parts=mesh.shape["dp"], quarters=mesh.shape["mp"]),
        mesh=mesh,
        in_specs=(by_row, P("dp", None)) + grids + gains + (by_row,),
        out_specs=(by_row, by_row) + grids + gains,
        check_vma=False,
    )
```

```python
import functools

import jax
import jax.numpy as jnp
from jax import lax
from jax.experimental import pallas as pl
from jax.experimental.pallas import tpu as pltpu
from jax.sharding import PartitionSpec as P

D = 768
HEADS = 12
HEAD = 64
EPS = 1e-05
MESH = pl.DeviceIdType.MESH
BF = jnp.bfloat16
F32 = jnp.float32


def dot(left, right, dims):
    return lax.dot_general(left, right, (dims, ((), ())), preferred_element_type=F32)


def natural(left, right):
    return dot(left, right, ((1,), (0,)))


def against(left, right):
    return dot(left, right, ((1,), (1,)))


def inner(left, right):
    return dot(left, right, ((0,), (0,)))


def norm(values):
    shifted = values - jnp.mean(values, axis=1, keepdims=True)
    scale = lax.rsqrt(jnp.mean(shifted * shifted, axis=1, keepdims=True) + EPS)
    return shifted * scale, scale


def norm_back(grad, xhat, scale, gain):
    e = grad * gain
    back = scale * (
        e - jnp.mean(e, axis=1, keepdims=True) - xhat * jnp.mean(e * xhat, axis=1, keepdims=True)
    )
    return back, jnp.sum(grad * xhat, axis=0)


def columns(w, first, count):
    part = w[:, :, first : first + count]
    return jnp.swapaxes(part, 0, 1).reshape(D, -1)


def row_layer(x, cotangent, segment, weights, gain_attn, gain_ffn):
    length = x.shape[0]
    quarters = weights.shape[1]
    width = D // quarters
    attn, up, down = weights[0], weights[1], weights[2]
    w_query, w_value, w_key, w_out = (columns(attn, i * width, width) for i in range(4))
    w_up, w_down = columns(up, 0, D), columns(down, 0, D)
    x = x.astype(F32)
    xhat_a, scale_a = norm(x)
    normed_a = (xhat_a * gain_attn).astype(BF)
    query, keys, values = (
        natural(normed_a, w).astype(BF).reshape(length, HEADS, HEAD) for w in (w_query, w_key, w_value)
    )
    same = segment[:, None] == segment[None, :]
    scores = jnp.einsum("qhd,khd->hqk", query, keys, preferred_element_type=F32) * HEAD**-0.5
    scores = jnp.where(same[None], scores, -1e30)
    exponent = jnp.exp(scores - jnp.max(scores, axis=2, keepdims=True))
    probs = exponent / jnp.sum(exponent, axis=2, keepdims=True)
    context = jnp.einsum("hqk,khd->qhd", probs.astype(BF), values, preferred_element_type=F32)
    context = context.reshape(length, D).astype(BF)
    middle = x + against(context, w_out)
    xhat_f, scale_f = norm(middle)
    normed_f = (xhat_f * gain_ffn).astype(BF)
    hidden = natural(normed_f, w_up)
    activated, gelu_back = jax.vjp(lambda v: jax.nn.gelu(v, approximate=False), hidden)
    activated = activated.astype(BF)
    output = (middle + against(activated, w_down)).astype(BF)

    grad_down = inner(cotangent, activated)
    grad_hidden = gelu_back(natural(cotangent, w_down))[0].astype(BF)
    grad_up = inner(normed_f, grad_hidden)
    back, grad_gain_ffn = norm_back(against(grad_hidden, w_up), xhat_f, scale_f, gain_ffn)
    grad_middle = cotangent.astype(F32) + back
    grad_attended = grad_middle.astype(BF)
    grad_out = inner(grad_attended, context)
    grad_context = natural(grad_attended, w_out).astype(BF).reshape(length, HEADS, HEAD)
    grad_probs = jnp.einsum("qhd,khd->hqk", grad_context, values, preferred_element_type=F32)
    grad_scores = (
        probs * (grad_probs - jnp.sum(probs * grad_probs, axis=2, keepdims=True))
    ).astype(BF)
    query_grad = jnp.einsum("hqk,khd->qhd", grad_scores, keys, preferred_element_type=F32) * HEAD**-0.5
    key_grad = jnp.einsum("hqk,qhd->khd", grad_scores, query, preferred_element_type=F32) * HEAD**-0.5
    value_grad = jnp.einsum(
        "hqk,qhd->khd", probs.astype(BF), grad_context, preferred_element_type=F32
    )
    query_grad, key_grad, value_grad = (
        g.reshape(length, D).astype(BF) for g in (query_grad, key_grad, value_grad)
    )
    grad_normed_a = (
        against(query_grad, w_query) + against(key_grad, w_key) + against(value_grad, w_value)
    )
    back, grad_gain_attn = norm_back(grad_normed_a, xhat_a, scale_a, gain_attn)
    input_grad = (grad_middle + back).astype(BF)

    def quarter(g, count):
        return g.astype(BF).reshape(D, quarters, count).swapaxes(0, 1)

    grads_attn = jnp.concatenate(
        [
            quarter(g, width)
            for g in (
                inner(normed_a, query_grad),
                inner(normed_a, value_grad),
                inner(normed_a, key_grad),
                grad_out,
            )
        ],
        axis=2,
    )
    grads = jnp.stack([grads_attn, quarter(grad_up, D), quarter(grad_down, D)])
    return output, input_grad, grads, jnp.stack([grad_gain_attn, grad_gain_ffn])


def between(value, first, count):
    lane = lax.broadcasted_iota(jnp.int32, value.shape, 1)
    return jnp.where((lane >= first) & (lane < first + count), value, jnp.zeros_like(value))


def place():
    dp, z = lax.axis_index("dp"), lax.axis_index("mp")
    c, x, y = lax.rem(dp, 2), lax.rem(dp // 2, 2), dp // 4
    return dp, z, c, dp + 2 - 4 * x, dp + 4 - 8 * y, dp + 1 - 2 * c


def send(src, dst, ssem, rsem, device):
    return pltpu.make_async_remote_copy(
        src_ref=src, dst_ref=dst, send_sem=ssem, recv_sem=rsem, device_id=device, device_id_type=MESH
    )


def nearest(z, k):
    inner_place = lax.rem((z + 1) // 2, 2)
    first_two = 1 - k // 2
    base = k + inner_place * first_two * (1 - 2 * k)
    return base + (z // 2) * (3 - 2 * base)


def gain_row(parts_ref, index):
    r = lax.broadcasted_iota(jnp.int32, (128, D), 0)
    col = lax.broadcasted_iota(jnp.int32, (128, D), 1)
    spread = jnp.where(lax.rem(col, 96) == r, 1.0, 0.0).astype(BF)
    total = jnp.zeros((1, D), F32)
    col = lax.broadcasted_iota(jnp.int32, (16, D), 1)
    row = lax.broadcasted_iota(jnp.int32, (16, D), 0)
    for p in range(8):
        full = natural(parts_ref[p], spread)
        keep = (row == index) & (col >= 96 * p) & (col < 96 * (p + 1))
        total = total + jnp.sum(jnp.where(keep, full, 0.0), axis=0, keepdims=True)
    return total


BLOCK = 128
LEN = 512

FIRST = ("b1", "a1", "z01", "s01", "z02", "s02", "z03", "s03", "x")
SECOND = (
    "p00", "p10", "p01", "iz11", "is11", "f00", "p02", "iz12", "is12", "p03", "f01", "iz13", "is13", "a2",
    "oz11", "os11", "f02", "oz12", "os12", "oz13", "os13", "b2", "f03",
)
THIRD = ()
ATTEND = {0: ('p11','z21','s21','iz22','is22','iz23','is23'), 1: ('p12','f10','c'), 3: ('p13',), 4: ('f11','p20'), 5: ('oz22','os22'), 6: ('p21',), 7: ('oz23','os23','f12')}
AFTER_NORM = ('f13',)
TURN = {}
UP = {0:('p22','f20'),1:('p23','f21',),2:('f22',),3:('f23',)}
AFTER_GRAD_DOWN = ()
DOWN = {0: ("e20",), 1: ("e21",), 2: ("e22",), 3: ("e23",)}
UP_BACK = {}
AFTER_NORM_BACK = ("l20", "l21", "l22", "l23")
ATTEND_BACK = {
    0: ("e10", "e11"), 1: ("e12", "e13", "r20", "r21"), 3: ("l10", "l11"), 5: ("l12", "l13", "r10", "r11", "e00"),
    7: ("t2", "e01"),
}
AFTER_ROWS = ('e02','l00','e03','t1')
LAST = ('l01',)
END = ("l02", "r00", "r01", "l03")


def block(i):
    return pl.ds(pl.multiple_of(i * BLOCK, BLOCK), BLOCK)


def loop(count, step):
    def body(i, _):
        step(i)
        return 0

    lax.fori_loop(0, count, body, 0)


def layer_kernel(
    x_in, ct_in, seg_ref, wq_ref, wk_ref, wv_ref, wo_ref, wup_ref, wdown_ref, ga_ref, gf_ref,
    outs_ref, dxs_ref, q_ref, k_ref, v_ref, o_ref, up_ref, down_ref, gain_a_ref, gain_f_ref,
    gain_own, gain_all, weights, x_ref, ct_ref, out_ref,
    nrm, na_t, nf_t, ct_t, qb, kb, vb, cb, lse_ref, bias, mid, acc, act, gp,
    staged, sums, from_core, corner, from_plane, from_z, small, small_z, gain_sum, gain_parts, gain_own_sum,
    local_sem, zs, zr, xs, xr, ys, yr, ds, dr, cs, cr, gs, gr, as_, ar,
    ecs, ecr, eks, ekr, eps, epr, ezs, ezr, egs, egr, egzs, egzr,
):
    dp, z, c, nx, ny, nc = place()
    yx, yx_x, yx_y, yx_d = dp // 2, nx // 2, ny // 2, 3 - dp // 2

    barrier = pltpu.get_barrier_semaphore()
    for i in range(1, 8):
        pl.semaphore_signal(barrier, inc=1, device_id=(lax.rem(dp + i, 8), z), device_id_type=MESH)
    for i in range(1, 4):
        pl.semaphore_signal(barrier, inc=1, device_id=(dp, lax.rem(z + i, 4)), device_id_type=MESH)

    weights[0, z, dp] = jnp.concatenate(
        [wq_ref[...], wv_ref[...], wk_ref[...], wo_ref[...].T], axis=1
    )
    weights[1, z, dp] = wup_ref[...]
    weights[2, z, dp] = wdown_ref[...]
    gain_own[...] = jnp.zeros_like(gain_own)
    gain_own[0:1, 0:96] = ga_ref[...]
    gain_own[1:2, 0:96] = gf_ref[...]
    pl.semaphore_wait(barrier, 10)

    def rows_start(i, src, dst):
        for j in range(1, 4):
            q = lax.rem(z + j, 4)
            send(src.at[q], dst.at[z], as_.at[i, q], ar.at[i, z], (dp, q)).start()
        pltpu.make_async_copy(src.at[z], dst.at[z], local_sem.at[i]).start()

    def rows_wait(i, src, dst):
        for j in range(1, 4):
            q = lax.rem(z + j, 4)
            cp = send(src.at[q], dst.at[q], as_.at[i, q], ar.at[i, q], (dp, q))
            cp.wait_send()
            cp.wait_recv()
        pltpu.make_async_copy(src.at[z], dst.at[z], local_sem.at[i]).wait()

    def tile(g, q, d):
        return weights.at[g, q, d]

    mate = z + 1 - 2 * lax.rem(z, 2)
    far_inner = 2 - z // 2
    outer = (z == 0) | (z == 3)
    other_side = 2 * (1 - z // 2)

    def z_copy(g, q, side, to):
        return send(tile(g, q, dp), tile(g, q, dp), zs.at[g, q, side], zr.at[g, q], (dp, to))

    def passes_on(q):
        return jnp.logical_not(outer) & (q // 2 != z // 2)

    def own_z(g):
        z_copy(g, z, 0, mate).start()
        z_copy(g, z, 1, far_inner).start()

    def z_done(g, q):
        @pl.when(q == z)
        def _():
            z_copy(g, q, 0, mate).wait_send()
            z_copy(g, q, 1, far_inner).wait_send()

        @pl.when(passes_on(q))
        def _():
            z_copy(g, q, 0, mate).wait_send()

    def x_copy(g, q):
        return send(tile(g, q, dp), tile(g, q, dp), xs.at[g, q], xr.at[g, q], (nx, z))

    def y_copy(g, q):
        return send(tile(g, q, dp), tile(g, q, dp), ys.at[g, q], yr.at[g, q], (ny, z))

    def core_copy(g, q, pos):
        d = 2 * pos + c
        return send(tile(g, q, d), tile(g, q, d), cs.at[g, q, pos], cr.at[g, q, pos], (nc, z))

    def forward(g, q, along_y):
        src, to = (nx, ny) if along_y else (ny, nx)
        return send(tile(g, q, src), tile(g, q, src), ds.at[g, q], dr.at[g, q], (to, z))

    def own_plane(g):
        x_copy(g, z).start()
        y_copy(g, z).start()
        core_copy(g, z, yx).start()

    def z_step(g, k):
        q = nearest(z, k)
        z_copy(g, q, 0, mate).wait_recv()

        @pl.when(passes_on(q))
        def _():
            z_copy(g, q, 0, mate).start()

    def spread_step(g, k):
        q = nearest(z, k)
        x_copy(g, q).start()
        y_copy(g, q).start()
        core_copy(g, q, yx).start()

    def plane_step(g, k):
        q = nearest(z, k)
        x_copy(g, q).wait_recv()

        @pl.when(lax.rem(q, 2) == 0)
        def _():
            forward(g, q, True).start()

        core_copy(g, q, yx_x).start()
        y_copy(g, q).wait_recv()

        @pl.when(lax.rem(q, 2) == 1)
        def _():
            forward(g, q, False).start()

        core_copy(g, q, yx_y).start()

    def far_step(g, k):
        q = nearest(z, k)
        d = 2 * yx_d + c
        send(tile(g, q, d), tile(g, q, d), ds.at[g, q], dr.at[g, q], (nx, z)).wait_recv()
        core_copy(g, q, yx_d).start()

    def core_ready(g, q):
        for pos in range(4):
            d = 2 * pos + 1 - c
            send(
                tile(g, q, d), tile(g, q, d), cs.at[g, q, pos], cr.at[g, q, pos], (nc, z)
            ).wait_recv()

    def weights_sent(g):
        def step(q):
            z_done(g, q)
            x_copy(g, q).wait_send()
            y_copy(g, q).wait_send()

            @pl.when(lax.rem(q, 2) == 0)
            def _():
                forward(g, q, True).wait_send()

            @pl.when(lax.rem(q, 2) == 1)
            def _():
                forward(g, q, False).wait_send()

            for pos in range(4):
                core_copy(g, q, pos).wait_send()

        loop(4, step)

    def out_core(g, q):
        return send(staged.at[q], from_core.at[q], ecs.at[g, q], ecr.at[g, q], (nc, z))

    def out_corner(g, q):
        to = nx + (ny - nx) * lax.rem(q, 2)
        return send(sums.at[g, q, yx_d], corner.at[g, q], eks.at[g, q], ekr.at[g, q], (to, z))

    def out_plane(g, q, side):
        to = nx + (ny - nx) * side
        pos = yx_x + (yx_y - yx_x) * side
        return send(
            sums.at[g, q, pos], from_plane.at[g, q, side], eps.at[g, q, side], epr.at[g, q, side], (to, z)
        )

    def out_z(g, q, slot, to):
        return send(sums.at[g, q, yx], from_z.at[g, slot], ezs.at[g, q], ezr.at[g, slot], (dp, to))

    def in_z(g, slot):
        return send(sums.at[g, 0, yx], from_z.at[g, slot], ezs.at[g, 0], ezr.at[g, slot], (dp, mate))

    def corner_add(g, q):
        side = 1 - lax.rem(q, 2)
        pos = yx_x + (yx_y - yx_x) * side
        out_corner(g, q).wait_recv()
        sums[g, q, pos] = (sums[g, q, pos].astype(F32) + corner[g, q].astype(F32)).astype(BF)
        out_plane(g, q, side).start()

    def plane_add(g, q):
        out_plane(g, q, 0).wait_recv()
        out_plane(g, q, 1).wait_recv()
        sums[g, q, yx] = (
            sums[g, q, yx].astype(F32)
            + from_plane[g, q, 0].astype(F32)
            + from_plane[g, q, 1].astype(F32)
        ).astype(BF)

        @pl.when(q == mate)
        def _():
            out_z(g, q, 0, mate).start()

        @pl.when(outer & (q // 2 != z // 2))
        def _():
            out_z(g, q, 2 + lax.rem(q, 2), mate).start()

    def relay(g, k):
        q = quarter(k)

        @pl.when(jnp.logical_not(outer))
        def _():
            slot = 2 + lax.rem(q, 2)
            in_z(g, slot).wait_recv()
            sums[g, q, yx] = (sums[g, q, yx].astype(F32) + from_z[g, slot].astype(F32)).astype(BF)
            out_z(g, q, 1, q).start()

    def last_add(g):
        in_z(g, 0).wait_recv()
        in_z(g, 1).wait_recv()
        total = sums[g, z, yx].astype(F32) + from_z[g, 0].astype(F32) + from_z[g, 1].astype(F32)
        if g == 0:
            q_ref[...] = total[:, 0:192]
            v_ref[...] = total[:, 192:384]
            k_ref[...] = total[:, 384:576]
            o_ref[...] = total[:, 576:768].T
        else:
            (up_ref if g == 1 else down_ref)[...] = total

    def grads_sent(g):
        def step(q):
            out_corner(g, q).wait_send()
            out_plane(g, q, 0).wait_send()
            out_plane(g, q, 1).wait_send()

            @pl.when(z != q)
            def _():
                out_z(g, q, 0, mate).wait_send()

        loop(4, step)

    def quarter(k):
        return nearest(z, 3 - k)

    def grad_rows(half, left, right, more):
        v = natural(left[:, half].reshape(384, LEN), right)
        if more is None:
            return ((0, v),)
        v2 = natural(more[0][:, half].reshape(384, LEN), more[1])
        return ((0, v[:, 0:512]), (512, v[:, 512:640] + v2[:, 0:128]), (640, v2[:, 128:256]))

    def emit_other(g, q, left, right, more=None):
        if g < 2:
            out_core(g + 1, q).wait_send()
        for first, v in grad_rows(1 - c, left, right, more):
            staged[q, :, :, first : first + v.shape[1]] = v.astype(BF).reshape(4, 96, v.shape[1])
        out_core(g, q).start()

    def emit_own(g, k, left, right, more=None):
        q = quarter(k)
        pieces = grad_rows(c, left, right, more)
        out_core(g, q).wait_recv()
        for first, v in pieces:
            lanes = slice(first, first + v.shape[1])
            theirs = from_core[q, :, :, lanes].astype(F32)
            sums[g, q, :, :, lanes] = (v.reshape(4, 96, v.shape[1]) + theirs).astype(BF)
        out_corner(g, q).start()

        @pl.when(k >= 1)
        def _():
            before = quarter(k - 1)
            out_plane(g, before, lax.rem(before, 2)).start()

        @pl.when(k == 3)
        def _():
            out_plane(g, q, lax.rem(q, 2)).start()

    def put_t(dst, i, v):
        dst[:, :, :, block(i)] = v.T.reshape(4, 2, 96, BLOCK)

    def add(i, value):
        @pl.when(i == 0)
        def _():
            acc[...] = value

        @pl.when(i > 0)
        def _():
            acc[...] += value

    steps = {
        "a": own_z, "b": own_plane, "z": z_step, "s": spread_step, "p": plane_step, "f": far_step,
        "x": lambda: rows_start(0, x_in, x_ref), "c": lambda: rows_start(1, ct_in, ct_ref),
        "e": lambda g, k: corner_add(g, quarter(k)), "l": lambda g, k: plane_add(g, quarter(k)), "r": relay, "t": last_add,
    }

    def take(names):
        for name in names:
            act_on = functools.partial(steps[name.lstrip("io")[0]], *map(int, name.lstrip("io")[1:]))
            if name[0] in "io":
                pl.when(outer if name[0] == "o" else jnp.logical_not(outer))(act_on)
            else:
                act_on()

    def serve(now, table):
        for due, names in table.items():
            pl.when(now == due)(functools.partial(take, names))

    own_z(0)
    own_plane(0)
    for i in range(1, 8):
        to = lax.rem(dp + i, 8)
        send(gain_own, gain_all.at[dp], gs.at[to], gr.at[dp], (to, z)).start()
    gain_all[dp] = gain_own[...]
    take(FIRST)
    seg_row = seg_ref[pl.ds(z, 1)].astype(F32)
    seg_col = jnp.broadcast_to(seg_row, (8, LEN)).T[:, 0:1]
    bias[...] = jnp.where(seg_col == seg_row, 0.0, -1e30)
    gain_sum[...] = jnp.zeros_like(gain_sum)
    gain_parts[...] = jnp.zeros_like(gain_parts)
    take(SECOND)
    for i in range(1, 8):
        other = lax.rem(dp + i, 8)
        send(gain_own, gain_all.at[other], gs.at[other], gr.at[other], (other, z)).wait_recv()
    gain_a = gain_row(gain_all, 0)
    gain_f = gain_row(gain_all, 1)
    take(THIRD)
    rows_wait(0, x_in, x_ref)

    def norm_a(i):
        xhat, _ = norm(x_ref[i].astype(F32))
        normed = (xhat * gain_a).astype(BF)
        nrm[block(i)] = normed
        put_t(na_t, i, normed)

    loop(4, norm_a)

    def attend(i):
        q = nearest(z, i)
        core_ready(0, q)
        w = weights[0, q].reshape(D, D)
        p = natural(nrm[...], w[:, 0:640])
        q8 = p[:, 0:256].astype(BF) * jnp.asarray(0.125, BF)
        v = p[:, 128:384].astype(BF)
        k = p[:, 384:640].astype(BF)
        qb[q] = q8
        vb[q] = v
        kb[q] = k
        for r in range(2):
            rs = slice(256 * r, 256 * (r + 1))
            ctx = jnp.zeros((256, 256), F32)
            lane = lax.broadcasted_iota(jnp.int32, (256, 128), 1)
            lse = lse_ref[rs]
            for h in range(3):
                s = against(between(q8[rs], 64 * h, 64), k) + bias[rs]
                m = jnp.max(s, axis=1, keepdims=True)
                e = jnp.exp(s - m)
                total = jnp.sum(e, axis=1, keepdims=True)
                ctx += natural(e.astype(BF), between(v, 64 + 64 * h, 64)) * (1.0 / total)
                lse = jnp.where(lane == 3 * q + h, m + jnp.log(total), lse)
            lse_ref[rs] = lse
            cb[q, rs] = ctx.astype(BF)
            serve(2 * i + r, ATTEND)

    loop(4, attend)

    def attend_out(i):
        add(i, against(cb[i], weights[0, i].reshape(D, D)[:, 512:768]))

    loop(4, attend_out)

    def norm_f(i):
        m = x_ref[i].astype(F32) + acc[block(i)]
        mid[block(i)] = m
        xhat, _ = norm(m)
        normed = (xhat * gain_f).astype(BF)
        nrm[block(i)] = normed
        put_t(nf_t, i, normed)

    loop(4, norm_f)
    take(AFTER_NORM)
    rows_wait(1, ct_in, ct_ref)

    def turn_ct(i):
        put_t(ct_t, i, ct_ref[i])
        serve(i, TURN)

    loop(4, turn_ct)

    def up(i):
        q = quarter(i)
        core_ready(1, q)
        w = weights[1, q].reshape(D, D)
        for r in range(2):
            rs = slice(256 * r, 256 * (r + 1))
            h = natural(nrm[rs], w)
            cdf = 0.5 + 0.5 * lax.erf(h * 0.7071067811865476)
            act[q, rs] = (h * cdf).astype(BF)
            gp[q, rs] = (cdf + h * (jnp.exp(-0.5 * h * h) * 0.3989422804014327)).astype(BF)
        emit_other(2, q, ct_t, act[q])

        @pl.when(i > 0)
        def _():
            emit_own(2, i - 1, ct_t, act[quarter(i - 1)])

        serve(i, UP)

    loop(4, up)
    emit_own(2, 3, ct_t, act[quarter(3)])
    take(AFTER_GRAD_DOWN)

    def down(i):
        q = nearest(z, i)
        core_ready(2, q)
        w = weights[2, q].reshape(D, D)
        gp[q] = (natural(ct_ref[...].reshape(LEN, D), w) * gp[q].astype(F32)).astype(BF)
        add(i, against(act[q], w))
        serve(i, DOWN)

    loop(4, down)
    out_ref[...] = (mid[...] + acc[...]).astype(BF).reshape(4, BLOCK, D)
    rows_start(2, out_ref, outs_ref)

    def up_back(i):
        q = quarter(i)
        emit_other(1, q, nf_t, gp[q])
        add(i, against(gp[q], weights[1, q].reshape(D, D)))
        emit_own(1, i, nf_t, gp[q])

        serve(i, UP_BACK)

    loop(4, up_back)

    def norm_f_back(i):
        xhat, scale = norm(mid[block(i)])
        back, grad_gain = norm_back(acc[block(i)], xhat, scale, gain_f)
        gain_sum[1:2] += grad_gain[None]
        grad_middle = ct_ref[i].astype(F32) + back
        mid[block(i)] = grad_middle
        attended = grad_middle.astype(BF)
        nrm[block(i)] = attended
        put_t(ct_t, i, attended)

    loop(4, norm_f_back)
    take(AFTER_NORM_BACK)

    def own_attention(k):
        q = quarter(k)
        emit_own(0, k, na_t, act[q, :, 0:640], (ct_t, cb[q]))

    def attend_back(i):
        q = quarter(i)
        w = weights[0, q].reshape(D, D)
        dctx = between(natural(nrm[...], w[:, 512:768]), 64, 192).astype(BF)

        @pl.when(i > 0)
        def _():
            own_attention(i - 1)

        q8, v, k, cx = qb[q], vb[q], kb[q], cb[q]
        dq = jnp.zeros((LEN, 256), F32)
        dk = jnp.zeros((LEN, 256), F32)
        dv = jnp.zeros((LEN, 256), F32)
        for h in range(3):
            lane = lax.broadcasted_iota(jnp.int32, (LEN, 128), 1)
            lse = jnp.sum(jnp.where(lane == 3 * q + h, lse_ref[...], 0.0), axis=1, keepdims=True)
            p = jnp.exp(against(between(q8, 64 * h, 64), k) + bias[...] - lse)
            dm = between(dctx, 64 + 64 * h, 64)
            delta = jnp.sum(dm.astype(F32) * cx.astype(F32), axis=1, keepdims=True)
            ds_ = (p * (against(dm, v) - delta)).astype(BF)
            dq += between(natural(ds_, k), 64 * h, 64)
            dk += between(inner(ds_, q8), 64 * h, 64)
            dv += between(inner(p.astype(BF), dctx), 64 + 64 * h, 64)
        dq = dq * 0.125
        d = jnp.concatenate(
            [dq[:, 0:128], dq[:, 128:256] + dv[:, 0:128], dv[:, 128:256], dk], axis=1
        ).astype(BF)

        serve(2 * i, ATTEND_BACK)
        emit_other(0, q, na_t, d, (ct_t, cx))
        add(i, against(d, w[:, 0:640]))
        act[q, :, 0:640] = d
        serve(2 * i + 1, ATTEND_BACK)

    loop(4, attend_back)

    def norm_a_back(i):
        xhat, scale = norm(x_ref[i].astype(F32))
        back, grad_gain = norm_back(acc[block(i)], xhat, scale, gain_a)
        gain_sum[0:1] += grad_gain[None]
        ct_ref[i] = (mid[block(i)] + back).astype(BF)

    def back_and_send(k):
        q = nearest(z, 3 - k)
        norm_a_back(q)

        @pl.when(k < 3)
        def _():
            send(ct_ref.at[q], dxs_ref.at[z], as_.at[3, q], ar.at[3, z], (dp, q)).start()

        @pl.when(k == 3)
        def _():
            pltpu.make_async_copy(ct_ref.at[z], dxs_ref.at[z], local_sem.at[3]).start()

    loop(4, back_and_send)
    own_attention(3)
    for i in range(2):
        for p in range(8):
            gain_parts[p, i : i + 1, 0:96] = gain_sum[i : i + 1, 96 * p : 96 * (p + 1)]

    def small_copy(i):
        to = lax.rem(dp + i, 8)
        return send(gain_parts.at[to], small.at[dp], egs.at[to], egr.at[dp], (to, z))

    def small_in(i):
        other = lax.rem(dp + i, 8)
        return send(gain_parts.at[other], small.at[other], egs.at[other], egr.at[other], (other, z))

    for i in range(1, 8):
        small_copy(i).start()
    take(AFTER_ROWS)
    take(LAST)
    total = gain_parts[dp]
    for i in range(1, 8):
        small_in(i).wait_recv()
        total = total + small[lax.rem(dp + i, 8)]
    gain_own_sum[...] = total
    for j in range(1, 4):
        q = lax.rem(z + j, 4)
        send(gain_own_sum, small_z.at[z], egzs.at[q], egzr.at[z], (dp, q)).start()
    take(END)
    for i in range(1, 8):
        other = lax.rem(dp + i, 8)
        send(gain_own, gain_all.at[other], gs.at[other], gr.at[other], (other, z)).wait_send()
        small_copy(i).wait_send()
    for g in range(3):
        weights_sent(g)
    grads_sent(2)
    grads_sent(1)
    loop(4, lambda q: out_core(0, q).wait_send())
    rows_wait(2, out_ref, outs_ref)
    total = gain_own_sum[...]
    for j in range(1, 4):
        q = lax.rem(z + j, 4)
        cp = send(gain_own_sum, small_z.at[q], egzs.at[q], egzr.at[q], (dp, q))
        cp.wait()
        total = total + small_z[q]
    gain_a_ref[...] = total[0:1, 0:96]
    gain_f_ref[...] = total[1:2, 0:96]
    rows_wait(3, ct_ref, dxs_ref)
    last_add(0)
    grads_sent(0)


def layer(x, ct, segment_ids, w_query, w_key, w_value, w_output, w_up, w_down, gain_attn, gain_ffn):
    sem = pltpu.SemaphoreType.DMA
    vm = pltpu.VMEM
    anywhere = pl.BlockSpec(memory_space=pl.ANY)
    vmem = pl.BlockSpec(memory_space=pltpu.VMEM)
    return pl.pallas_call(
        layer_kernel,
        out_shape=(
            jax.ShapeDtypeStruct(x.shape, BF),
            jax.ShapeDtypeStruct(x.shape, BF),
            *(jax.ShapeDtypeStruct(n, F32) for n in [(96, 192)] * 3 + [(192, 96)] + [(96, D)] * 2 + [(1, 96)] * 2),
        ),
        in_specs=[anywhere] * 2 + [vmem] * 9,
        out_specs=[anywhere] * 2 + [vmem] * 8,
        scratch_shapes=[
            vm((16, 128), BF), vm((8, 16, 128), BF),
            vm((3, 4, 8, 96, D), BF),
            vm((4, BLOCK, D), BF), vm((4, BLOCK, D), BF), vm((4, BLOCK, D), BF),
            vm((LEN, D), BF),
            vm((4, 2, 96, LEN), BF), vm((4, 2, 96, LEN), BF), vm((4, 2, 96, LEN), BF),
            vm((4, LEN, 256), BF), vm((4, LEN, 256), BF), vm((4, LEN, 256), BF), vm((4, LEN, 256), BF),
            vm((LEN, 128), F32), vm((LEN, LEN), F32), vm((LEN, D), F32), vm((LEN, D), F32),
            vm((4, LEN, D), BF), vm((4, LEN, D), BF),
            vm((4, 4, 96, D), BF), vm((3, 4, 4, 96, D), BF), vm((4, 4, 96, D), BF),
            vm((3, 4, 96, D), BF), vm((3, 4, 2, 96, D), BF), vm((3, 4, 96, D), BF),
            vm((8, 8, 128), F32), vm((4, 8, 128), F32), vm((8, D), F32), vm((8, 8, 128), F32), vm((8, 128), F32),
            sem((4,)),
            sem((3, 4, 2)), sem((3, 4)),
            sem((3, 4)), sem((3, 4)),
            sem((3, 4)), sem((3, 4)),
            sem((3, 4)), sem((3, 4)),
            sem((3, 4, 4)), sem((3, 4, 4)),
            sem((8,)), sem((8,)),
            sem((4, 4)), sem((4, 4)),
            sem((3, 4)), sem((3, 4)),
            sem((3, 4)), sem((3, 4)),
            sem((3, 4, 2)), sem((3, 4, 2)),
            sem((3, 4)), sem((3, 4)),
            sem((8,)), sem((8,)),
            sem((4,)), sem((4,)),
        ],
        compiler_params=pltpu.CompilerParams(
            collective_id=0, has_side_effects=True, vmem_limit_bytes=VMEM_LIMIT
        ),
        name="layer_with_copies",
    )(x, ct, segment_ids, w_query, w_key, w_value, w_output, w_up, w_down, gain_attn, gain_ffn)


VMEM_LIMIT = 62 * 2**20


def part_kernel(*refs):
    count = (len(refs) - 2) // 3
    sources, targets, held, (arrive, leave) = (
        refs[:count], refs[count : 2 * count], refs[2 * count : 3 * count], refs[3 * count :]
    )
    coming = [pltpu.make_async_copy(sources[i], held[i], arrive.at[i]) for i in range(count)]
    going = [pltpu.make_async_copy(held[i], targets[i], leave.at[i]) for i in range(count)]
    for copy in coming:
        copy.start()
    for copy_in, copy_out in zip(coming, going):
        copy_in.wait()
        copy_out.start()
    for copy in going:
        copy.wait()


def part(*results):
    anywhere = pl.BlockSpec(memory_space=pl.ANY)
    return pl.pallas_call(
        part_kernel,
        out_shape=[jax.ShapeDtypeStruct(r.shape, r.dtype) for r in results],
        in_specs=[anywhere] * len(results),
        out_specs=[anywhere] * len(results),
        scratch_shapes=[pltpu.VMEM(r.shape, r.dtype) for r in results]
        + [pltpu.SemaphoreType.DMA((len(results),))] * 2,
        name="part_outputs",
    )(*results)


def shards(
    inputs, segment_ids, w_query, w_key, w_value, w_output, w_up, w_down, gain_attn, gain_ffn, cotangent,
    *, parts, quarters,
):
    depth, width = w_query.shape
    if parts == 8 and quarters == 4:
        results = layer(
            inputs, cotangent, segment_ids, w_query, w_key, w_value, w_output, w_up, w_down.T,
            gain_attn.reshape(1, depth), gain_ffn.reshape(1, depth),
        )
        *outs, grad_down, grad_gain_attn, grad_gain_ffn = part(*results)
        return (*outs, grad_down.T, grad_gain_attn.reshape(depth), grad_gain_ffn.reshape(depth))
    else:
        z = lax.axis_index("mp")
        segment = lax.dynamic_index_in_dim(segment_ids, z, 0, keepdims=False)
        own = jnp.stack(
            [jnp.concatenate([w_query, w_value, w_key, w_output.T], axis=1), w_up, w_down.T]
        )
        weights = lax.all_gather(own, ("dp", "mp"), axis=0).reshape(parts, quarters, 3, depth, D)
        weights = weights.transpose(2, 1, 0, 3, 4).reshape(3, quarters, D, D)
        gains = jnp.stack(
            [lax.all_gather(g, "dp", axis=0, tiled=True) for g in (gain_attn, gain_ffn)]
        ).astype(F32)
        x, ct = (
            lax.all_to_all(a, "mp", split_axis=0, concat_axis=0, tiled=True) for a in (inputs, cotangent)
        )
        out, dx, grads, gg = row_layer(
            x.reshape(-1, D), ct.reshape(-1, D), segment, weights, gains[0], gains[1]
        )
        grads = grads.reshape(3, quarters, parts, depth, D).transpose(2, 1, 0, 3, 4)
        grads = grads.reshape(parts * quarters, 3, depth, D)
        total = lax.psum_scatter(grads, ("dp", "mp"), scatter_dimension=0).astype(F32)
        gg = lax.psum(lax.psum_scatter(gg, "dp", scatter_dimension=1, tiled=True), "mp")
        out, dx = (
            lax.all_to_all(a.reshape(inputs.shape), "mp", split_axis=0, concat_axis=0, tiled=True)
            for a in (out, dx)
        )
    return (
        out,
        dx,
        total[0, :, :width],
        total[0, :, 2 * width : 3 * width],
        total[0, :, width : 2 * width],
        total[0, :, 3 * width :].T,
        total[1],
        total[2].T,
        gg[0],
        gg[1],
    )


def solution(mesh):
    by_row = P("dp", "mp", None)
    grids = (P("dp", "mp"), P("dp", "mp"), P("dp", "mp"), P("mp", "dp"), P("dp", "mp"), P("mp", "dp"))
    gains = (P("dp"), P("dp"))
    return jax.shard_map(
        functools.partial(shards, parts=mesh.shape["dp"], quarters=mesh.shape["mp"]),
        mesh=mesh,
        in_specs=(by_row, P("dp", None)) + grids + gains + (by_row,),
        out_specs=(by_row, by_row) + grids + gains,
        check_vma=False,
    )
```
